128 devices in a mesh: grp: 8 (over z, core), ad: 16 (over y, x).
Axes of the slice: x: 4, y: 4, z: 4, core: 2. Of those that a mesh axis runs over, the one named last changes fastest.
Arguments:
- tokens: bfloat16 [4096, 5120], P(('grp', 'ad')), may hold values from -6 to 6
- prompt_cache: bfloat16 [32, 8, 4096, 256], P('grp', None, 'ad'), may hold values from -100 to 100
- generated_cache: bfloat16 [1024, 256, 256], P('grp', 'ad'), may hold values from -9 to 9
- suffix_lengths: int32 [1024], P('grp'), may hold values from 1 to 32
- fanout: int32 [32, 2], replicated, may hold values from 0 to 7, as said below
- prompt_adapter: int32 [32], replicated, may hold values from 0 to 3
- query_weight: bfloat16 [5120, 8192], P(None, 'ad'), may hold values from -0.078125 to 0.078125
- key_value_weight: bfloat16 [5120, 2, 1024], P(None, None, 'ad'), may hold values from -0.078125 to 0.078125
- output_weight: bfloat16 [8192, 5120], P('ad'), may hold values from -0.0625 to 0.0625
- adapter_down_maps: bfloat16 [5120, 4, 128], P('ad'), may hold values from -0.078125 to 0.078125
- adapter_up_maps: bfloat16 [4, 128, 8192], P(None, None, 'ad'), may hold values from -0.5 to 0.5
- query_norm_gain: float32 [128], replicated, may hold values from 1 to 8
- key_norm_gain: float32 [128], replicated, may hold values from 1 to 3
Outputs:
- mixed: bfloat16 [4096, 5120], P(('grp', 'ad'))
The draws below stay inside these ranges and needn't reach their ends.
Inputs may be any that keep to these rules, and one draw needn't show every extreme that they name: `fanout`: each row lists 2 different groups. Among the 4 prompts of one owner group every group is listed exactly once.
All inputs are finite; a program needn't handle non-finite values.
Results may differ from the reference program's by a relative error of at most 0.035.
Values may be sent and summed in bfloat16 or wider, within the bound.
No kernel may reach another device: no remote copies, remote signals or barrier semaphores. Data moves between devices by JAX's collectives and lax.ppermute only.
A program may use at most 192 MiB of HBM per device.

```python
import math
import jax
import jax.numpy as jnp
from jax import lax

MODEL_WIDTH = 5120
QUERY_HEADS = 64
KEY_VALUE_HEADS = 8
HEAD_SIZE = 128
ADAPTER_RANK = 128
FAN = 2
DECODE_STEPS = 4
ADAPTER_COUNT = 4
SAMPLES_PER_GROUP = 16
PROMPT_TOKENS = 4096
SUFFIX_LENGTH = 32
OWNED = 4
PROMPT_COUNT = 32
SAMPLE_COUNT = 1024
NEW_TOKEN_ROWS = 4096
HEADS_DEV = 4
N_GRP = 8
N_AD = 16


def draw_fanout(key, part):
    key = jax.random.fold_in(key, 11)
    owner_keys = jax.random.split(key, PROMPT_COUNT // OWNED)
    orders = jax.vmap(lambda one_key: jax.random.permutation(one_key, OWNED * FAN))(owner_keys)
    return orders.reshape(PROMPT_COUNT, FAN).astype(jnp.int32)


def draw_prompt_cache(key, part):
    key = jax.random.fold_in(key, 21)
    key_main = jax.random.fold_in(key, 0)
    array_shape = (PROMPT_COUNT, KEY_VALUE_HEADS, PROMPT_TOKENS, 2 * HEAD_SIZE)
    entries = jnp.clip(jax.random.normal(key_main, array_shape, jnp.float32), -6.0, 6.0)
    return entries.astype(jnp.bfloat16)


def draw_query_norm_gain(key, part):
    key = jax.random.fold_in(key, 23)
    gains = jnp.exp(jax.random.uniform(key, (HEAD_SIZE,), jnp.float32, 0.0, math.log(3.0)))
    return gains


def plant(drawn, rng, least, high):
    longest = drawn.shape.index(max(drawn.shape))
    spots = []
    for shift in (0, 1):
        where = [jax.random.randint(jax.random.fold_in(rng, axis), (), 0, length) for axis, length in enumerate(drawn.shape)]
        where[longest] = (where[longest] + shift) % drawn.shape[longest]
        spots.append(tuple(where))
    return drawn.at[spots[0]].set(least).at[spots[1]].set(high)


def level_of(key, shape, cuts, smallest, largest):
    def one(axis_at, shards_of):
        heights = jax.random.uniform(jax.random.fold_in(jax.random.fold_in(key, 6), axis_at), (shards_of,), jnp.float32, smallest / len(cuts), largest / len(cuts))
        return jnp.repeat(jnp.exp(heights), shape[axis_at] // shards_of).reshape((-1,) + (1,) * (len(shape) - axis_at - 1))

    gain = one(*cuts[0])
    for cut in cuts[1:]:
        gain = gain * one(*cut)
    return gain


def centred(rng, dims, deviation, reach, pieces=(), kind=jnp.bfloat16):
    values = jax.random.normal(rng, dims, jnp.float32) * deviation
    if len(pieces) > 0:
        values = level_of(rng, dims, pieces, -0.22, 0.18) * values
    return jnp.clip(values, min=-reach, max=reach).astype(kind)


def setup_inputs(seed: int = 0) -> dict:
    seeds = jax.random.split(jax.random.key(seed), 14)
    tokens = centred(seeds[0], (NEW_TOKEN_ROWS, MODEL_WIDTH), 1.0, 6.0, ((0, 128),))
    prompt_cache = draw_prompt_cache(jax.random.fold_in(seeds[13], 71), 0)
    generated_cache = centred(seeds[2], (SAMPLE_COUNT, KEY_VALUE_HEADS * SUFFIX_LENGTH, 2 * HEAD_SIZE), 1.5, 9.0, ((0, 8), (1, 16)))
    suffix_lengths = plant(jax.random.randint(seeds[3], (SAMPLE_COUNT,), 1, SUFFIX_LENGTH + 1), jax.random.fold_in(seeds[3], 1), 1, SUFFIX_LENGTH).astype(jnp.int32)
    fanout = draw_fanout(jax.random.fold_in(seeds[13], 71), 0)
    prompt_adapter = plant(jax.random.randint(seeds[5], (PROMPT_COUNT,), 0, ADAPTER_COUNT), jax.random.fold_in(seeds[5], 1), 0, ADAPTER_COUNT - 1).astype(jnp.int32)
    query_weight = centred(seeds[6], (MODEL_WIDTH, QUERY_HEADS * HEAD_SIZE), MODEL_WIDTH ** -0.5, 0.078125, ((1, 16),))
    key_value_weight = centred(seeds[7], (MODEL_WIDTH, 2, KEY_VALUE_HEADS * HEAD_SIZE), MODEL_WIDTH ** -0.5, 0.078125, ((2, 16),))
    output_weight = centred(seeds[8], (QUERY_HEADS * HEAD_SIZE, MODEL_WIDTH), (QUERY_HEADS * HEAD_SIZE) ** -0.5, 0.0625, ((0, 16),))
    adapter_down_maps = centred(seeds[9], (MODEL_WIDTH, ADAPTER_COUNT, ADAPTER_RANK), MODEL_WIDTH ** -0.5, 0.078125, ((0, 16),))
    adapter_up_maps = centred(seeds[10], (ADAPTER_COUNT, ADAPTER_RANK, QUERY_HEADS * HEAD_SIZE), ADAPTER_RANK ** -0.5, 0.5, ((2, 16),))
    query_norm_gain = draw_query_norm_gain(jax.random.fold_in(seeds[13], 71), 0)
    key_norm_gain = jnp.clip(jnp.exp(jax.random.uniform(seeds[12], (HEAD_SIZE,), jnp.float32, math.log(1.0), math.log(3.0))), 1.0, 3.0)
    return dict(tokens=tokens, prompt_cache=prompt_cache, generated_cache=generated_cache, suffix_lengths=suffix_lengths, fanout=fanout, prompt_adapter=prompt_adapter, query_weight=query_weight, key_value_weight=key_value_weight, output_weight=output_weight, adapter_down_maps=adapter_down_maps, adapter_up_maps=adapter_up_maps, query_norm_gain=query_norm_gain, key_norm_gain=key_norm_gain)


theta_base = 1000000.0
norm_eps = 1e-06
masked_low = -1e+30

def rms_scale(vector, gain_vec):
    mean_sq = lax.optimization_barrier(jnp.mean(vector * vector, axis=-1, keepdims=True))
    return vector * lax.rsqrt(mean_sq + norm_eps) * gain_vec

def rotate(vector, position):
    half_len = vector.shape[-1] // 2
    inverse = theta_base ** (-2.0 * jnp.arange(half_len, dtype=jnp.float32) / vector.shape[-1])
    angles = position[..., None] * inverse
    cosine = jnp.cos(angles)
    sine_part = jnp.sin(angles)
    first_half = vector[..., :half_len]
    second_half = vector[..., half_len:]
    return jnp.concatenate([first_half * cosine - second_half * sine_part, second_half * cosine + first_half * sine_part], axis=-1)

def slot_prompts(fanout, groups, owned_count):
    listed = jnp.any(fanout[:, :, None] == jnp.arange(groups, dtype=jnp.int32)[None, None, :], axis=1)
    listed = listed.astype(jnp.int32).reshape(groups, owned_count, groups)
    local_index = lax.optimization_barrier(jnp.sum(listed * jnp.arange(owned_count, dtype=jnp.int32)[None, :, None], axis=1))
    prompt_ids = jnp.arange(groups, dtype=jnp.int32)[:, None] * owned_count + local_index
    return prompt_ids.T

def reference(tokens, prompt_cache, generated_cache, suffix_lengths, fanout, prompt_adapter, query_weight, key_value_weight, output_weight, adapter_down_maps, adapter_up_maps, query_norm_gain, key_norm_gain):
    slot_table = slot_prompts(fanout, N_GRP, OWNED)
    prompt_slots = slot_table.reshape(-1)
    sample_prompt = jnp.repeat(prompt_slots, SAMPLES_PER_GROUP)
    prompt_hit = (sample_prompt[:, None] == jnp.arange(PROMPT_COUNT, dtype=jnp.int32)[None, :]).astype(jnp.int32)
    sample_task = lax.optimization_barrier(jnp.sum(prompt_hit * prompt_adapter[None, :], axis=1))
    row_task = jnp.repeat(sample_task, DECODE_STEPS)
    adapter_row_block = (row_task[:, None] == jnp.arange(ADAPTER_COUNT, dtype=jnp.int32)[None, :]).astype(jnp.float32)
    query_plain = jnp.dot(tokens, query_weight, preferred_element_type=jnp.float32)
    key_value_rows = jnp.dot(tokens, key_value_weight.reshape(MODEL_WIDTH, 2 * KEY_VALUE_HEADS * HEAD_SIZE), preferred_element_type=jnp.float32)
    key_value_rows = lax.optimization_barrier(key_value_rows.astype(jnp.bfloat16))
    low_rank_term = jnp.zeros((NEW_TOKEN_ROWS, ADAPTER_RANK), jnp.float32)
    for adapter_index in range(ADAPTER_COUNT):
        low_rank_term = low_rank_term + adapter_row_block[:, adapter_index:adapter_index + 1] * jnp.dot(tokens, adapter_down_maps[:, adapter_index, :], preferred_element_type=jnp.float32)
    spread_rank_term = (low_rank_term.astype(jnp.bfloat16)[:, None, :] * adapter_row_block.astype(jnp.bfloat16)[:, :, None]).reshape(NEW_TOKEN_ROWS, ADAPTER_COUNT * ADAPTER_RANK)
    query_complete = query_plain + jnp.dot(spread_rank_term, adapter_up_maps.reshape(ADAPTER_COUNT * ADAPTER_RANK, QUERY_HEADS * HEAD_SIZE), preferred_element_type=jnp.float32)
    position = (PROMPT_TOKENS + jnp.repeat(suffix_lengths, DECODE_STEPS) + jnp.tile(jnp.arange(DECODE_STEPS, dtype=jnp.int32), SAMPLE_COUNT)).astype(jnp.float32)
    query_vectors = rotate(rms_scale(query_complete.reshape(NEW_TOKEN_ROWS, QUERY_HEADS, HEAD_SIZE), query_norm_gain), position[:, None]).astype(jnp.bfloat16)
    key_value_rows = key_value_rows.reshape(NEW_TOKEN_ROWS, 2, KEY_VALUE_HEADS, HEAD_SIZE)
    incoming_keys = rotate(rms_scale(key_value_rows[:, 0].astype(jnp.float32), key_norm_gain), position[:, None]).astype(jnp.bfloat16)
    incoming_values = key_value_rows[:, 1]
    total_slots = N_GRP * N_GRP
    group_length = QUERY_HEADS // KEY_VALUE_HEADS
    query_slot_table = query_vectors.reshape(total_slots, SAMPLES_PER_GROUP, DECODE_STEPS, KEY_VALUE_HEADS, group_length, HEAD_SIZE)
    key_slot_table = incoming_keys.reshape(total_slots, SAMPLES_PER_GROUP, DECODE_STEPS, KEY_VALUE_HEADS, HEAD_SIZE)
    value_slot_table = incoming_values.reshape(total_slots, SAMPLES_PER_GROUP, DECODE_STEPS, KEY_VALUE_HEADS, HEAD_SIZE)
    generated_slots = generated_cache.reshape(total_slots, SAMPLES_PER_GROUP, KEY_VALUE_HEADS, SUFFIX_LENGTH, 2 * HEAD_SIZE)
    length_slots = suffix_lengths.reshape(total_slots, SAMPLES_PER_GROUP)
    score_scale = HEAD_SIZE ** (-0.5)

    def one_slot(slot_index):
        page_set = lax.dynamic_index_in_dim(prompt_cache, prompt_slots[slot_index], 0, keepdims=False).astype(jnp.float32)
        query_slot = query_slot_table[slot_index].astype(jnp.float32)
        suffix_pages = generated_slots[slot_index].astype(jnp.float32)
        latest_keys = key_slot_table[slot_index].astype(jnp.float32)
        fresh_values = value_slot_table[slot_index].astype(jnp.float32)
        lengths = length_slots[slot_index]
        prefix_part = jnp.einsum('sthgd,hkd->sthgk', query_slot, page_set[..., :HEAD_SIZE]) * score_scale
        suffix_part = jnp.einsum('sthgd,shkd->sthgk', query_slot, suffix_pages[..., :HEAD_SIZE]) * score_scale
        suffix_part = jnp.where(jnp.arange(SUFFIX_LENGTH)[None, None, None, None, :] < lengths[:, None, None, None, None], suffix_part, masked_low)
        fresh_part = jnp.einsum('sthgd,suhd->sthgu', query_slot, latest_keys) * score_scale
        fresh_part = jnp.where(jnp.arange(DECODE_STEPS)[None, None, None, None, :] <= jnp.arange(DECODE_STEPS)[None, :, None, None, None], fresh_part, masked_low)
        peak = jnp.maximum(jnp.maximum(lax.optimization_barrier(jnp.max(prefix_part, axis=-1)), lax.optimization_barrier(jnp.max(suffix_part, axis=-1))), lax.optimization_barrier(jnp.max(fresh_part, axis=-1)))
        prefix_exp = jnp.exp(prefix_part - peak[..., None])
        suffix_exp = jnp.exp(suffix_part - peak[..., None])
        fresh_exp = jnp.exp(fresh_part - peak[..., None])
        denominator = lax.optimization_barrier(jnp.sum(prefix_exp, axis=-1)) + lax.optimization_barrier(jnp.sum(suffix_exp, axis=-1)) + lax.optimization_barrier(jnp.sum(fresh_exp, axis=-1))
        prefix_weight = lax.optimization_barrier(prefix_exp.astype(jnp.bfloat16)).astype(jnp.float32)
        suffix_weight = lax.optimization_barrier(suffix_exp.astype(jnp.bfloat16)).astype(jnp.float32)
        fresh_weight = lax.optimization_barrier(fresh_exp.astype(jnp.bfloat16)).astype(jnp.float32)
        summed = jnp.einsum('sthgk,hkd->sthgd', prefix_weight, page_set[..., HEAD_SIZE:])
        summed = summed + jnp.einsum('sthgk,shkd->sthgd', suffix_weight, suffix_pages[..., HEAD_SIZE:])
        summed = summed + jnp.einsum('sthgu,suhd->sthgd', fresh_weight, fresh_values)
        return (summed / denominator[..., None]).astype(jnp.bfloat16)
    attended = lax.map(one_slot, jnp.arange(total_slots, dtype=jnp.int32)).reshape(NEW_TOKEN_ROWS, QUERY_HEADS * HEAD_SIZE)
    block_width = HEADS_DEV * HEAD_SIZE

    def add_block(running, block_index):
        product = jnp.dot(lax.dynamic_slice_in_dim(attended, block_index * block_width, block_width, 1), lax.dynamic_slice_in_dim(output_weight, block_index * block_width, block_width, 0), preferred_element_type=jnp.float32)
        rounded = lax.optimization_barrier(product.astype(jnp.bfloat16))
        return (running + rounded.astype(jnp.float32), None)
    running, unused = lax.scan(add_block, jnp.zeros((NEW_TOKEN_ROWS, MODEL_WIDTH), jnp.float32), jnp.arange(N_AD, dtype=jnp.int32))
    return running.astype(jnp.bfloat16)
```

```python
import functools

import jax
import jax.numpy as jnp
from jax import lax
from jax.experimental import pallas as pl
from jax.experimental.pallas import tpu as pltpu
from jax.sharding import PartitionSpec as P

MODEL_WIDTH = 5120
KEY_VALUE_HEADS = 8
HEAD_SIZE = 128
ADAPTER_RANK = 128
FAN = 2
DECODE_STEPS = 4
ADAPTER_COUNT = 4
PROMPT_TOKENS = 4096
GROUPS = 8
SHARDS = 16
OWNED = 4
SLOT_SAMPLES = 16
SLOT_ROWS = SLOT_SAMPLES * DECODE_STEPS
HALF_ROWS = SLOT_ROWS // 2
ROWS = GROUPS * SLOT_ROWS
OWN_HEADS = 4
OWN_WIDTH = OWN_HEADS * HEAD_SIZE
HEAD_FAN = 2 * OWN_HEADS
SENT_WIDTH = OWN_WIDTH + HEAD_SIZE
BACK_WIDTH = HEAD_FAN * HEAD_SIZE + HEAD_SIZE

theta_base = 1000000.0
norm_eps = 1e-06
masked_low = -1e30
exponent_scale = HEAD_SIZE**-0.5 * 1.4426950408889634

ROLE_GROUPS = [[0, 3, 4, 7, 8, 11, 12, 15], [1, 2, 5, 6, 9, 10, 13, 14]]
HEAD_GROUPS = [
    [group * SHARDS + 2 * head + half for group in range(GROUPS) for half in range(2)]
    for head in range(KEY_VALUE_HEADS)
]
PARTNERS = [(shard, shard ^ 1) for shard in range(SHARDS)]


def slot_prompts(fanout, groups, owned_count):
    listed = jnp.any(
        fanout[:, :, None] == jnp.arange(groups, dtype=jnp.int32)[None, None, :], axis=1
    )
    listed = listed.astype(jnp.int32).reshape(groups, owned_count, groups)
    return jnp.sum(listed * jnp.arange(owned_count, dtype=jnp.int32)[None, :, None], axis=1)


def angle_tables(position):
    half_len = HEAD_SIZE // 2
    inverse = theta_base ** (-2.0 * jnp.arange(half_len, dtype=jnp.float32) / HEAD_SIZE)
    angles = position[..., None] * inverse
    cosine = jnp.cos(angles)
    sine = jnp.sin(angles)
    return (
        jnp.concatenate([cosine, cosine], axis=-1),
        jnp.concatenate([-sine, sine], axis=-1),
    )


def norm_rotate(vector, gain, cosine, sine):
    mean_sq = jnp.mean(vector * vector, axis=-1, keepdims=True)
    scaled = vector * lax.rsqrt(mean_sq + norm_eps) * gain
    return scaled * cosine + pltpu.roll(scaled, HEAD_SIZE // 2, 1) * sine


def dot_nt(left, right):
    return lax.dot_general(
        left, right, (((1,), (1,)), ((), ())), preferred_element_type=jnp.float32
    )


def project_kernel(
    task_ref,
    tokens_ref,
    query_ref,
    keyval_ref,
    rank_ref,
    up_ref,
    cos_ref,
    sin_ref,
    gain_ref,
    out_ref,
    query_sum,
    keyval_sum,
):
    step = pl.program_id(0)

    @pl.when(step == 0)
    def _():
        query_sum[...] = jnp.zeros_like(query_sum)
        keyval_sum[...] = jnp.zeros_like(keyval_sum)

    part = tokens_ref[...]
    query_sum[...] += jnp.dot(part, query_ref[...], preferred_element_type=jnp.float32)
    keyval_sum[...] += dot_nt(part, keyval_ref[...])

    @pl.when(step == pl.num_programs(0) - 1)
    def _():
        for slot in range(GROUPS):
            rows = slice(slot * SLOT_ROWS, (slot + 1) * SLOT_ROWS)
            query = query_sum[rows, :] + jnp.dot(
                rank_ref[rows, :], up_ref[task_ref[slot]], preferred_element_type=jnp.float32
            )
            for head in range(OWN_HEADS):
                lanes = slice(head * HEAD_SIZE, (head + 1) * HEAD_SIZE)
                out_ref[rows, lanes] = norm_rotate(
                    query[:, lanes], gain_ref[...], cos_ref[rows, :], sin_ref[rows, :]
                ).astype(jnp.bfloat16)
        out_ref[:, OWN_WIDTH:] = keyval_sum[...].astype(jnp.bfloat16)


def project(tasks, tokens, query_weight, keyval_weight, low_rank, up_maps, cosine, sine, gain):
    tile = 512
    whole = lambda *shape: pl.BlockSpec(shape, lambda k, tasks: (0,) * len(shape))
    return pl.pallas_call(
        project_kernel,
        grid_spec=pltpu.PrefetchScalarGridSpec(
            num_scalar_prefetch=1,
            grid=(MODEL_WIDTH // tile,),
            in_specs=[
                pl.BlockSpec((ROWS, tile), lambda k, tasks: (0, k)),
                pl.BlockSpec((tile, OWN_WIDTH), lambda k, tasks: (k, 0)),
                pl.BlockSpec((HEAD_SIZE, tile), lambda k, tasks: (0, k)),
                whole(ROWS, ADAPTER_RANK),
                whole(ADAPTER_COUNT, ADAPTER_RANK, OWN_WIDTH),
                whole(ROWS, HEAD_SIZE),
                whole(ROWS, HEAD_SIZE),
                whole(1, HEAD_SIZE),
            ],
            out_specs=whole(ROWS, SENT_WIDTH),
            scratch_shapes=[
                pltpu.VMEM((ROWS, OWN_WIDTH), jnp.float32),
                pltpu.VMEM((ROWS, HEAD_SIZE), jnp.float32),
            ],
        ),
        out_shape=jax.ShapeDtypeStruct((ROWS, SENT_WIDTH), jnp.bfloat16),
        compiler_params=pltpu.CompilerParams(vmem_limit_bytes=40 * 2**20),
        cost_estimate=pl.CostEstimate(
            flops=2 * ROWS * MODEL_WIDTH * SENT_WIDTH, bytes_accessed=13_000_000, transcendentals=0
        ),
        name="project",
    )(tasks, tokens, query_weight, keyval_weight, low_rank, up_maps, cosine, sine, gain)


def attend_kernel(
    order_ref,
    local_ref,
    place_ref,
    sent_ref,
    page_ref,
    suffix_ref,
    cos_ref,
    sin_ref,
    gain_ref,
    out_ref,
):
    half = place_ref[0]
    flip = place_ref[1]
    span = GROUPS * PROMPT_TOKENS // SHARDS
    pages = page_ref[...].reshape(span, 2 * HEAD_SIZE)
    keys = pages[:, :HEAD_SIZE]
    values = jnp.concatenate(
        [jnp.ones((span, HEAD_SIZE), jnp.bfloat16), pages[:, HEAD_SIZE:]], axis=1
    )
    low_part = sent_ref[0, 0, :, OWN_WIDTH:].astype(jnp.float32)
    high_part = sent_ref[0, 1, :, OWN_WIDTH:].astype(jnp.float32)
    lane = lax.broadcasted_iota(jnp.int32, (SLOT_ROWS, HEAD_SIZE), 1)
    low_lanes = lane < HEAD_SIZE // 2
    new_keys = jnp.where(low_lanes, low_part, pltpu.roll(high_part, HEAD_SIZE // 2, 1))
    new_values = jnp.where(low_lanes, pltpu.roll(low_part, HEAD_SIZE // 2, 1), high_part)
    new_keys = norm_rotate(new_keys, gain_ref[...], cos_ref[0], sin_ref[0])
    suffix_rows = SLOT_SAMPLES * 16
    extra = suffix_rows + 2 * SLOT_ROWS
    suffix = suffix_ref[0, :suffix_rows, :]
    zeros = jnp.zeros((SLOT_ROWS, HEAD_SIZE), jnp.bfloat16)
    extra_keys = jnp.concatenate(
        [suffix[:, :HEAD_SIZE], new_keys.astype(jnp.bfloat16), zeros], axis=0
    )
    extra_values = jnp.concatenate(
        [suffix[:, HEAD_SIZE:], new_values.astype(jnp.bfloat16), zeros], axis=0
    )
    extra_values = jnp.concatenate(
        [jnp.ones((extra, HEAD_SIZE), jnp.bfloat16), extra_values], axis=1
    )
    lengths = suffix_ref[0, suffix_rows:, :].astype(jnp.float32)
    sample_of = lax.broadcasted_iota(jnp.int32, (SLOT_SAMPLES, suffix_rows), 0)
    column_sample = lax.broadcasted_iota(jnp.int32, (SLOT_SAMPLES, suffix_rows), 1) // 16
    column_length = jnp.sum(
        jnp.where(sample_of == column_sample, lengths, 0.0), axis=0, keepdims=True
    )
    row = lax.broadcasted_iota(jnp.int32, (SLOT_ROWS, suffix_rows), 0)
    column = lax.broadcasted_iota(jnp.int32, (SLOT_ROWS, suffix_rows), 1)
    suffix_seen = (row // DECODE_STEPS == column // 16) & (
        (half * 16 + column % 16).astype(jnp.float32) < column_length
    )
    row = lax.broadcasted_iota(jnp.int32, (SLOT_ROWS, 2 * SLOT_ROWS), 0)
    column = lax.broadcasted_iota(jnp.int32, (SLOT_ROWS, 2 * SLOT_ROWS), 1)
    new_seen = (
        (row // DECODE_STEPS == column // DECODE_STEPS)
        & (column % DECODE_STEPS <= row % DECODE_STEPS)
        & (column // HALF_ROWS == half)
    )
    bias = jnp.concatenate(
        [jnp.where(suffix_seen, 0.0, masked_low), jnp.where(new_seen, 0.0, masked_low)], axis=1
    )
    pair_bias = jnp.concatenate([bias, bias], axis=0)
    logs = jnp.zeros((SLOT_ROWS, HEAD_SIZE), jnp.float32)
    for first in range(0, HEAD_FAN, 2):
        source, start = divmod(first, OWN_HEADS)
        start = start * HEAD_SIZE
        query = jnp.concatenate(
            [
                sent_ref[0, source, :, start : start + HEAD_SIZE],
                sent_ref[0, source, :, start + HEAD_SIZE : start + 2 * HEAD_SIZE],
            ],
            axis=0,
        )
        prefix_score = dot_nt(query, keys)
        extra_score = dot_nt(query, extra_keys) + pair_bias
        peak = jnp.maximum(
            jnp.max(prefix_score, axis=-1, keepdims=True),
            jnp.max(extra_score, axis=-1, keepdims=True),
        )
        scaled_peak = peak * exponent_scale
        prefix_weight = jnp.exp2(prefix_score * exponent_scale - scaled_peak).astype(jnp.bfloat16)
        extra_weight = jnp.exp2(extra_score * exponent_scale - scaled_peak).astype(jnp.bfloat16)
        total = jnp.dot(prefix_weight, values, preferred_element_type=jnp.float32) + jnp.dot(
            extra_weight, extra_values, preferred_element_type=jnp.float32
        )
        denominator = total[:, :HEAD_SIZE]
        attended = total[:, HEAD_SIZE:] / denominator
        log_sum = scaled_peak + jnp.log2(denominator)
        for index in range(2):
            head = first + index
            rows = slice(index * SLOT_ROWS, (index + 1) * SLOT_ROWS)
            top = attended[index * SLOT_ROWS : index * SLOT_ROWS + HALF_ROWS].astype(jnp.bfloat16)
            low = attended[index * SLOT_ROWS + HALF_ROWS : (index + 1) * SLOT_ROWS].astype(
                jnp.bfloat16
            )
            lanes = slice(head * HEAD_SIZE, (head + 1) * HEAD_SIZE)
            out_ref[0, 0, :, lanes] = jnp.where(flip == 0, top, low)
            out_ref[0, 1, :, lanes] = jnp.where(flip == 0, low, top)
            logs = jnp.where(lane == head, log_sum[rows], logs)
    high_term = logs.astype(jnp.bfloat16).astype(jnp.float32)
    rest = logs - high_term
    mid_term = rest.astype(jnp.bfloat16).astype(jnp.float32)
    low_term = rest - mid_term
    packed = (
        high_term + pltpu.roll(mid_term, HEAD_FAN, 1) + pltpu.roll(low_term, 2 * HEAD_FAN, 1)
    ).astype(jnp.bfloat16)
    top = packed[:HALF_ROWS]
    low = packed[HALF_ROWS:]
    out_ref[0, 0, :, HEAD_FAN * HEAD_SIZE :] = jnp.where(flip == 0, top, low)
    out_ref[0, 1, :, HEAD_FAN * HEAD_SIZE :] = jnp.where(flip == 0, low, top)


def attend(order, local, place, sent, pages, suffix, cosine, sine, gain):
    block = PROMPT_TOKENS // SHARDS
    return pl.pallas_call(
        attend_kernel,
        grid_spec=pltpu.PrefetchScalarGridSpec(
            num_scalar_prefetch=3,
            grid=(GROUPS,),
            in_specs=[
                pl.BlockSpec((1, 2, SLOT_ROWS, SENT_WIDTH), lambda i, o, l, p: (o[i], 0, 0, 0)),
                pl.BlockSpec(
                    (GROUPS, 1, block, 2 * HEAD_SIZE), lambda i, o, l, p: (0, l[i], 0, 0)
                ),
                pl.BlockSpec(
                    (1, suffix.shape[1], 2 * HEAD_SIZE), lambda i, o, l, p: (o[i], 0, 0)
                ),
                pl.BlockSpec((1, SLOT_ROWS, HEAD_SIZE), lambda i, o, l, p: (o[i], 0, 0)),
                pl.BlockSpec((1, SLOT_ROWS, HEAD_SIZE), lambda i, o, l, p: (o[i], 0, 0)),
                pl.BlockSpec((1, HEAD_SIZE), lambda i, o, l, p: (0, 0)),
            ],
            out_specs=pl.BlockSpec(
                (1, 2, HALF_ROWS, BACK_WIDTH), lambda i, o, l, p: (o[i], 0, 0, 0)
            ),
        ),
        out_shape=jax.ShapeDtypeStruct((GROUPS, 2, HALF_ROWS, BACK_WIDTH), jnp.bfloat16),
        compiler_params=pltpu.CompilerParams(vmem_limit_bytes=48 * 2**20),
        cost_estimate=pl.CostEstimate(
            flops=2 * GROUPS * 512 * 2432 * 384,
            bytes_accessed=8_000_000,
            transcendentals=GROUPS * 512 * 2432,
        ),
        name="attend",
    )(order, local, place, sent, pages, suffix, cosine, sine, gain)


def output_kernel(place_ref, back_ref, own_ref, other_ref, out_ref, mixed):
    half = place_ref[0]
    rows = GROUPS * HALF_ROWS

    @pl.when(pl.program_id(0) == 0)
    def _():
        lane = lax.broadcasted_iota(jnp.int32, (rows, HEAD_SIZE), 1)

        def log_of(source):
            packed = back_ref[:, source, :, HEAD_FAN * HEAD_SIZE :]
            packed = packed.reshape(rows, HEAD_SIZE).astype(jnp.float32)
            return (
                packed
                + pltpu.roll(packed, HEAD_SIZE - HEAD_FAN, 1)
                + pltpu.roll(packed, HEAD_SIZE - 2 * HEAD_FAN, 1)
            )

        first_log = log_of(0)
        second_log = log_of(1)
        peak = jnp.maximum(first_log, second_log)
        first_part = jnp.exp2(first_log - peak)
        second_part = jnp.exp2(second_log - peak)
        both = first_part + second_part
        first_part = first_part / both
        second_part = second_part / both

        def attended(head):
            lanes = slice(head * HEAD_SIZE, (head + 1) * HEAD_SIZE)
            first = back_ref[:, 0, :, lanes].reshape(rows, HEAD_SIZE).astype(jnp.float32)
            second = back_ref[:, 1, :, lanes].reshape(rows, HEAD_SIZE).astype(jnp.float32)
            return (
                first * first_part[:, head : head + 1] + second * second_part[:, head : head + 1]
            ).astype(jnp.bfloat16)

        for head in range(OWN_HEADS):
            low = attended(head)
            high = attended(head + OWN_HEADS)
            lanes = slice(head * HEAD_SIZE, (head + 1) * HEAD_SIZE)
            mixed[0, :, lanes] = jnp.where(half == 0, low, high)
            mixed[1, :, lanes] = jnp.where(half == 0, high, low)

    out_ref[...] = (
        jnp.dot(mixed[0], own_ref[...], preferred_element_type=jnp.float32)
        + jnp.dot(mixed[1], other_ref[...], preferred_element_type=jnp.float32)
    ).astype(jnp.bfloat16)


def output_part(place, back, own_weight, other_weight):
    tile = 1024
    rows = GROUPS * HALF_ROWS
    return pl.pallas_call(
        output_kernel,
        grid_spec=pltpu.PrefetchScalarGridSpec(
            num_scalar_prefetch=1,
            grid=(MODEL_WIDTH // tile,),
            in_specs=[
                pl.BlockSpec((GROUPS, 2, HALF_ROWS, BACK_WIDTH), lambda n, p: (0, 0, 0, 0)),
                pl.BlockSpec((OWN_WIDTH, tile), lambda n, p: (0, n)),
                pl.BlockSpec((OWN_WIDTH, tile), lambda n, p: (0, n)),
            ],
            out_specs=pl.BlockSpec((rows, tile), lambda n, p: (0, n)),
            scratch_shapes=[pltpu.VMEM((2, rows, OWN_WIDTH), jnp.bfloat16)],
        ),
        out_shape=jax.ShapeDtypeStruct((rows, MODEL_WIDTH), jnp.bfloat16),
        compiler_params=pltpu.CompilerParams(vmem_limit_bytes=40 * 2**20),
        cost_estimate=pl.CostEstimate(
            flops=2 * rows * MODEL_WIDTH * 1024, bytes_accessed=14_000_000, transcendentals=0
        ),
        name="output_part",
    )(place, back, own_weight, other_weight)


def swap(block, axes, groups=None):
    return lax.all_to_all(
        block, axes, split_axis=0, concat_axis=0, tiled=True, axis_index_groups=groups
    )


def shards(
    tokens,
    prompt_cache,
    generated_cache,
    suffix_lengths,
    fanout,
    prompt_adapter,
    query_weight,
    key_value_weight,
    output_weight,
    adapter_down_maps,
    adapter_up_maps,
    query_norm_gain,
    key_norm_gain,
):
    group = lax.axis_index("grp")
    shard = lax.axis_index("ad")
    head = shard // 2
    half = shard % 2
    local_table = slot_prompts(fanout, GROUPS, OWNED)

    arrived = swap(jnp.swapaxes(prompt_cache, 0, 1), "ad", ROLE_GROUPS)
    part_rows = lax.all_gather(tokens, "ad", axis=0, tiled=True)

    slot_suffix = generated_cache.reshape(GROUPS, SLOT_SAMPLES * 16, 2 * HEAD_SIZE)
    slot_lengths = suffix_lengths.reshape(GROUPS, SLOT_SAMPLES, 1).astype(jnp.bfloat16)
    slot_suffix = jnp.concatenate(
        [slot_suffix, jnp.broadcast_to(slot_lengths, (GROUPS, SLOT_SAMPLES, 2 * HEAD_SIZE))], axis=1
    )
    suffix = swap(slot_suffix, "grp")

    slice_rows = OWN_WIDTH // GROUPS
    weight_slice = lax.dynamic_slice_in_dim(output_weight, group * slice_rows, slice_rows, 0)
    other_weight = lax.all_gather(
        lax.ppermute(weight_slice, "ad", PARTNERS), "grp", axis=0, tiled=True
    )

    owners = jnp.arange(GROUPS, dtype=jnp.int32)
    local_of_slot = lax.dynamic_index_in_dim(local_table, group, 1, keepdims=False)
    prompts = owners * OWNED + local_of_slot
    hit = prompts[:, None] == jnp.arange(prompt_adapter.shape[0], dtype=jnp.int32)[None, :]
    tasks = jnp.sum(hit.astype(jnp.int32) * prompt_adapter[None, :], axis=1)
    own_rows = tokens.shape[0]
    columns = swap(jnp.swapaxes(tokens.reshape(own_rows, SHARDS, -1), 0, 1), "ad")
    rank_all = jnp.dot(
        columns.reshape(ROWS, -1),
        adapter_down_maps.reshape(-1, ADAPTER_COUNT * ADAPTER_RANK),
        preferred_element_type=jnp.float32,
    ).reshape(GROUPS, SLOT_ROWS, ADAPTER_COUNT, ADAPTER_RANK)
    chosen = (tasks[:, None] == jnp.arange(ADAPTER_COUNT, dtype=jnp.int32)[None, :]).astype(
        jnp.float32
    )
    rank_part = jnp.sum(rank_all * chosen[:, None, :, None], axis=2)
    rank_rows = jnp.sum(swap(rank_part.reshape(SHARDS, own_rows, ADAPTER_RANK), "ad"), axis=0)
    rank_rows = rank_rows.astype(jnp.bfloat16)
    low_rank = swap(jnp.broadcast_to(rank_rows[None], (SHARDS,) + rank_rows.shape), "ad")

    steps = jnp.arange(DECODE_STEPS, dtype=jnp.int32)
    position = (PROMPT_TOKENS + suffix_lengths[:, None] + steps[None, :]).astype(jnp.float32)
    cosine, sine = angle_tables(position.reshape(ROWS))
    sent = project(
        tasks,
        part_rows,
        query_weight,
        key_value_weight.transpose(1, 2, 0).reshape(HEAD_SIZE, MODEL_WIDTH),
        low_rank.reshape(ROWS, ADAPTER_RANK),
        adapter_up_maps,
        cosine,
        sine,
        query_norm_gain.reshape(1, HEAD_SIZE),
    )
    received = swap(
        jnp.broadcast_to(
            sent.reshape(GROUPS, 1, SLOT_ROWS, SENT_WIDTH), (GROUPS, 2, SLOT_ROWS, SENT_WIDTH)
        ).reshape(2 * GROUPS, SLOT_ROWS, SENT_WIDTH),
        ("grp", "ad"),
        HEAD_GROUPS,
    ).reshape(GROUPS, 2, SLOT_ROWS, SENT_WIDTH)

    local = lax.dynamic_index_in_dim(local_table, group, 0, keepdims=False)
    rank_key = local * GROUPS + owners
    spot = jnp.sum((rank_key[None, :] < rank_key[:, None]).astype(jnp.int32), axis=1)
    placed = (spot[None, :] == owners[:, None]).astype(jnp.int32)
    order = jnp.sum(placed * owners[None, :], axis=1)
    local_sorted = jnp.sum(placed * local[None, :], axis=1)
    flip = (head + group) % 2
    place = jnp.stack([half, flip]).astype(jnp.int32)
    far_lengths = suffix[:, SLOT_SAMPLES * 16 :, 0].astype(jnp.float32)
    far_position = PROMPT_TOKENS + far_lengths[:, :, None] + steps.astype(jnp.float32)
    far_cosine, far_sine = angle_tables(far_position.reshape(GROUPS, SLOT_ROWS))
    partial = attend(
        order,
        local_sorted,
        place,
        received,
        arrived,
        suffix,
        far_cosine,
        far_sine,
        key_norm_gain.reshape(1, HEAD_SIZE),
    )
    back = swap(
        partial.reshape(2 * GROUPS, HALF_ROWS, BACK_WIDTH), ("grp", "ad"), HEAD_GROUPS
    ).reshape(GROUPS, 2, HALF_ROWS, BACK_WIDTH)
    product = output_part(place, back, output_weight, other_weight)
    blocks = swap(product.reshape(GROUPS, HALF_ROWS, MODEL_WIDTH), "ad", ROLE_GROUPS)
    return jnp.sum(blocks.astype(jnp.float32), axis=0).astype(jnp.bfloat16)


def solution(mesh):
    return jax.shard_map(
        shards,
        mesh=mesh,
        in_specs=(
            P(("grp", "ad"), None),
            P("grp", None, "ad", None),
            P("grp", "ad", None),
            P("grp"),
            P(),
            P(),
            P(None, "ad"),
            P(None, None, "ad"),
            P("ad", None),
            P("ad", None, None),
            P(None, None, "ad"),
            P(),
            P(),
        ),
        out_specs=P(("grp", "ad"), None),
        check_vma=False,
    )
```

```python
import functools

import jax
import jax.numpy as jnp
from jax import lax
from jax.experimental import pallas as pl
from jax.experimental.pallas import tpu as pltpu
from jax.sharding import PartitionSpec as P

MODEL_WIDTH = 5120
KEY_VALUE_HEADS = 8
HEAD_SIZE = 128
ADAPTER_RANK = 128
FAN = 2
DECODE_STEPS = 4
ADAPTER_COUNT = 4
PROMPT_TOKENS = 4096
GROUPS = 8
SHARDS = 16
OWNED = 4
SLOT_SAMPLES = 16
SLOT_ROWS = SLOT_SAMPLES * DECODE_STEPS
HALF_ROWS = SLOT_ROWS // 2
ROWS = GROUPS * SLOT_ROWS
OWN_HEADS = 4
OWN_WIDTH = OWN_HEADS * HEAD_SIZE
HEAD_FAN = 2 * OWN_HEADS
SENT_WIDTH = OWN_WIDTH + HEAD_SIZE
BACK_WIDTH = HEAD_FAN * HEAD_SIZE + HEAD_SIZE

theta_base = 1000000.0
norm_eps = 1e-06
masked_low = -1e30
exponent_scale = HEAD_SIZE**-0.5 * 1.4426950408889634

ROLE_GROUPS = [[0, 3, 4, 7, 8, 11, 12, 15], [1, 2, 5, 6, 9, 10, 13, 14]]
HEAD_GROUPS = [
    [group * SHARDS + 2 * head + half for group in range(GROUPS) for half in range(2)]
    for head in range(KEY_VALUE_HEADS)
]
PARTNERS = [(shard, shard ^ 1) for shard in range(SHARDS)]


def slot_prompts(fanout, groups, owned_count):
    listed = jnp.any(
        fanout[:, :, None] == jnp.arange(groups, dtype=jnp.int32)[None, None, :], axis=1
    )
    listed = listed.astype(jnp.int32).reshape(groups, owned_count, groups)
    return jnp.sum(listed * jnp.arange(owned_count, dtype=jnp.int32)[None, :, None], axis=1)


def angle_tables(position):
    half_len = HEAD_SIZE // 2
    inverse = theta_base ** (-2.0 * jnp.arange(half_len, dtype=jnp.float32) / HEAD_SIZE)
    angles = position[..., None] * inverse
    cosine = jnp.cos(angles)
    sine = jnp.sin(angles)
    return (
        jnp.concatenate([cosine, cosine], axis=-1),
        jnp.concatenate([-sine, sine], axis=-1),
    )


def norm_rotate(vector, gain, cosine, sine):
    mean_sq = jnp.mean(vector * vector, axis=-1, keepdims=True)
    scaled = vector * lax.rsqrt(mean_sq + norm_eps) * gain
    return scaled * cosine + pltpu.roll(scaled, HEAD_SIZE // 2, 1) * sine


def dot_nt(left, right):
    return lax.dot_general(
        left, right, (((1,), (1,)), ((), ())), preferred_element_type=jnp.float32
    )


def project_kernel(
    task_ref,
    spot_ref,
    tokens_ref,
    query_ref,
    keyval_ref,
    rank_ref,
    up_ref,
    cos_ref,
    sin_ref,
    gain_ref,
    out_ref,
    query_sum,
    keyval_sum,
):
    step = pl.program_id(0)

    @pl.when(step == 0)
    def _():
        query_sum[...] = jnp.zeros_like(query_sum)
        keyval_sum[...] = jnp.zeros_like(keyval_sum)

    part = tokens_ref[...]
    query_sum[...] += jnp.dot(part, query_ref[...], preferred_element_type=jnp.float32)
    keyval_sum[...] += dot_nt(part, keyval_ref[...])

    @pl.when(step == pl.num_programs(0) - 1)
    def _():
        for slot in range(GROUPS):
            rows = slice(slot * SLOT_ROWS, (slot + 1) * SLOT_ROWS)
            low_rank = jnp.concatenate(
                [rank_ref[spot_ref[2 * slot]], rank_ref[spot_ref[2 * slot + 1]]], axis=0
            )
            query = query_sum[rows, :] + jnp.dot(
                low_rank, up_ref[task_ref[slot]], preferred_element_type=jnp.float32
            )
            for head in range(OWN_HEADS):
                lanes = slice(head * HEAD_SIZE, (head + 1) * HEAD_SIZE)
                out_ref[rows, lanes] = norm_rotate(
                    query[:, lanes], gain_ref[...], cos_ref[rows, :], sin_ref[rows, :]
                ).astype(jnp.bfloat16)
        out_ref[:, OWN_WIDTH:] = keyval_sum[...].astype(jnp.bfloat16)


def project(tasks, spots, tokens, query_weight, keyval_weight, low_rank, up_maps, cosine, sine, gain):
    tile = 512
    whole = lambda *shape: pl.BlockSpec(shape, lambda k, t, s: (0,) * len(shape))
    return pl.pallas_call(
        project_kernel,
        grid_spec=pltpu.PrefetchScalarGridSpec(
            num_scalar_prefetch=2,
            grid=(MODEL_WIDTH // tile,),
            in_specs=[
                pl.BlockSpec((ROWS, tile), lambda k, t, s: (0, k)),
                pl.BlockSpec((tile, OWN_WIDTH), lambda k, t, s: (k, 0)),
                pl.BlockSpec((HEAD_SIZE, tile), lambda k, t, s: (0, k)),
                whole(SHARDS, HALF_ROWS, ADAPTER_RANK),
                whole(ADAPTER_COUNT, ADAPTER_RANK, OWN_WIDTH),
                whole(ROWS, HEAD_SIZE),
                whole(ROWS, HEAD_SIZE),
                whole(1, HEAD_SIZE),
            ],
            out_specs=whole(ROWS, SENT_WIDTH),
            scratch_shapes=[
                pltpu.VMEM((ROWS, OWN_WIDTH), jnp.float32),
                pltpu.VMEM((ROWS, HEAD_SIZE), jnp.float32),
            ],
        ),
        out_shape=jax.ShapeDtypeStruct((ROWS, SENT_WIDTH), jnp.bfloat16),
        compiler_params=pltpu.CompilerParams(vmem_limit_bytes=60 * 2**20),
        cost_estimate=pl.CostEstimate(
            flops=2 * ROWS * MODEL_WIDTH * SENT_WIDTH, bytes_accessed=13_000_000, transcendentals=0
        ),
        name="project",
    )(tasks, spots, tokens, query_weight, keyval_weight, low_rank, up_maps, cosine, sine, gain)


def attend_kernel(
    order_ref,
    local_ref,
    reach_ref,
    place_ref,
    sent_ref,
    page_ref,
    suffix_ref,
    cos_ref,
    sin_ref,
    gain_ref,
    out_ref,
):
    half = place_ref[0]
    flip = place_ref[1]
    span = GROUPS * PROMPT_TOKENS // SHARDS
    pages = page_ref[...].reshape(span, 2 * HEAD_SIZE)
    keys = pages[:, :HEAD_SIZE]
    values = jnp.concatenate(
        [jnp.ones((span, HEAD_SIZE), jnp.bfloat16), pages[:, HEAD_SIZE:]], axis=1
    )
    low_part = sent_ref[0, 0, :, OWN_WIDTH:].astype(jnp.float32)
    high_part = sent_ref[0, 1, :, OWN_WIDTH:].astype(jnp.float32)
    lane = lax.broadcasted_iota(jnp.int32, (SLOT_ROWS, HEAD_SIZE), 1)
    low_lanes = lane < HEAD_SIZE // 2
    new_keys = jnp.where(low_lanes, low_part, pltpu.roll(high_part, HEAD_SIZE // 2, 1))
    new_values = jnp.where(low_lanes, pltpu.roll(low_part, HEAD_SIZE // 2, 1), high_part)
    new_keys = norm_rotate(new_keys, gain_ref[...], cos_ref[0], sin_ref[0])
    suffix_rows = SLOT_SAMPLES * 16
    extra = suffix_rows + 2 * SLOT_ROWS
    suffix = suffix_ref[0, :suffix_rows, :]
    zeros = jnp.zeros((SLOT_ROWS, HEAD_SIZE), jnp.bfloat16)
    extra_keys = jnp.concatenate(
        [suffix[:, :HEAD_SIZE], new_keys.astype(jnp.bfloat16), zeros], axis=0
    )
    extra_values = jnp.concatenate(
        [suffix[:, HEAD_SIZE:], new_values.astype(jnp.bfloat16), zeros], axis=0
    )
    extra_values = jnp.concatenate(
        [jnp.ones((extra, HEAD_SIZE), jnp.bfloat16), extra_values], axis=1
    )
    lengths = suffix_ref[0, suffix_rows:, :].astype(jnp.float32)
    sample_of = lax.broadcasted_iota(jnp.int32, (SLOT_SAMPLES, suffix_rows), 0)
    column_sample = lax.broadcasted_iota(jnp.int32, (SLOT_SAMPLES, suffix_rows), 1) // 16
    column_length = jnp.sum(
        jnp.where(sample_of == column_sample, lengths, 0.0), axis=0, keepdims=True
    )
    row = lax.broadcasted_iota(jnp.int32, (SLOT_ROWS, suffix_rows), 0)
    column = lax.broadcasted_iota(jnp.int32, (SLOT_ROWS, suffix_rows), 1)
    suffix_seen = (row // DECODE_STEPS == column // 16) & (
        (half * 16 + column % 16).astype(jnp.float32) < column_length
    )
    row = lax.broadcasted_iota(jnp.int32, (SLOT_ROWS, 2 * SLOT_ROWS), 0)
    column = lax.broadcasted_iota(jnp.int32, (SLOT_ROWS, 2 * SLOT_ROWS), 1)
    new_seen = (
        (row // DECODE_STEPS == column // DECODE_STEPS)
        & (column % DECODE_STEPS <= row % DECODE_STEPS)
        & (column // HALF_ROWS == half)
    )
    bias = jnp.concatenate(
        [jnp.where(suffix_seen, 0.0, masked_low), jnp.where(new_seen, 0.0, masked_low)], axis=1
    )
    pair_bias = jnp.concatenate([bias, bias], axis=0)
    logs = jnp.zeros((SLOT_ROWS, HEAD_SIZE), jnp.float32)
    for first in range(0, HEAD_FAN, 2):
        source, start = divmod(first, OWN_HEADS)
        start = start * HEAD_SIZE
        query = jnp.concatenate(
            [
                sent_ref[0, source, :, start : start + HEAD_SIZE],
                sent_ref[0, source, :, start + HEAD_SIZE : start + 2 * HEAD_SIZE],
            ],
            axis=0,
        )
        prefix_score = dot_nt(query, keys)
        extra_score = dot_nt(query, extra_keys) + pair_bias
        peak = jnp.maximum(
            jnp.max(prefix_score, axis=-1, keepdims=True),
            jnp.max(extra_score, axis=-1, keepdims=True),
        )
        scaled_peak = peak * exponent_scale
        prefix_weight = jnp.exp2(prefix_score * exponent_scale - scaled_peak).astype(jnp.bfloat16)
        extra_weight = jnp.exp2(extra_score * exponent_scale - scaled_peak).astype(jnp.bfloat16)
        total = jnp.dot(prefix_weight, values, preferred_element_type=jnp.float32) + jnp.dot(
            extra_weight, extra_values, preferred_element_type=jnp.float32
        )
        denominator = total[:, :HEAD_SIZE]
        attended = total[:, HEAD_SIZE:] / denominator
        log_sum = scaled_peak + jnp.log2(denominator)
        for index in range(2):
            head = first + index
            rows = slice(index * SLOT_ROWS, (index + 1) * SLOT_ROWS)
            top = attended[index * SLOT_ROWS : index * SLOT_ROWS + HALF_ROWS].astype(jnp.bfloat16)
            low = attended[index * SLOT_ROWS + HALF_ROWS : (index + 1) * SLOT_ROWS].astype(
                jnp.bfloat16
            )
            lanes = slice(head * HEAD_SIZE, (head + 1) * HEAD_SIZE)
            out_ref[0, 0, :, lanes] = jnp.where(flip == 0, top, low)
            out_ref[0, 1, :, lanes] = jnp.where(flip == 0, low, top)
            logs = jnp.where(lane == head, log_sum[rows], logs)
    high_term = logs.astype(jnp.bfloat16).astype(jnp.float32)
    rest = logs - high_term
    mid_term = rest.astype(jnp.bfloat16).astype(jnp.float32)
    low_term = rest - mid_term
    packed = (
        high_term + pltpu.roll(mid_term, HEAD_FAN, 1) + pltpu.roll(low_term, 2 * HEAD_FAN, 1)
    ).astype(jnp.bfloat16)
    top = packed[:HALF_ROWS]
    low = packed[HALF_ROWS:]
    out_ref[0, 0, :, HEAD_FAN * HEAD_SIZE :] = jnp.where(flip == 0, top, low)
    out_ref[0, 1, :, HEAD_FAN * HEAD_SIZE :] = jnp.where(flip == 0, low, top)


def attend(order, local, reach, place, sent, pages, suffix, cosine, sine, gain):
    block = PROMPT_TOKENS // SHARDS
    return pl.pallas_call(
        attend_kernel,
        grid_spec=pltpu.PrefetchScalarGridSpec(
            num_scalar_prefetch=4,
            grid=(GROUPS,),
            in_specs=[
                pl.BlockSpec((1, 2, SLOT_ROWS, SENT_WIDTH), lambda i, o, l, r, p: (o[i], 0, 0, 0)),
                pl.BlockSpec(
                    (GROUPS, 1, block, 2 * HEAD_SIZE), lambda i, o, l, r, p: (0, l[i], 0, 0)
                ),
                pl.BlockSpec(
                    (1, suffix.shape[1], 2 * HEAD_SIZE), lambda i, o, l, r, p: (r[i], 0, 0)
                ),
                pl.BlockSpec((1, SLOT_ROWS, HEAD_SIZE), lambda i, o, l, r, p: (r[i], 0, 0)),
                pl.BlockSpec((1, SLOT_ROWS, HEAD_SIZE), lambda i, o, l, r, p: (r[i], 0, 0)),
                pl.BlockSpec((1, HEAD_SIZE), lambda i, o, l, r, p: (0, 0)),
            ],
            out_specs=pl.BlockSpec(
                (1, 2, HALF_ROWS, BACK_WIDTH), lambda i, o, l, r, p: (o[i], 0, 0, 0)
            ),
        ),
        out_shape=jax.ShapeDtypeStruct((GROUPS, 2, HALF_ROWS, BACK_WIDTH), jnp.bfloat16),
        compiler_params=pltpu.CompilerParams(vmem_limit_bytes=60 * 2**20),
        cost_estimate=pl.CostEstimate(
            flops=2 * GROUPS * 512 * 2432 * 384,
            bytes_accessed=8_000_000,
            transcendentals=GROUPS * 512 * 2432,
        ),
        name="attend",
    )(order, local, reach, place, sent, pages, suffix, cosine, sine, gain)


def output_kernel(place_ref, back_ref, own_ref, other_ref, out_ref, mixed):
    half = place_ref[0]
    rows = GROUPS * HALF_ROWS

    @pl.when(pl.program_id(0) == 0)
    def _():
        lane = lax.broadcasted_iota(jnp.int32, (rows, HEAD_SIZE), 1)

        def log_of(source):
            packed = back_ref[:, source, :, HEAD_FAN * HEAD_SIZE :]
            packed = packed.reshape(rows, HEAD_SIZE).astype(jnp.float32)
            return (
                packed
                + pltpu.roll(packed, HEAD_SIZE - HEAD_FAN, 1)
                + pltpu.roll(packed, HEAD_SIZE - 2 * HEAD_FAN, 1)
            )

        first_log = log_of(0)
        second_log = log_of(1)
        peak = jnp.maximum(first_log, second_log)
        first_part = jnp.exp2(first_log - peak)
        second_part = jnp.exp2(second_log - peak)
        both = first_part + second_part
        first_part = first_part / both
        second_part = second_part / both

        def attended(head):
            lanes = slice(head * HEAD_SIZE, (head + 1) * HEAD_SIZE)
            first = back_ref[:, 0, :, lanes].reshape(rows, HEAD_SIZE).astype(jnp.float32)
            second = back_ref[:, 1, :, lanes].reshape(rows, HEAD_SIZE).astype(jnp.float32)
            return (
                first * first_part[:, head : head + 1] + second * second_part[:, head : head + 1]
            ).astype(jnp.bfloat16)

        for head in range(OWN_HEADS):
            low = attended(head)
            high = attended(head + OWN_HEADS)
            lanes = slice(head * HEAD_SIZE, (head + 1) * HEAD_SIZE)
            mixed[0, :, lanes] = jnp.where(half == 0, low, high)
            mixed[1, :, lanes] = jnp.where(half == 0, high, low)

    out_ref[...] = (
        jnp.dot(mixed[0], own_ref[...], preferred_element_type=jnp.float32)
        + jnp.dot(mixed[1], other_ref[...], preferred_element_type=jnp.float32)
    ).astype(jnp.bfloat16)


def output_part(place, back, own_weight, other_weight):
    tile = 1024
    rows = GROUPS * HALF_ROWS
    return pl.pallas_call(
        output_kernel,
        grid_spec=pltpu.PrefetchScalarGridSpec(
            num_scalar_prefetch=1,
            grid=(MODEL_WIDTH // tile,),
            in_specs=[
                pl.BlockSpec((GROUPS, 2, HALF_ROWS, BACK_WIDTH), lambda n, p: (0, 0, 0, 0)),
                pl.BlockSpec((OWN_WIDTH, tile), lambda n, p: (0, n)),
                pl.BlockSpec((OWN_WIDTH, tile), lambda n, p: (0, n)),
            ],
            out_specs=pl.BlockSpec((rows, tile), lambda n, p: (0, n)),
            scratch_shapes=[pltpu.VMEM((2, rows, OWN_WIDTH), jnp.bfloat16)],
        ),
        out_shape=jax.ShapeDtypeStruct((rows, MODEL_WIDTH), jnp.bfloat16),
        compiler_params=pltpu.CompilerParams(vmem_limit_bytes=60 * 2**20),
        cost_estimate=pl.CostEstimate(
            flops=2 * rows * MODEL_WIDTH * 1024, bytes_accessed=14_000_000, transcendentals=0
        ),
        name="output_part",
    )(place, back, own_weight, other_weight)


def along_x(distance):
    return [(shard, shard // 4 * 4 + (shard + distance) % 4) for shard in range(SHARDS)]


def along_y(distance):
    return [(shard, (shard + 4 * distance) % SHARDS) for shard in range(SHARDS)]


def swap(block, axes, groups=None):
    return lax.all_to_all(
        block, axes, split_axis=0, concat_axis=0, tiled=True, axis_index_groups=groups
    )


def shards(
    tokens,
    prompt_cache,
    generated_cache,
    suffix_lengths,
    fanout,
    prompt_adapter,
    query_weight,
    key_value_weight,
    output_weight,
    adapter_down_maps,
    adapter_up_maps,
    query_norm_gain,
    key_norm_gain,
):
    group = lax.axis_index("grp")
    shard = lax.axis_index("ad")
    head = shard // 2
    half = shard % 2
    local_table = slot_prompts(fanout, GROUPS, OWNED)

    part_rows = lax.all_gather(tokens, "ad", axis=0, tiled=True)

    owners = jnp.arange(GROUPS, dtype=jnp.int32)
    local_of_slot = lax.dynamic_index_in_dim(local_table, group, 1, keepdims=False)
    prompts = owners * OWNED + local_of_slot
    hit = prompts[:, None] == jnp.arange(prompt_adapter.shape[0], dtype=jnp.int32)[None, :]
    tasks = jnp.sum(hit.astype(jnp.int32) * prompt_adapter[None, :], axis=1)
    own_rows = tokens.shape[0]
    columns = swap(jnp.swapaxes(tokens.reshape(own_rows, SHARDS, -1), 0, 1), "ad")
    rank_all = jnp.dot(
        columns.reshape(ROWS, -1),
        adapter_down_maps.reshape(-1, ADAPTER_COUNT * ADAPTER_RANK),
        preferred_element_type=jnp.float32,
    ).reshape(GROUPS, SLOT_ROWS, ADAPTER_COUNT, ADAPTER_RANK)
    chosen = (tasks[:, None] == jnp.arange(ADAPTER_COUNT, dtype=jnp.int32)[None, :]).astype(
        jnp.float32
    )
    rank_part = jnp.sum(rank_all * chosen[:, None, :, None], axis=2)
    rank_rows = jnp.sum(swap(rank_part.reshape(SHARDS, own_rows, ADAPTER_RANK), "ad"), axis=0)
    rank_rows = rank_rows.astype(jnp.bfloat16)

    rank_rows, page_source, suffix_source, weight_source = lax.optimization_barrier(
        (rank_rows, prompt_cache, generated_cache, output_weight)
    )

    arrived = swap(jnp.swapaxes(page_source, 0, 1), "ad", ROLE_GROUPS)

    ring = [rank_rows] + [lax.ppermute(rank_rows, "ad", along_x(k)) for k in (1, 2, 3)]
    ring = jnp.stack(ring)
    low_rank = jnp.stack([ring] + [lax.ppermute(ring, "ad", along_y(k)) for k in (1, 2, 3)])
    every = jnp.arange(SHARDS, dtype=jnp.int32)
    spots = ((shard // 4 - every // 4) % 4) * 4 + (shard % 4 - every % 4) % 4

    slot_suffix = suffix_source.reshape(GROUPS, SLOT_SAMPLES * 16, 2 * HEAD_SIZE)
    slot_lengths = suffix_lengths.reshape(GROUPS, SLOT_SAMPLES, 1).astype(jnp.bfloat16)
    slot_suffix = jnp.concatenate(
        [slot_suffix, jnp.broadcast_to(slot_lengths, (GROUPS, SLOT_SAMPLES, 2 * HEAD_SIZE))], axis=1
    )
    suffix = []
    for k in range(GROUPS):
        block = lax.dynamic_index_in_dim(slot_suffix, group ^ k, 0, keepdims=False)
        if k:
            block = lax.ppermute(block, "grp", [(g, g ^ k) for g in range(GROUPS)])
        suffix.append(block)
    suffix = jnp.stack(suffix)

    slice_rows = OWN_WIDTH // GROUPS
    weight_slice = lax.dynamic_slice_in_dim(weight_source, group * slice_rows, slice_rows, 0)
    other_weight = lax.all_gather(
        lax.ppermute(weight_slice, "ad", PARTNERS), "grp", axis=0, tiled=True
    )

    steps = jnp.arange(DECODE_STEPS, dtype=jnp.int32)
    position = (PROMPT_TOKENS + suffix_lengths[:, None] + steps[None, :]).astype(jnp.float32)
    cosine, sine = angle_tables(position.reshape(ROWS))
    sent = project(
        tasks,
        spots,
        part_rows,
        query_weight,
        key_value_weight.transpose(1, 2, 0).reshape(HEAD_SIZE, MODEL_WIDTH),
        low_rank.reshape(SHARDS, own_rows, ADAPTER_RANK),
        adapter_up_maps,
        cosine,
        sine,
        query_norm_gain.reshape(1, HEAD_SIZE),
    )
    received = swap(
        jnp.broadcast_to(
            sent.reshape(GROUPS, 1, SLOT_ROWS, SENT_WIDTH), (GROUPS, 2, SLOT_ROWS, SENT_WIDTH)
        ).reshape(2 * GROUPS, SLOT_ROWS, SENT_WIDTH),
        ("grp", "ad"),
        HEAD_GROUPS,
    ).reshape(GROUPS, 2, SLOT_ROWS, SENT_WIDTH)

    local = lax.dynamic_index_in_dim(local_table, group, 0, keepdims=False)
    rank_key = local * GROUPS + owners
    spot = jnp.sum((rank_key[None, :] < rank_key[:, None]).astype(jnp.int32), axis=1)
    placed = (spot[None, :] == owners[:, None]).astype(jnp.int32)
    order = jnp.sum(placed * owners[None, :], axis=1)
    local_sorted = jnp.sum(placed * local[None, :], axis=1)
    flip = (head + group) % 2
    place = jnp.stack([half, flip]).astype(jnp.int32)
    far_lengths = suffix[:, SLOT_SAMPLES * 16 :, 0].astype(jnp.float32)
    far_position = PROMPT_TOKENS + far_lengths[:, :, None] + steps.astype(jnp.float32)
    far_cosine, far_sine = angle_tables(far_position.reshape(GROUPS, SLOT_ROWS))
    partial = attend(
        order,
        local_sorted,
        order ^ group,
        place,
        received,
        arrived,
        suffix,
        far_cosine,
        far_sine,
        key_norm_gain.reshape(1, HEAD_SIZE),
    )
    back = swap(
        partial.reshape(2 * GROUPS, HALF_ROWS, BACK_WIDTH), ("grp", "ad"), HEAD_GROUPS
    ).reshape(GROUPS, 2, HALF_ROWS, BACK_WIDTH)
    product = output_part(place, back, output_weight, other_weight)
    blocks = swap(product.reshape(GROUPS, HALF_ROWS, MODEL_WIDTH), "ad", ROLE_GROUPS)
    return jnp.sum(blocks.astype(jnp.float32), axis=0).astype(jnp.bfloat16)


def solution(mesh):
    return jax.shard_map(
        shards,
        mesh=mesh,
        in_specs=(
            P(("grp", "ad"), None),
            P("grp", None, "ad", None),
            P("grp", "ad", None),
            P("grp"),
            P(),
            P(),
            P(None, "ad"),
            P(None, None, "ad"),
            P("ad", None),
            P("ad", None, None),
            P(None, None, "ad"),
            P(),
            P(),
        ),
        out_specs=P(("grp", "ad"), None),
        check_vma=False,
    )
```

```python
import functools

import jax
import jax.numpy as jnp
from jax import lax
from jax.experimental import pallas as pl
from jax.experimental.pallas import tpu as pltpu
from jax.sharding import PartitionSpec as P

MODEL_WIDTH = 5120
KEY_VALUE_HEADS = 8
HEAD_SIZE = 128
ADAPTER_RANK = 128
FAN = 2
DECODE_STEPS = 4
ADAPTER_COUNT = 4
PROMPT_TOKENS = 4096
GROUPS = 8
SHARDS = 16
OWNED = 4
SLOT_SAMPLES = 16
SLOT_ROWS = SLOT_SAMPLES * DECODE_STEPS
HALF_ROWS = SLOT_ROWS // 2
ROWS = GROUPS * SLOT_ROWS
OWN_HEADS = 4
OWN_WIDTH = OWN_HEADS * HEAD_SIZE
HEAD_FAN = 2 * OWN_HEADS
SENT_WIDTH = OWN_WIDTH + HEAD_SIZE
BACK_WIDTH = HEAD_FAN * HEAD_SIZE + HEAD_SIZE

theta_base = 1000000.0
norm_eps = 1e-06
masked_low = -1e30
exponent_scale = HEAD_SIZE**-0.5 * 1.4426950408889634

ROLE_GROUPS = [[0, 3, 4, 7, 8, 11, 12, 15], [1, 2, 5, 6, 9, 10, 13, 14]]
HEAD_GROUPS = [
    [group * SHARDS + 2 * head + half for group in range(GROUPS) for half in range(2)]
    for head in range(KEY_VALUE_HEADS)
]
PARTNERS = [(shard, shard ^ 1) for shard in range(SHARDS)]


def slot_prompts(fanout, groups, owned_count):
    listed = jnp.any(
        fanout[:, :, None] == jnp.arange(groups, dtype=jnp.int32)[None, None, :], axis=1
    )
    listed = listed.astype(jnp.int32).reshape(groups, owned_count, groups)
    return jnp.sum(listed * jnp.arange(owned_count, dtype=jnp.int32)[None, :, None], axis=1)


def angle_tables(position):
    half_len = HEAD_SIZE // 2
    inverse = theta_base ** (-2.0 * jnp.arange(half_len, dtype=jnp.float32) / HEAD_SIZE)
    angles = position[..., None] * inverse
    cosine = jnp.cos(angles)
    sine = jnp.sin(angles)
    return (
        jnp.concatenate([cosine, cosine], axis=-1),
        jnp.concatenate([-sine, sine], axis=-1),
    )


def norm_rotate(vector, gain, cosine, sine):
    mean_sq = jnp.mean(vector * vector, axis=-1, keepdims=True)
    scaled = vector * lax.rsqrt(mean_sq + norm_eps) * gain
    return scaled * cosine + pltpu.roll(scaled, HEAD_SIZE // 2, 1) * sine


def dot_nt(left, right):
    return lax.dot_general(
        left, right, (((1,), (1,)), ((), ())), preferred_element_type=jnp.float32
    )


def project_kernel(
    task_ref,
    spot_ref,
    tokens_ref,
    query_ref,
    keyval_ref,
    rank_ref,
    up_ref,
    cos_ref,
    sin_ref,
    gain_ref,
    out_ref,
    query_sum,
    keyval_sum,
):
    step = pl.program_id(0)

    @pl.when(step == 0)
    def _():
        query_sum[...] = jnp.zeros_like(query_sum)
        keyval_sum[...] = jnp.zeros_like(keyval_sum)

    part = tokens_ref[...]
    query_sum[...] += jnp.dot(part, query_ref[...], preferred_element_type=jnp.float32)
    keyval_sum[...] += dot_nt(part, keyval_ref[...])

    @pl.when(step == pl.num_programs(0) - 1)
    def _():
        for slot in range(GROUPS):
            rows = slice(slot * SLOT_ROWS, (slot + 1) * SLOT_ROWS)
            low_rank = jnp.concatenate(
                [rank_ref[spot_ref[2 * slot]], rank_ref[spot_ref[2 * slot + 1]]], axis=0
            )
            query = query_sum[rows, :] + jnp.dot(
                low_rank, up_ref[task_ref[slot]], preferred_element_type=jnp.float32
            )
            for head in range(OWN_HEADS):
                lanes = slice(head * HEAD_SIZE, (head + 1) * HEAD_SIZE)
                turned = norm_rotate(
                    query[:, lanes], gain_ref[...], cos_ref[rows, :], sin_ref[rows, :]
                ).astype(jnp.bfloat16)
                out_ref[slot, 0, :, lanes] = turned
                out_ref[slot, 1, :, lanes] = turned
            keyval = keyval_sum[rows, :].astype(jnp.bfloat16)
            out_ref[slot, 0, :, OWN_WIDTH:] = keyval
            out_ref[slot, 1, :, OWN_WIDTH:] = keyval


def project(tasks, spots, tokens, query_weight, keyval_weight, low_rank, up_maps, cosine, sine, gain):
    tile = 1280
    whole = lambda *shape: pl.BlockSpec(shape, lambda k, t, s: (0,) * len(shape))
    return pl.pallas_call(
        project_kernel,
        grid_spec=pltpu.PrefetchScalarGridSpec(
            num_scalar_prefetch=2,
            grid=(MODEL_WIDTH // tile,),
            in_specs=[
                pl.BlockSpec((ROWS, tile), lambda k, t, s: (0, k)),
                pl.BlockSpec((tile, OWN_WIDTH), lambda k, t, s: (k, 0)),
                pl.BlockSpec((HEAD_SIZE, tile), lambda k, t, s: (0, k)),
                whole(SHARDS, HALF_ROWS, ADAPTER_RANK),
                whole(ADAPTER_COUNT, ADAPTER_RANK, OWN_WIDTH),
                whole(ROWS, HEAD_SIZE),
                whole(ROWS, HEAD_SIZE),
                whole(1, HEAD_SIZE),
            ],
            out_specs=whole(GROUPS, 2, SLOT_ROWS, SENT_WIDTH),
            scratch_shapes=[
                pltpu.VMEM((ROWS, OWN_WIDTH), jnp.float32),
                pltpu.VMEM((ROWS, HEAD_SIZE), jnp.float32),
            ],
        ),
        out_shape=jax.ShapeDtypeStruct((GROUPS, 2, SLOT_ROWS, SENT_WIDTH), jnp.bfloat16),
        compiler_params=pltpu.CompilerParams(vmem_limit_bytes=60 * 2**20),
        cost_estimate=pl.CostEstimate(
            flops=2 * ROWS * MODEL_WIDTH * SENT_WIDTH, bytes_accessed=13_000_000, transcendentals=0
        ),
        name="project",
    )(tasks, spots, tokens, query_weight, keyval_weight, low_rank, up_maps, cosine, sine, gain)


def attend_kernel(
    order_ref,
    local_ref,
    reach_ref,
    place_ref,
    sent_ref,
    page_ref,
    suffix_ref,
    cos_ref,
    sin_ref,
    gain_ref,
    out_ref,
):
    half = place_ref[0]
    flip = place_ref[1]
    span = GROUPS * PROMPT_TOKENS // SHARDS
    pages = page_ref[...].reshape(span, 2 * HEAD_SIZE)
    keys = pages[:, :HEAD_SIZE]
    values = jnp.concatenate(
        [jnp.ones((span, HEAD_SIZE), jnp.bfloat16), pages[:, HEAD_SIZE:]], axis=1
    )
    low_part = sent_ref[0, 0, :, OWN_WIDTH:].astype(jnp.float32)
    high_part = sent_ref[0, 1, :, OWN_WIDTH:].astype(jnp.float32)
    lane = lax.broadcasted_iota(jnp.int32, (SLOT_ROWS, HEAD_SIZE), 1)
    low_lanes = lane < HEAD_SIZE // 2
    new_keys = jnp.where(low_lanes, low_part, pltpu.roll(high_part, HEAD_SIZE // 2, 1))
    new_values = jnp.where(low_lanes, pltpu.roll(low_part, HEAD_SIZE // 2, 1), high_part)
    new_keys = norm_rotate(new_keys, gain_ref[...], cos_ref[0], sin_ref[0])
    suffix_rows = SLOT_SAMPLES * 16
    extra = suffix_rows + 2 * SLOT_ROWS
    suffix = suffix_ref[0, :suffix_rows, :]
    zeros = jnp.zeros((SLOT_ROWS, HEAD_SIZE), jnp.bfloat16)
    extra_keys = jnp.concatenate(
        [suffix[:, :HEAD_SIZE], new_keys.astype(jnp.bfloat16), zeros], axis=0
    )
    extra_values = jnp.concatenate(
        [suffix[:, HEAD_SIZE:], new_values.astype(jnp.bfloat16), zeros], axis=0
    )
    extra_values = jnp.concatenate(
        [jnp.ones((extra, HEAD_SIZE), jnp.bfloat16), extra_values], axis=1
    )
    lengths = suffix_ref[0, suffix_rows:, :].astype(jnp.float32)
    sample_of = lax.broadcasted_iota(jnp.int32, (SLOT_SAMPLES, suffix_rows), 0)
    column_sample = lax.broadcasted_iota(jnp.int32, (SLOT_SAMPLES, suffix_rows), 1) // 16
    column_length = jnp.sum(
        jnp.where(sample_of == column_sample, lengths, 0.0), axis=0, keepdims=True
    )
    row = lax.broadcasted_iota(jnp.int32, (SLOT_ROWS, suffix_rows), 0)
    column = lax.broadcasted_iota(jnp.int32, (SLOT_ROWS, suffix_rows), 1)
    suffix_seen = (row // DECODE_STEPS == column // 16) & (
        (half * 16 + column % 16).astype(jnp.float32) < column_length
    )
    row = lax.broadcasted_iota(jnp.int32, (SLOT_ROWS, 2 * SLOT_ROWS), 0)
    column = lax.broadcasted_iota(jnp.int32, (SLOT_ROWS, 2 * SLOT_ROWS), 1)
    new_seen = (
        (row // DECODE_STEPS == column // DECODE_STEPS)
        & (column % DECODE_STEPS <= row % DECODE_STEPS)
        & (column // HALF_ROWS == half)
    )
    bias = jnp.concatenate(
        [jnp.where(suffix_seen, 0.0, masked_low), jnp.where(new_seen, 0.0, masked_low)], axis=1
    )
    pair_bias = jnp.concatenate([bias, bias], axis=0)
    logs = jnp.zeros((SLOT_ROWS, HEAD_SIZE), jnp.float32)
    for first in range(0, HEAD_FAN, 2):
        source, start = divmod(first, OWN_HEADS)
        start = start * HEAD_SIZE
        query = jnp.concatenate(
            [
                sent_ref[0, source, :, start : start + HEAD_SIZE],
                sent_ref[0, source, :, start + HEAD_SIZE : start + 2 * HEAD_SIZE],
            ],
            axis=0,
        )
        prefix_score = dot_nt(query, keys)
        extra_score = dot_nt(query, extra_keys) + pair_bias
        peak = jnp.maximum(
            jnp.max(prefix_score, axis=-1, keepdims=True),
            jnp.max(extra_score, axis=-1, keepdims=True),
        )
        scaled_peak = peak * exponent_scale
        prefix_weight = jnp.exp2(prefix_score * exponent_scale - scaled_peak).astype(jnp.bfloat16)
        extra_weight = jnp.exp2(extra_score * exponent_scale - scaled_peak).astype(jnp.bfloat16)
        total = jnp.dot(prefix_weight, values, preferred_element_type=jnp.float32) + jnp.dot(
            extra_weight, extra_values, preferred_element_type=jnp.float32
        )
        denominator = total[:, :HEAD_SIZE]
        attended = total[:, HEAD_SIZE:] / denominator
        log_sum = scaled_peak + jnp.log2(denominator)
        for index in range(2):
            head = first + index
            rows = slice(index * SLOT_ROWS, (index + 1) * SLOT_ROWS)
            top = attended[index * SLOT_ROWS : index * SLOT_ROWS + HALF_ROWS].astype(jnp.bfloat16)
            low = attended[index * SLOT_ROWS + HALF_ROWS : (index + 1) * SLOT_ROWS].astype(
                jnp.bfloat16
            )
            lanes = slice(head * HEAD_SIZE, (head + 1) * HEAD_SIZE)
            out_ref[0, 0, :, lanes] = jnp.where(flip == 0, top, low)
            out_ref[0, 1, :, lanes] = jnp.where(flip == 0, low, top)
            logs = jnp.where(lane == head, log_sum[rows], logs)
    high_term = logs.astype(jnp.bfloat16).astype(jnp.float32)
    rest = logs - high_term
    mid_term = rest.astype(jnp.bfloat16).astype(jnp.float32)
    low_term = rest - mid_term
    packed = (
        high_term + pltpu.roll(mid_term, HEAD_FAN, 1) + pltpu.roll(low_term, 2 * HEAD_FAN, 1)
    ).astype(jnp.bfloat16)
    top = packed[:HALF_ROWS]
    low = packed[HALF_ROWS:]
    out_ref[0, 0, :, HEAD_FAN * HEAD_SIZE :] = jnp.where(flip == 0, top, low)
    out_ref[0, 1, :, HEAD_FAN * HEAD_SIZE :] = jnp.where(flip == 0, low, top)


def attend(order, local, reach, place, sent, pages, suffix, cosine, sine, gain):
    block = PROMPT_TOKENS // SHARDS
    return pl.pallas_call(
        attend_kernel,
        grid_spec=pltpu.PrefetchScalarGridSpec(
            num_scalar_prefetch=4,
            grid=(GROUPS,),
            in_specs=[
                pl.BlockSpec((1, 2, SLOT_ROWS, SENT_WIDTH), lambda i, o, l, r, p: (o[i], 0, 0, 0)),
                pl.BlockSpec(
                    (GROUPS, 1, block, 2 * HEAD_SIZE), lambda i, o, l, r, p: (0, l[i], 0, 0)
                ),
                pl.BlockSpec(
                    (1, suffix.shape[1], 2 * HEAD_SIZE), lambda i, o, l, r, p: (r[i], 0, 0)
                ),
                pl.BlockSpec((1, SLOT_ROWS, HEAD_SIZE), lambda i, o, l, r, p: (r[i], 0, 0)),
                pl.BlockSpec((1, SLOT_ROWS, HEAD_SIZE), lambda i, o, l, r, p: (r[i], 0, 0)),
                pl.BlockSpec((1, HEAD_SIZE), lambda i, o, l, r, p: (0, 0)),
            ],
            out_specs=pl.BlockSpec(
                (1, 2, HALF_ROWS, BACK_WIDTH), lambda i, o, l, r, p: (o[i], 0, 0, 0)
            ),
        ),
        out_shape=jax.ShapeDtypeStruct((GROUPS, 2, HALF_ROWS, BACK_WIDTH), jnp.bfloat16),
        compiler_params=pltpu.CompilerParams(vmem_limit_bytes=60 * 2**20),
        cost_estimate=pl.CostEstimate(
            flops=2 * GROUPS * 512 * 2432 * 384,
            bytes_accessed=8_000_000,
            transcendentals=GROUPS * 512 * 2432,
        ),
        name="attend",
    )(order, local, reach, place, sent, pages, suffix, cosine, sine, gain)


def output_kernel(place_ref, back_ref, own_ref, other_ref, out_ref, mixed):
    half = place_ref[0]
    rows = GROUPS * HALF_ROWS

    @pl.when(pl.program_id(0) == 0)
    def _():
        lane = lax.broadcasted_iota(jnp.int32, (rows, HEAD_SIZE), 1)

        def log_of(source):
            packed = back_ref[:, source, :, HEAD_FAN * HEAD_SIZE :]
            packed = packed.reshape(rows, HEAD_SIZE).astype(jnp.float32)
            return (
                packed
                + pltpu.roll(packed, HEAD_SIZE - HEAD_FAN, 1)
                + pltpu.roll(packed, HEAD_SIZE - 2 * HEAD_FAN, 1)
            )

        first_log = log_of(0)
        second_log = log_of(1)
        peak = jnp.maximum(first_log, second_log)
        first_part = jnp.exp2(first_log - peak)
        second_part = jnp.exp2(second_log - peak)
        both = first_part + second_part
        first_part = first_part / both
        second_part = second_part / both

        def attended(head):
            lanes = slice(head * HEAD_SIZE, (head + 1) * HEAD_SIZE)
            first = back_ref[:, 0, :, lanes].reshape(rows, HEAD_SIZE).astype(jnp.float32)
            second = back_ref[:, 1, :, lanes].reshape(rows, HEAD_SIZE).astype(jnp.float32)
            return (
                first * first_part[:, head : head + 1] + second * second_part[:, head : head + 1]
            ).astype(jnp.bfloat16)

        for head in range(OWN_HEADS):
            low = attended(head)
            high = attended(head + OWN_HEADS)
            lanes = slice(head * HEAD_SIZE, (head + 1) * HEAD_SIZE)
            mixed[0, :, lanes] = jnp.where(half == 0, low, high)
            mixed[1, :, lanes] = jnp.where(half == 0, high, low)

    out_ref[...] = (
        jnp.dot(mixed[0], own_ref[...], preferred_element_type=jnp.float32)
        + jnp.dot(mixed[1], other_ref[...], preferred_element_type=jnp.float32)
    ).astype(jnp.bfloat16)


def output_part(place, back, own_weight, other_weight):
    tile = 1024
    rows = GROUPS * HALF_ROWS
    return pl.pallas_call(
        output_kernel,
        grid_spec=pltpu.PrefetchScalarGridSpec(
            num_scalar_prefetch=1,
            grid=(MODEL_WIDTH // tile,),
            in_specs=[
                pl.BlockSpec((GROUPS, 2, HALF_ROWS, BACK_WIDTH), lambda n, p: (0, 0, 0, 0)),
                pl.BlockSpec((OWN_WIDTH, tile), lambda n, p: (0, n)),
                pl.BlockSpec((OWN_WIDTH, tile), lambda n, p: (0, n)),
            ],
            out_specs=pl.BlockSpec((rows, tile), lambda n, p: (0, n)),
            scratch_shapes=[pltpu.VMEM((2, rows, OWN_WIDTH), jnp.bfloat16)],
        ),
        out_shape=jax.ShapeDtypeStruct((rows, MODEL_WIDTH), jnp.bfloat16),
        compiler_params=pltpu.CompilerParams(vmem_limit_bytes=60 * 2**20),
        cost_estimate=pl.CostEstimate(
            flops=2 * rows * MODEL_WIDTH * 1024, bytes_accessed=14_000_000, transcendentals=0
        ),
        name="output_part",
    )(place, back, own_weight, other_weight)


def along_x(distance):
    return [(shard, shard // 4 * 4 + (shard + distance) % 4) for shard in range(SHARDS)]


def along_y(distance):
    return [(shard, (shard + 4 * distance) % SHARDS) for shard in range(SHARDS)]


def across_groups(bits):
    return [(group, group ^ bits) for group in range(GROUPS)]


def swap(block, axes, groups=None):
    return lax.all_to_all(
        block, axes, split_axis=0, concat_axis=0, tiled=True, axis_index_groups=groups
    )


def shards(
    tokens,
    prompt_cache,
    generated_cache,
    suffix_lengths,
    fanout,
    prompt_adapter,
    query_weight,
    key_value_weight,
    output_weight,
    adapter_down_maps,
    adapter_up_maps,
    query_norm_gain,
    key_norm_gain,
):
    group = lax.axis_index("grp")
    shard = lax.axis_index("ad")
    head = shard // 2
    half = shard % 2
    local_table = slot_prompts(fanout, GROUPS, OWNED)

    part_rows = lax.all_gather(tokens, "ad", axis=0, tiled=True)

    slot_suffix = generated_cache.reshape(GROUPS, SLOT_SAMPLES * 16, 2 * HEAD_SIZE)
    slot_lengths = suffix_lengths.reshape(GROUPS, SLOT_SAMPLES, 1).astype(jnp.bfloat16)
    slot_suffix = jnp.concatenate(
        [slot_suffix, jnp.broadcast_to(slot_lengths, (GROUPS, SLOT_SAMPLES, 2 * HEAD_SIZE))], axis=1
    )
    by_core = slot_suffix.reshape((GROUPS // 2, 2) + slot_suffix.shape[1:])
    kept = lax.dynamic_index_in_dim(by_core, group % 2, 1, keepdims=True)
    given = lax.dynamic_index_in_dim(by_core, 1 - group % 2, 1, keepdims=True)
    given = lax.ppermute(given, "grp", across_groups(1))
    both = jnp.concatenate([kept, given], axis=1)
    suffix = []
    for k in range(GROUPS // 2):
        block = lax.dynamic_index_in_dim(both, (group // 2) ^ k, 0, keepdims=False)
        suffix.append(lax.ppermute(block, "grp", across_groups(2 * k)) if k else block)
    suffix = jnp.concatenate(suffix, axis=0)

    owners = jnp.arange(GROUPS, dtype=jnp.int32)
    local_of_slot = lax.dynamic_index_in_dim(local_table, group, 1, keepdims=False)
    prompts = owners * OWNED + local_of_slot
    hit = prompts[:, None] == jnp.arange(prompt_adapter.shape[0], dtype=jnp.int32)[None, :]
    tasks = jnp.sum(hit.astype(jnp.int32) * prompt_adapter[None, :], axis=1)
    own_rows = tokens.shape[0]
    columns = swap(jnp.swapaxes(tokens.reshape(own_rows, SHARDS, -1), 0, 1), "ad")
    rank_all = jnp.dot(
        columns.reshape(ROWS, -1),
        adapter_down_maps.reshape(-1, ADAPTER_COUNT * ADAPTER_RANK),
        preferred_element_type=jnp.float32,
    ).reshape(GROUPS, SLOT_ROWS, ADAPTER_COUNT, ADAPTER_RANK)
    chosen = (tasks[:, None] == jnp.arange(ADAPTER_COUNT, dtype=jnp.int32)[None, :]).astype(
        jnp.float32
    )
    rank_part = jnp.sum(rank_all * chosen[:, None, :, None], axis=2)
    rank_part, suffix = lax.optimization_barrier((rank_part, suffix))
    rank_rows = jnp.sum(swap(rank_part.reshape(SHARDS, own_rows, ADAPTER_RANK), "ad"), axis=0)
    rank_rows = rank_rows.astype(jnp.bfloat16)

    rank_rows, head_pages = lax.optimization_barrier((rank_rows, jnp.swapaxes(prompt_cache, 0, 1)))
    arrived = swap(head_pages, "ad", ROLE_GROUPS)

    ring = [rank_rows] + [lax.ppermute(rank_rows, "ad", along_x(k)) for k in (1, 2, 3)]
    ring = jnp.stack(ring)
    low_rank = jnp.stack([ring] + [lax.ppermute(ring, "ad", along_y(k)) for k in (1, 2, 3)])
    every = jnp.arange(SHARDS, dtype=jnp.int32)
    spots = ((shard // 4 - every // 4) % 4) * 4 + (shard % 4 - every % 4) % 4

    part_rows, weight_source = lax.optimization_barrier((part_rows, output_weight))
    slice_rows = OWN_WIDTH // GROUPS
    weight_slice = lax.dynamic_slice_in_dim(weight_source, group * slice_rows, slice_rows, 0)
    other_weight = lax.all_gather(
        lax.ppermute(weight_slice, "ad", PARTNERS), "grp", axis=0, tiled=True
    )

    steps = jnp.arange(DECODE_STEPS, dtype=jnp.int32)
    position = (PROMPT_TOKENS + suffix_lengths[:, None] + steps[None, :]).astype(jnp.float32)
    cosine, sine = angle_tables(position.reshape(ROWS))
    sent = project(
        tasks,
        spots,
        part_rows,
        query_weight,
        key_value_weight.transpose(1, 2, 0).reshape(HEAD_SIZE, MODEL_WIDTH),
        low_rank.reshape(SHARDS, own_rows, ADAPTER_RANK),
        adapter_up_maps,
        cosine,
        sine,
        query_norm_gain.reshape(1, HEAD_SIZE),
    )
    received = swap(
        sent.reshape(2 * GROUPS, SLOT_ROWS, SENT_WIDTH), ("grp", "ad"), HEAD_GROUPS
    ).reshape(GROUPS, 2, SLOT_ROWS, SENT_WIDTH)

    local = lax.dynamic_index_in_dim(local_table, group, 0, keepdims=False)
    rank_key = local * GROUPS + owners
    spot = jnp.sum((rank_key[None, :] < rank_key[:, None]).astype(jnp.int32), axis=1)
    placed = (spot[None, :] == owners[:, None]).astype(jnp.int32)
    order = jnp.sum(placed * owners[None, :], axis=1)
    local_sorted = jnp.sum(placed * local[None, :], axis=1)
    flip = (head + group) % 2
    place = jnp.stack([half, flip]).astype(jnp.int32)
    far_lengths = suffix[:, SLOT_SAMPLES * 16 :, 0].astype(jnp.float32)
    far_position = PROMPT_TOKENS + far_lengths[:, :, None] + steps.astype(jnp.float32)
    far_cosine, far_sine = angle_tables(far_position.reshape(GROUPS, SLOT_ROWS))
    partial = attend(
        order,
        local_sorted,
        order ^ group,
        place,
        received,
        arrived,
        suffix,
        far_cosine,
        far_sine,
        key_norm_gain.reshape(1, HEAD_SIZE),
    )
    back = swap(
        partial.reshape(2 * GROUPS, HALF_ROWS, BACK_WIDTH), ("grp", "ad"), HEAD_GROUPS
    ).reshape(GROUPS, 2, HALF_ROWS, BACK_WIDTH)
    product = output_part(place, back, output_weight, other_weight)
    blocks = swap(product.reshape(GROUPS, HALF_ROWS, MODEL_WIDTH), "ad", ROLE_GROUPS)
    return jnp.sum(blocks.astype(jnp.float32), axis=0).astype(jnp.bfloat16)


def solution(mesh):
    return jax.shard_map(
        shards,
        mesh=mesh,
        in_specs=(
            P(("grp", "ad"), None),
            P("grp", None, "ad", None),
            P("grp", "ad", None),
            P("grp"),
            P(),
            P(),
            P(None, "ad"),
            P(None, None, "ad"),
            P("ad", None),
            P("ad", None, None),
            P(None, None, "ad"),
            P(),
            P(),
        ),
        out_specs=P(("grp", "ad"), None),
        check_vma=False,
    )
```

```python
import functools

import jax
import jax.numpy as jnp
from jax import lax
from jax.experimental import pallas as pl
from jax.experimental.pallas import tpu as pltpu
from jax.sharding import PartitionSpec as P

MODEL_WIDTH = 5120
KEY_VALUE_HEADS = 8
HEAD_SIZE = 128
ADAPTER_RANK = 128
FAN = 2
DECODE_STEPS = 4
ADAPTER_COUNT = 4
PROMPT_TOKENS = 4096
GROUPS = 8
SHARDS = 16
OWNED = 4
SLOT_SAMPLES = 16
SLOT_ROWS = SLOT_SAMPLES * DECODE_STEPS
HALF_ROWS = SLOT_ROWS // 2
ROWS = GROUPS * SLOT_ROWS
OWN_HEADS = 4
OWN_WIDTH = OWN_HEADS * HEAD_SIZE
HEAD_FAN = 2 * OWN_HEADS
SENT_WIDTH = OWN_WIDTH + HEAD_SIZE
TILE_HEADS = 4
BACK_WIDTH = HEAD_FAN * HEAD_SIZE + HEAD_SIZE

theta_base = 1000000.0
norm_eps = 1e-06
masked_low = -1e30
exponent_scale = HEAD_SIZE**-0.5 * 1.4426950408889634

ROLE_GROUPS = [[0, 3, 4, 7, 8, 11, 12, 15], [1, 2, 5, 6, 9, 10, 13, 14]]
HEAD_GROUPS = [
    [group * SHARDS + 2 * head + half for group in range(GROUPS) for half in range(2)]
    for head in range(KEY_VALUE_HEADS)
]
PARTNERS = [(shard, shard ^ 1) for shard in range(SHARDS)]


def slot_prompts(fanout, groups, owned_count):
    listed = jnp.any(
        fanout[:, :, None] == jnp.arange(groups, dtype=jnp.int32)[None, None, :], axis=1
    )
    listed = listed.astype(jnp.int32).reshape(groups, owned_count, groups)
    return jnp.sum(listed * jnp.arange(owned_count, dtype=jnp.int32)[None, :, None], axis=1)


def angle_tables(position):
    half_len = HEAD_SIZE // 2
    inverse = theta_base ** (-2.0 * jnp.arange(half_len, dtype=jnp.float32) / HEAD_SIZE)
    angles = position[..., None] * inverse
    cosine = jnp.cos(angles)
    sine = jnp.sin(angles)
    return (
        jnp.concatenate([cosine, cosine], axis=-1),
        jnp.concatenate([-sine, sine], axis=-1),
    )


def norm_rotate(vector, gain, cosine, sine):
    mean_sq = jnp.mean(vector * vector, axis=-1, keepdims=True)
    scaled = vector * lax.rsqrt(mean_sq + norm_eps) * gain
    return scaled * cosine + pltpu.roll(scaled, HEAD_SIZE // 2, 1) * sine


def dot_nt(left, right):
    return lax.dot_general(
        left, right, (((1,), (1,)), ((), ())), preferred_element_type=jnp.float32
    )


def project_kernel(
    task_ref,
    spot_ref,
    tokens_ref,
    query_ref,
    keyval_ref,
    rank_ref,
    up_ref,
    cos_ref,
    sin_ref,
    gain_ref,
    out_ref,
    query_sum,
    keyval_sum,
):
    step = pl.program_id(0)

    @pl.when(step == 0)
    def _():
        query_sum[...] = jnp.zeros_like(query_sum)
        keyval_sum[...] = jnp.zeros_like(keyval_sum)

    part = tokens_ref[...]
    query_sum[...] += jnp.dot(part, query_ref[...], preferred_element_type=jnp.float32)
    keyval_sum[...] += dot_nt(part, keyval_ref[...])

    @pl.when(step == pl.num_programs(0) - 1)
    def _():
        for slot in range(GROUPS):
            rows = slice(slot * SLOT_ROWS, (slot + 1) * SLOT_ROWS)
            low_rank = jnp.concatenate(
                [rank_ref[spot_ref[2 * slot]], rank_ref[spot_ref[2 * slot + 1]]], axis=0
            )
            query = query_sum[rows, :] + jnp.dot(
                low_rank, up_ref[task_ref[slot]], preferred_element_type=jnp.float32
            )
            for head in range(OWN_HEADS):
                lanes = slice(head * HEAD_SIZE, (head + 1) * HEAD_SIZE)
                turned = norm_rotate(
                    query[:, lanes], gain_ref[...], cos_ref[rows, :], sin_ref[rows, :]
                ).astype(jnp.bfloat16)
                out_ref[slot, :, lanes] = turned
            out_ref[slot, :, OWN_WIDTH:] = keyval_sum[rows, :].astype(jnp.bfloat16)


def project(tasks, spots, tokens, query_weight, keyval_weight, low_rank, up_maps, cosine, sine, gain):
    tile = 2560
    whole = lambda *shape: pl.BlockSpec(shape, lambda k, t, s: (0,) * len(shape))
    return pl.pallas_call(
        project_kernel,
        grid_spec=pltpu.PrefetchScalarGridSpec(
            num_scalar_prefetch=2,
            grid=(MODEL_WIDTH // tile,),
            in_specs=[
                pl.BlockSpec((ROWS, tile), lambda k, t, s: (0, k)),
                pl.BlockSpec((tile, OWN_WIDTH), lambda k, t, s: (k, 0)),
                pl.BlockSpec((HEAD_SIZE, tile), lambda k, t, s: (0, k)),
                whole(SHARDS, HALF_ROWS, ADAPTER_RANK),
                whole(ADAPTER_COUNT, ADAPTER_RANK, OWN_WIDTH),
                whole(ROWS, HEAD_SIZE),
                whole(ROWS, HEAD_SIZE),
                whole(1, HEAD_SIZE),
            ],
            out_specs=whole(GROUPS, SLOT_ROWS, SENT_WIDTH),
            scratch_shapes=[
                pltpu.VMEM((ROWS, OWN_WIDTH), jnp.float32),
                pltpu.VMEM((ROWS, HEAD_SIZE), jnp.float32),
            ],
        ),
        out_shape=jax.ShapeDtypeStruct((GROUPS, SLOT_ROWS, SENT_WIDTH), jnp.bfloat16),
        compiler_params=pltpu.CompilerParams(vmem_limit_bytes=60 * 2**20),
        cost_estimate=pl.CostEstimate(
            flops=20 * ROWS * MODEL_WIDTH * SENT_WIDTH, bytes_accessed=13_000_000, transcendentals=0
        ),
        name="project",
    )(tasks, spots, tokens, query_weight, keyval_weight, low_rank, up_maps, cosine, sine, gain)


def attend_kernel(
    order_ref,
    local_ref,
    reach_ref,
    place_ref,
    own_ref,
    other_ref,
    page_ref,
    suffix_ref,
    cos_ref,
    sin_ref,
    gain_ref,
    out_ref,
):
    half = place_ref[0]
    flip = place_ref[1]
    span = GROUPS * PROMPT_TOKENS // SHARDS
    pages = page_ref[...].reshape(span, 2 * HEAD_SIZE)
    keys = pages[:, :HEAD_SIZE]
    values = jnp.concatenate(
        [jnp.ones((span, HEAD_SIZE), jnp.bfloat16), pages[:, HEAD_SIZE:]], axis=1
    )
    first_sent = jnp.where(half == 0, own_ref[0], other_ref[0])
    second_sent = jnp.where(half == 0, other_ref[0], own_ref[0])
    low_part = first_sent[:, OWN_WIDTH:].astype(jnp.float32)
    high_part = second_sent[:, OWN_WIDTH:].astype(jnp.float32)
    lane = lax.broadcasted_iota(jnp.int32, (SLOT_ROWS, HEAD_SIZE), 1)
    low_lanes = lane < HEAD_SIZE // 2
    new_keys = jnp.where(low_lanes, low_part, pltpu.roll(high_part, HEAD_SIZE // 2, 1))
    new_values = jnp.where(low_lanes, pltpu.roll(low_part, HEAD_SIZE // 2, 1), high_part)
    new_keys = norm_rotate(new_keys, gain_ref[...], cos_ref[0], sin_ref[0])
    suffix_rows = SLOT_SAMPLES * 16
    extra = suffix_rows + 2 * SLOT_ROWS
    suffix = suffix_ref[0, :suffix_rows, :]
    zeros = jnp.zeros((SLOT_ROWS, HEAD_SIZE), jnp.bfloat16)
    extra_keys = jnp.concatenate(
        [suffix[:, :HEAD_SIZE], new_keys.astype(jnp.bfloat16), zeros], axis=0
    )
    extra_values = jnp.concatenate(
        [suffix[:, HEAD_SIZE:], new_values.astype(jnp.bfloat16), zeros], axis=0
    )
    extra_values = jnp.concatenate(
        [jnp.ones((extra, HEAD_SIZE), jnp.bfloat16), extra_values], axis=1
    )
    lengths = suffix_ref[0, suffix_rows:, :].astype(jnp.float32)
    sample_of = lax.broadcasted_iota(jnp.int32, (SLOT_SAMPLES, suffix_rows), 0)
    column_sample = lax.broadcasted_iota(jnp.int32, (SLOT_SAMPLES, suffix_rows), 1) // 16
    column_length = jnp.sum(
        jnp.where(sample_of == column_sample, lengths, 0.0), axis=0, keepdims=True
    )
    row = lax.broadcasted_iota(jnp.int32, (SLOT_ROWS, suffix_rows), 0)
    column = lax.broadcasted_iota(jnp.int32, (SLOT_ROWS, suffix_rows), 1)
    suffix_seen = (row // DECODE_STEPS == column // 16) & (
        (half * 16 + column % 16).astype(jnp.float32) < column_length
    )
    row = lax.broadcasted_iota(jnp.int32, (SLOT_ROWS, 2 * SLOT_ROWS), 0)
    column = lax.broadcasted_iota(jnp.int32, (SLOT_ROWS, 2 * SLOT_ROWS), 1)
    new_seen = (
        (row // DECODE_STEPS == column // DECODE_STEPS)
        & (column % DECODE_STEPS <= row % DECODE_STEPS)
        & (column // HALF_ROWS == half)
    )
    bias = jnp.concatenate(
        [jnp.where(suffix_seen, 0.0, masked_low), jnp.where(new_seen, 0.0, masked_low)], axis=1
    )
    bias = jnp.concatenate([bias] * TILE_HEADS, axis=0)
    logs = jnp.zeros((SLOT_ROWS, HEAD_SIZE), jnp.float32)

    def finish(first, total, peak):
        nonlocal logs
        denominator = total[:, :HEAD_SIZE]
        attended = (total[:, HEAD_SIZE:] / denominator).astype(jnp.bfloat16)
        log_sum = peak + jnp.log2(denominator)
        for index in range(TILE_HEADS):
            head = first + index
            rows = slice(index * SLOT_ROWS, (index + 1) * SLOT_ROWS)
            top = attended[rows][:HALF_ROWS]
            low = attended[rows][HALF_ROWS:]
            lanes = slice(head * HEAD_SIZE, (head + 1) * HEAD_SIZE)
            out_ref[0, 0, :, lanes] = jnp.where(flip == 0, top, low)
            out_ref[0, 1, :, lanes] = jnp.where(flip == 0, low, top)
            logs = jnp.where(lane == head, log_sum[rows], logs)

    def query_of(first):
        query = []
        for head in range(first, first + TILE_HEADS):
            source, start = divmod(head, OWN_HEADS)
            sent = second_sent if source else first_sent
            query.append(sent[:, start * HEAD_SIZE : (start + 1) * HEAD_SIZE])
        return jnp.concatenate(query, axis=0)


    def scores(first):
        query = query_of(first)
        return dot_nt(query, keys), dot_nt(query, extra_keys) + bias

    tiles = list(range(0, HEAD_FAN, TILE_HEADS))
    ready = scores(tiles[0])
    for number, first in enumerate(tiles):
        prefix_score, extra_score = ready
        if number + 1 < len(tiles):
            ready = scores(tiles[number + 1])
        peak = jnp.maximum(
            jnp.max(prefix_score, axis=-1, keepdims=True),
            jnp.max(extra_score, axis=-1, keepdims=True),
        )
        prefix_weight = jnp.exp2(prefix_score - peak).astype(jnp.bfloat16)
        extra_weight = jnp.exp2(extra_score - peak).astype(jnp.bfloat16)
        total = jnp.dot(prefix_weight, values, preferred_element_type=jnp.float32) + jnp.dot(
            extra_weight, extra_values, preferred_element_type=jnp.float32
        )
        finish(first, total, peak)
    high_term = logs.astype(jnp.bfloat16).astype(jnp.float32)
    rest = logs - high_term
    mid_term = rest.astype(jnp.bfloat16).astype(jnp.float32)
    low_term = rest - mid_term
    packed = (
        high_term + pltpu.roll(mid_term, HEAD_FAN, 1) + pltpu.roll(low_term, 2 * HEAD_FAN, 1)
    ).astype(jnp.bfloat16)
    top = packed[:HALF_ROWS]
    low = packed[HALF_ROWS:]
    out_ref[0, 0, :, HEAD_FAN * HEAD_SIZE :] = jnp.where(flip == 0, top, low)
    out_ref[0, 1, :, HEAD_FAN * HEAD_SIZE :] = jnp.where(flip == 0, low, top)


def attend(order, local, reach, place, own, other, pages, suffix, cosine, sine, gain):
    block = PROMPT_TOKENS // SHARDS
    return pl.pallas_call(
        attend_kernel,
        grid_spec=pltpu.PrefetchScalarGridSpec(
            num_scalar_prefetch=4,
            grid=(GROUPS,),
            in_specs=[
                pl.BlockSpec((1, SLOT_ROWS, SENT_WIDTH), lambda i, o, l, r, p: (r[i], 0, 0)),
                pl.BlockSpec((1, SLOT_ROWS, SENT_WIDTH), lambda i, o, l, r, p: (r[i], 0, 0)),
                pl.BlockSpec(
                    (GROUPS, 1, block, 2 * HEAD_SIZE), lambda i, o, l, r, p: (0, l[i], 0, 0)
                ),
                pl.BlockSpec(
                    (1, suffix.shape[1], 2 * HEAD_SIZE), lambda i, o, l, r, p: (r[i], 0, 0)
                ),
                pl.BlockSpec((1, SLOT_ROWS, HEAD_SIZE), lambda i, o, l, r, p: (r[i], 0, 0)),
                pl.BlockSpec((1, SLOT_ROWS, HEAD_SIZE), lambda i, o, l, r, p: (r[i], 0, 0)),
                pl.BlockSpec((1, HEAD_SIZE), lambda i, o, l, r, p: (0, 0)),
            ],
            out_specs=pl.BlockSpec(
                (1, 2, HALF_ROWS, BACK_WIDTH), lambda i, o, l, r, p: (o[i], 0, 0, 0)
            ),
        ),
        out_shape=jax.ShapeDtypeStruct((GROUPS, 2, HALF_ROWS, BACK_WIDTH), jnp.bfloat16),
        compiler_params=pltpu.CompilerParams(vmem_limit_bytes=60 * 2**20),
        cost_estimate=pl.CostEstimate(
            flops=20 * GROUPS * 512 * 2432 * 384,
            bytes_accessed=8_000_000,
            transcendentals=GROUPS * 512 * 2432,
        ),
        name="attend",
    )(order, local, reach, place, own, other, pages, suffix, cosine, sine, gain)


def output_kernel(place_ref, back_ref, own_ref, other_ref, out_ref, mixed):
    half = place_ref[0]
    rows = GROUPS * HALF_ROWS

    @pl.when(pl.program_id(0) == 0)
    def _():
        lane = lax.broadcasted_iota(jnp.int32, (rows, HEAD_SIZE), 1)

        def log_of(source):
            packed = back_ref[:, source, :, HEAD_FAN * HEAD_SIZE :]
            packed = packed.reshape(rows, HEAD_SIZE).astype(jnp.float32)
            return (
                packed
                + pltpu.roll(packed, HEAD_SIZE - HEAD_FAN, 1)
                + pltpu.roll(packed, HEAD_SIZE - 2 * HEAD_FAN, 1)
            )

        first_log = log_of(0)
        second_log = log_of(1)
        peak = jnp.maximum(first_log, second_log)
        first_part = jnp.exp2(first_log - peak)
        second_part = jnp.exp2(second_log - peak)
        both = first_part + second_part
        first_part = first_part / both
        second_part = second_part / both

        def attended(head):
            lanes = slice(head * HEAD_SIZE, (head + 1) * HEAD_SIZE)
            first = back_ref[:, 0, :, lanes].reshape(rows, HEAD_SIZE).astype(jnp.float32)
            second = back_ref[:, 1, :, lanes].reshape(rows, HEAD_SIZE).astype(jnp.float32)
            return (
                first * first_part[:, head : head + 1] + second * second_part[:, head : head + 1]
            ).astype(jnp.bfloat16)

        for head in range(OWN_HEADS):
            low = attended(head)
            high = attended(head + OWN_HEADS)
            lanes = slice(head * HEAD_SIZE, (head + 1) * HEAD_SIZE)
            mixed[0, :, lanes] = jnp.where(half == 0, low, high)
            mixed[1, :, lanes] = jnp.where(half == 0, high, low)

    out_ref[...] = (
        jnp.dot(mixed[0], own_ref[...], preferred_element_type=jnp.float32)
        + jnp.dot(mixed[1], other_ref[...], preferred_element_type=jnp.float32)
    ).astype(jnp.bfloat16)


def output_part(place, back, own_weight, other_weight):
    tile = 2560
    rows = GROUPS * HALF_ROWS
    return pl.pallas_call(
        output_kernel,
        grid_spec=pltpu.PrefetchScalarGridSpec(
            num_scalar_prefetch=1,
            grid=(MODEL_WIDTH // tile,),
            in_specs=[
                pl.BlockSpec((GROUPS, 2, HALF_ROWS, BACK_WIDTH), lambda n, p: (0, 0, 0, 0)),
                pl.BlockSpec((OWN_WIDTH, tile), lambda n, p: (0, n)),
                pl.BlockSpec((OWN_WIDTH, tile), lambda n, p: (0, n)),
            ],
            out_specs=pl.BlockSpec((rows, tile), lambda n, p: (0, n)),
            scratch_shapes=[pltpu.VMEM((2, rows, OWN_WIDTH), jnp.bfloat16)],
        ),
        out_shape=jax.ShapeDtypeStruct((rows, MODEL_WIDTH), jnp.bfloat16),
        compiler_params=pltpu.CompilerParams(vmem_limit_bytes=60 * 2**20),
        cost_estimate=pl.CostEstimate(
            flops=2 * rows * MODEL_WIDTH * 1024, bytes_accessed=14_000_000, transcendentals=0
        ),
        name="output_part",
    )(place, back, own_weight, other_weight)


def along_x(distance):
    return [(shard, shard // 4 * 4 + (shard + distance) % 4) for shard in range(SHARDS)]


def along_y(distance):
    return [(shard, (shard + 4 * distance) % SHARDS) for shard in range(SHARDS)]


def across_groups(bits):
    return [(group, group ^ bits) for group in range(GROUPS)]


def exchange_groups(blocks, group):
    by_core = blocks.reshape((GROUPS // 2, 2) + blocks.shape[1:])
    kept = lax.dynamic_index_in_dim(by_core, group % 2, 1, keepdims=True)
    given = lax.dynamic_index_in_dim(by_core, 1 - group % 2, 1, keepdims=True)
    given = lax.ppermute(given, "grp", across_groups(1))
    both = jnp.concatenate([kept, given], axis=1)
    arrived = []
    for k in range(GROUPS // 2):
        block = lax.dynamic_index_in_dim(both, (group // 2) ^ k, 0, keepdims=False)
        arrived.append(lax.ppermute(block, "grp", across_groups(2 * k)) if k else block)
    return jnp.concatenate(arrived, axis=0)


def swap(block, axes, groups=None):
    return lax.all_to_all(
        block, axes, split_axis=0, concat_axis=0, tiled=True, axis_index_groups=groups
    )


def shards(
    tokens,
    prompt_cache,
    generated_cache,
    suffix_lengths,
    fanout,
    prompt_adapter,
    query_weight,
    key_value_weight,
    output_weight,
    adapter_down_maps,
    adapter_up_maps,
    query_norm_gain,
    key_norm_gain,
):
    group = lax.axis_index("grp")
    shard = lax.axis_index("ad")
    head = shard // 2
    half = shard % 2
    local_table = slot_prompts(fanout, GROUPS, OWNED)

    part_rows = lax.all_gather(tokens, "ad", axis=0, tiled=True)

    slot_suffix = generated_cache.reshape(GROUPS, SLOT_SAMPLES * 16, 2 * HEAD_SIZE)
    slot_lengths = suffix_lengths.reshape(GROUPS, SLOT_SAMPLES, 1).astype(jnp.bfloat16)
    slot_suffix = jnp.concatenate(
        [slot_suffix, jnp.broadcast_to(slot_lengths, (GROUPS, SLOT_SAMPLES, 2 * HEAD_SIZE))], axis=1
    )
    suffix = exchange_groups(slot_suffix, group)

    owners = jnp.arange(GROUPS, dtype=jnp.int32)
    local_of_slot = lax.dynamic_index_in_dim(local_table, group, 1, keepdims=False)
    prompts = owners * OWNED + local_of_slot
    hit = prompts[:, None] == jnp.arange(prompt_adapter.shape[0], dtype=jnp.int32)[None, :]
    tasks = jnp.sum(hit.astype(jnp.int32) * prompt_adapter[None, :], axis=1)
    own_rows = tokens.shape[0]
    columns = swap(jnp.swapaxes(tokens.reshape(own_rows, SHARDS, -1), 0, 1), "ad")
    rank_all = jnp.dot(
        columns.reshape(ROWS, -1),
        adapter_down_maps.reshape(-1, ADAPTER_COUNT * ADAPTER_RANK),
        preferred_element_type=jnp.float32,
    ).reshape(GROUPS, SLOT_ROWS, ADAPTER_COUNT, ADAPTER_RANK)
    chosen = (tasks[:, None] == jnp.arange(ADAPTER_COUNT, dtype=jnp.int32)[None, :]).astype(
        jnp.float32
    )
    rank_part = jnp.sum(rank_all * chosen[:, None, :, None], axis=2)
    rank_rows = jnp.sum(swap(rank_part.reshape(SHARDS, own_rows, ADAPTER_RANK), "ad"), axis=0)
    rank_rows = rank_rows.astype(jnp.bfloat16)

    ring = [rank_rows] + [lax.ppermute(rank_rows, "ad", along_x(k)) for k in (1, 2, 3)]
    ring = jnp.stack(ring)

    low_rank = jnp.stack([ring] + [lax.ppermute(ring, "ad", along_y(k)) for k in (1, 2, 3)])
    every = jnp.arange(SHARDS, dtype=jnp.int32)
    spots = ((shard // 4 - every // 4) % 4) * 4 + (shard % 4 - every % 4) % 4

    slice_rows = OWN_WIDTH // GROUPS
    weight_slice = lax.dynamic_slice_in_dim(output_weight, group * slice_rows, slice_rows, 0)
    low_rank, head_pages, weight_slice = lax.optimization_barrier(
        (low_rank, jnp.swapaxes(prompt_cache, 0, 1), weight_slice)
    )
    arrived = swap(head_pages, "ad", ROLE_GROUPS)
    weight_slice = lax.ppermute(weight_slice, "ad", PARTNERS)
    part_rows, weight_slice = lax.optimization_barrier((part_rows, weight_slice))
    other_weight = lax.all_gather(weight_slice, "grp", axis=0, tiled=True)

    steps = jnp.arange(DECODE_STEPS, dtype=jnp.int32)
    position = (PROMPT_TOKENS + suffix_lengths[:, None] + steps[None, :]).astype(jnp.float32)
    cosine, sine = angle_tables(position.reshape(ROWS))
    sent = project(
        tasks,
        spots,
        part_rows,
        query_weight,
        key_value_weight.transpose(1, 2, 0).reshape(HEAD_SIZE, MODEL_WIDTH),
        low_rank.reshape(SHARDS, own_rows, ADAPTER_RANK),
        adapter_up_maps,
        cosine,
        sine,
        query_norm_gain.reshape(1, HEAD_SIZE) * exponent_scale,
    )
    own_sent = exchange_groups(sent, group)
    other_sent = lax.ppermute(own_sent, "ad", PARTNERS)

    local = lax.dynamic_index_in_dim(local_table, group, 0, keepdims=False)
    rank_key = local * GROUPS + owners
    spot = jnp.sum((rank_key[None, :] < rank_key[:, None]).astype(jnp.int32), axis=1)
    placed = (spot[None, :] == owners[:, None]).astype(jnp.int32)
    order = jnp.sum(placed * owners[None, :], axis=1)
    local_sorted = jnp.sum(placed * local[None, :], axis=1)
    flip = (head + group) % 2
    place = jnp.stack([half, flip]).astype(jnp.int32)
    far_lengths = suffix[:, SLOT_SAMPLES * 16 :, 0].astype(jnp.float32)
    far_position = PROMPT_TOKENS + far_lengths[:, :, None] + steps.astype(jnp.float32)
    far_cosine, far_sine = angle_tables(far_position.reshape(GROUPS, SLOT_ROWS))
    partial = attend(
        order,
        local_sorted,
        order ^ group,
        place,
        own_sent,
        other_sent,
        arrived,
        suffix,
        far_cosine,
        far_sine,
        key_norm_gain.reshape(1, HEAD_SIZE),
    )
    back = swap(
        partial.reshape(2 * GROUPS, HALF_ROWS, BACK_WIDTH), ("grp", "ad"), HEAD_GROUPS
    ).reshape(GROUPS, 2, HALF_ROWS, BACK_WIDTH)
    product = output_part(place, back, output_weight, other_weight)
    blocks = swap(product.reshape(GROUPS, HALF_ROWS, MODEL_WIDTH), "ad", ROLE_GROUPS)
    return jnp.sum(blocks.astype(jnp.float32), axis=0).astype(jnp.bfloat16)


def solution(mesh):
    return jax.shard_map(
        shards,
        mesh=mesh,
        in_specs=(
            P(("grp", "ad"), None),
            P("grp", None, "ad", None),
            P("grp", "ad", None),
            P("grp"),
            P(),
            P(),
            P(None, "ad"),
            P(None, None, "ad"),
            P("ad", None),
            P("ad", None, None),
            P(None, None, "ad"),
            P(),
            P(),
        ),
        out_specs=P(("grp", "ad"), None),
        check_vma=False,
    )
```

```python
import functools

import jax
import jax.numpy as jnp
from jax import lax
from jax.experimental import pallas as pl
from jax.experimental.pallas import tpu as pltpu
from jax.sharding import PartitionSpec as P

MODEL_WIDTH = 5120
KEY_VALUE_HEADS = 8
HEAD_SIZE = 128
ADAPTER_RANK = 128
FAN = 2
DECODE_STEPS = 4
ADAPTER_COUNT = 4
PROMPT_TOKENS = 4096
GROUPS = 8
SHARDS = 16
OWNED = 4
SLOT_SAMPLES = 16
SLOT_ROWS = SLOT_SAMPLES * DECODE_STEPS
HALF_ROWS = SLOT_ROWS // 2
ROWS = GROUPS * SLOT_ROWS
OWN_HEADS = 4
OWN_WIDTH = OWN_HEADS * HEAD_SIZE
HEAD_FAN = 2 * OWN_HEADS
SENT_WIDTH = OWN_WIDTH + HEAD_SIZE
TILE_HEADS = 4
BACK_WIDTH = HEAD_FAN * HEAD_SIZE + HEAD_SIZE

theta_base = 1000000.0
norm_eps = 1e-06
masked_low = -1e30
exponent_scale = HEAD_SIZE**-0.5 * 1.4426950408889634

ROLE_GROUPS = [[0, 3, 4, 7, 8, 11, 12, 15], [1, 2, 5, 6, 9, 10, 13, 14]]
HEAD_GROUPS = [
    [group * SHARDS + 2 * head + half for group in range(GROUPS) for half in range(2)]
    for head in range(KEY_VALUE_HEADS)
]
PARTNERS = [(shard, shard ^ 1) for shard in range(SHARDS)]


def slot_prompts(fanout, groups, owned_count):
    listed = jnp.any(
        fanout[:, :, None] == jnp.arange(groups, dtype=jnp.int32)[None, None, :], axis=1
    )
    listed = listed.astype(jnp.int32).reshape(groups, owned_count, groups)
    return jnp.sum(listed * jnp.arange(owned_count, dtype=jnp.int32)[None, :, None], axis=1)


def angle_tables(position):
    half_len = HEAD_SIZE // 2
    inverse = theta_base ** (-2.0 * jnp.arange(half_len, dtype=jnp.float32) / HEAD_SIZE)
    angles = position[..., None] * inverse
    cosine = jnp.cos(angles)
    sine = jnp.sin(angles)
    return (
        jnp.concatenate([cosine, cosine], axis=-1),
        jnp.concatenate([-sine, sine], axis=-1),
    )


def norm_rotate(vector, gain, cosine, sine):
    mean_sq = jnp.mean(vector * vector, axis=-1, keepdims=True)
    scaled = vector * lax.rsqrt(mean_sq + norm_eps) * gain
    return scaled * cosine + pltpu.roll(scaled, HEAD_SIZE // 2, 1) * sine


def dot_nt(left, right):
    return lax.dot_general(
        left, right, (((1,), (1,)), ((), ())), preferred_element_type=jnp.float32
    )


def project_kernel(
    task_ref,
    spot_ref,
    tokens_ref,
    query_ref,
    keyval_ref,
    rank_ref,
    up_ref,
    cos_ref,
    sin_ref,
    gain_ref,
    out_ref,
    query_sum,
    keyval_sum,
):
    step = pl.program_id(0)

    @pl.when(step == 0)
    def _():
        query_sum[...] = jnp.zeros_like(query_sum)
        keyval_sum[...] = jnp.zeros_like(keyval_sum)

    part = tokens_ref[...]
    query_sum[...] += jnp.dot(part, query_ref[...], preferred_element_type=jnp.float32)
    keyval_sum[...] += dot_nt(part, keyval_ref[...])

    @pl.when(step == pl.num_programs(0) - 1)
    def _():
        for slot in range(GROUPS):
            rows = slice(slot * SLOT_ROWS, (slot + 1) * SLOT_ROWS)
            low_rank = jnp.concatenate(
                [rank_ref[spot_ref[2 * slot]], rank_ref[spot_ref[2 * slot + 1]]], axis=0
            )
            query = query_sum[rows, :] + jnp.dot(
                low_rank, up_ref[task_ref[slot]], preferred_element_type=jnp.float32
            )
            for head in range(OWN_HEADS):
                lanes = slice(head * HEAD_SIZE, (head + 1) * HEAD_SIZE)
                turned = norm_rotate(
                    query[:, lanes], gain_ref[...], cos_ref[rows, :], sin_ref[rows, :]
                ).astype(jnp.bfloat16)
                out_ref[slot, :, lanes] = turned
            out_ref[slot, :, OWN_WIDTH:] = keyval_sum[rows, :].astype(jnp.bfloat16)


def project(tasks, spots, tokens, query_weight, keyval_weight, low_rank, up_maps, cosine, sine, gain):
    tile = 2560
    whole = lambda *shape: pl.BlockSpec(shape, lambda k, t, s: (0,) * len(shape))
    return pl.pallas_call(
        project_kernel,
        grid_spec=pltpu.PrefetchScalarGridSpec(
            num_scalar_prefetch=2,
            grid=(MODEL_WIDTH // tile,),
            in_specs=[
                pl.BlockSpec((ROWS, tile), lambda k, t, s: (0, k)),
                pl.BlockSpec((tile, OWN_WIDTH), lambda k, t, s: (k, 0)),
                pl.BlockSpec((HEAD_SIZE, tile), lambda k, t, s: (0, k)),
                whole(SHARDS, HALF_ROWS, ADAPTER_RANK),
                whole(ADAPTER_COUNT, ADAPTER_RANK, OWN_WIDTH),
                whole(ROWS, HEAD_SIZE),
                whole(ROWS, HEAD_SIZE),
                whole(1, HEAD_SIZE),
            ],
            out_specs=whole(GROUPS, SLOT_ROWS, SENT_WIDTH),
            scratch_shapes=[
                pltpu.VMEM((ROWS, OWN_WIDTH), jnp.float32),
                pltpu.VMEM((ROWS, HEAD_SIZE), jnp.float32),
            ],
        ),
        out_shape=jax.ShapeDtypeStruct((GROUPS, SLOT_ROWS, SENT_WIDTH), jnp.bfloat16),
        compiler_params=pltpu.CompilerParams(vmem_limit_bytes=60 * 2**20),
        cost_estimate=pl.CostEstimate(
            flops=20 * ROWS * MODEL_WIDTH * SENT_WIDTH, bytes_accessed=13_000_000, transcendentals=0
        ),
        name="project",
    )(tasks, spots, tokens, query_weight, keyval_weight, low_rank, up_maps, cosine, sine, gain)


def attend_kernel(
    order_ref,
    local_ref,
    reach_ref,
    place_ref,
    own_ref,
    other_ref,
    page_ref,
    suffix_ref,
    cos_ref,
    sin_ref,
    gain_ref,
    out_ref,
):
    half = place_ref[0]
    flip = place_ref[1]
    span = GROUPS * PROMPT_TOKENS // SHARDS
    pages = page_ref[...].reshape(span, 2 * HEAD_SIZE)
    keys = pages[:, :HEAD_SIZE]
    values = jnp.concatenate(
        [jnp.ones((span, HEAD_SIZE), jnp.bfloat16), pages[:, HEAD_SIZE:]], axis=1
    )
    first_sent = jnp.where(half == 0, own_ref[0], other_ref[0])
    second_sent = jnp.where(half == 0, other_ref[0], own_ref[0])
    low_part = first_sent[:, OWN_WIDTH:].astype(jnp.float32)
    high_part = second_sent[:, OWN_WIDTH:].astype(jnp.float32)
    lane = lax.broadcasted_iota(jnp.int32, (SLOT_ROWS, HEAD_SIZE), 1)
    low_lanes = lane < HEAD_SIZE // 2
    new_keys = jnp.where(low_lanes, low_part, pltpu.roll(high_part, HEAD_SIZE // 2, 1))
    new_values = jnp.where(low_lanes, pltpu.roll(low_part, HEAD_SIZE // 2, 1), high_part)
    new_keys = norm_rotate(new_keys, gain_ref[...], cos_ref[0], sin_ref[0])
    suffix_rows = SLOT_SAMPLES * 16
    extra = suffix_rows + 2 * SLOT_ROWS
    suffix = suffix_ref[0, :suffix_rows, :]
    zeros = jnp.zeros((SLOT_ROWS, HEAD_SIZE), jnp.bfloat16)
    extra_keys = jnp.concatenate(
        [suffix[:, :HEAD_SIZE], new_keys.astype(jnp.bfloat16), zeros], axis=0
    )
    extra_values = jnp.concatenate(
        [suffix[:, HEAD_SIZE:], new_values.astype(jnp.bfloat16), zeros], axis=0
    )
    extra_values = jnp.concatenate(
        [jnp.ones((extra, HEAD_SIZE), jnp.bfloat16), extra_values], axis=1
    )
    lengths = suffix_ref[0, suffix_rows:, :].astype(jnp.float32)
    sample_of = lax.broadcasted_iota(jnp.int32, (SLOT_SAMPLES, suffix_rows), 0)
    column_sample = lax.broadcasted_iota(jnp.int32, (SLOT_SAMPLES, suffix_rows), 1) // 16
    column_length = jnp.sum(
        jnp.where(sample_of == column_sample, lengths, 0.0), axis=0, keepdims=True
    )
    row = lax.broadcasted_iota(jnp.int32, (SLOT_ROWS, suffix_rows), 0)
    column = lax.broadcasted_iota(jnp.int32, (SLOT_ROWS, suffix_rows), 1)
    suffix_seen = (row // DECODE_STEPS == column // 16) & (
        (half * 16 + column % 16).astype(jnp.float32) < column_length
    )
    row = lax.broadcasted_iota(jnp.int32, (SLOT_ROWS, 2 * SLOT_ROWS), 0)
    column = lax.broadcasted_iota(jnp.int32, (SLOT_ROWS, 2 * SLOT_ROWS), 1)
    new_seen = (
        (row // DECODE_STEPS == column // DECODE_STEPS)
        & (column % DECODE_STEPS <= row % DECODE_STEPS)
        & (column // HALF_ROWS == half)
    )
    bias = jnp.concatenate(
        [jnp.where(suffix_seen, 0.0, masked_low), jnp.where(new_seen, 0.0, masked_low)], axis=1
    )
    bias = jnp.concatenate([bias] * TILE_HEADS, axis=0)
    logs = jnp.zeros((SLOT_ROWS, HEAD_SIZE), jnp.float32)

    def finish(first, total, peak):
        nonlocal logs
        denominator = total[:, :HEAD_SIZE]
        attended = (total[:, HEAD_SIZE:] / denominator).astype(jnp.bfloat16)
        log_sum = peak + jnp.log2(denominator)
        for index in range(TILE_HEADS):
            head = first + index
            rows = slice(index * SLOT_ROWS, (index + 1) * SLOT_ROWS)
            top = attended[rows][:HALF_ROWS]
            low = attended[rows][HALF_ROWS:]
            lanes = slice(head * HEAD_SIZE, (head + 1) * HEAD_SIZE)
            out_ref[0, 0, :, lanes] = jnp.where(flip == 0, top, low)
            out_ref[0, 1, :, lanes] = jnp.where(flip == 0, low, top)
            logs = jnp.where(lane == head, log_sum[rows], logs)

    def query_of(first):
        query = []
        for head in range(first, first + TILE_HEADS):
            source, start = divmod(head, OWN_HEADS)
            sent = second_sent if source else first_sent
            query.append(sent[:, start * HEAD_SIZE : (start + 1) * HEAD_SIZE])
        return jnp.concatenate(query, axis=0)


    def scores(first):
        query = query_of(first)
        return dot_nt(query, keys), dot_nt(query, extra_keys) + bias

    tiles = list(range(0, HEAD_FAN, TILE_HEADS))
    ready = scores(tiles[0])
    for number, first in enumerate(tiles):
        prefix_score, extra_score = ready
        if number + 1 < len(tiles):
            ready = scores(tiles[number + 1])
        peak = jnp.maximum(
            jnp.max(prefix_score, axis=-1, keepdims=True),
            jnp.max(extra_score, axis=-1, keepdims=True),
        )
        prefix_weight = jnp.exp2(prefix_score - peak).astype(jnp.bfloat16)
        extra_weight = jnp.exp2(extra_score - peak).astype(jnp.bfloat16)
        total = jnp.dot(prefix_weight, values, preferred_element_type=jnp.float32) + jnp.dot(
            extra_weight, extra_values, preferred_element_type=jnp.float32
        )
        finish(first, total, peak)
    high_term = logs.astype(jnp.bfloat16).astype(jnp.float32)
    rest = logs - high_term
    mid_term = rest.astype(jnp.bfloat16).astype(jnp.float32)
    low_term = rest - mid_term
    packed = (
        high_term + pltpu.roll(mid_term, HEAD_FAN, 1) + pltpu.roll(low_term, 2 * HEAD_FAN, 1)
    ).astype(jnp.bfloat16)
    top = packed[:HALF_ROWS]
    low = packed[HALF_ROWS:]
    out_ref[0, 0, :, HEAD_FAN * HEAD_SIZE :] = jnp.where(flip == 0, top, low)
    out_ref[0, 1, :, HEAD_FAN * HEAD_SIZE :] = jnp.where(flip == 0, low, top)


def attend(order, local, reach, place, own, other, pages, suffix, cosine, sine, gain):
    block = PROMPT_TOKENS // SHARDS
    return pl.pallas_call(
        attend_kernel,
        grid_spec=pltpu.PrefetchScalarGridSpec(
            num_scalar_prefetch=4,
            grid=(GROUPS,),
            in_specs=[
                pl.BlockSpec((1, SLOT_ROWS, SENT_WIDTH), lambda i, o, l, r, p: (r[i], 0, 0)),
                pl.BlockSpec((1, SLOT_ROWS, SENT_WIDTH), lambda i, o, l, r, p: (r[i], 0, 0)),
                pl.BlockSpec(
                    (GROUPS, 1, block, 2 * HEAD_SIZE), lambda i, o, l, r, p: (0, l[i], 0, 0)
                ),
                pl.BlockSpec(
                    (1, suffix.shape[1], 2 * HEAD_SIZE), lambda i, o, l, r, p: (r[i], 0, 0)
                ),
                pl.BlockSpec((1, SLOT_ROWS, HEAD_SIZE), lambda i, o, l, r, p: (r[i], 0, 0)),
                pl.BlockSpec((1, SLOT_ROWS, HEAD_SIZE), lambda i, o, l, r, p: (r[i], 0, 0)),
                pl.BlockSpec((1, HEAD_SIZE), lambda i, o, l, r, p: (0, 0)),
            ],
            out_specs=pl.BlockSpec(
                (1, 2, HALF_ROWS, BACK_WIDTH), lambda i, o, l, r, p: (o[i], 0, 0, 0)
            ),
        ),
        out_shape=jax.ShapeDtypeStruct((GROUPS, 2, HALF_ROWS, BACK_WIDTH), jnp.bfloat16),
        compiler_params=pltpu.CompilerParams(vmem_limit_bytes=60 * 2**20),
        cost_estimate=pl.CostEstimate(
            flops=20 * GROUPS * 512 * 2432 * 384,
            bytes_accessed=8_000_000,
            transcendentals=GROUPS * 512 * 2432,
        ),
        name="attend",
    )(order, local, reach, place, own, other, pages, suffix, cosine, sine, gain)


def output_kernel(place_ref, back_ref, own_ref, other_ref, out_ref, mixed):
    half = place_ref[0]
    rows = GROUPS * HALF_ROWS

    @pl.when(pl.program_id(0) == 0)
    def _():
        lane = lax.broadcasted_iota(jnp.int32, (rows, HEAD_SIZE), 1)

        def log_of(source):
            packed = back_ref[:, source, :, HEAD_FAN * HEAD_SIZE :]
            packed = packed.reshape(rows, HEAD_SIZE).astype(jnp.float32)
            return (
                packed
                + pltpu.roll(packed, HEAD_SIZE - HEAD_FAN, 1)
                + pltpu.roll(packed, HEAD_SIZE - 2 * HEAD_FAN, 1)
            )

        first_log = log_of(0)
        second_log = log_of(1)
        peak = jnp.maximum(first_log, second_log)
        first_part = jnp.exp2(first_log - peak)
        second_part = jnp.exp2(second_log - peak)
        both = first_part + second_part
        first_part = first_part / both
        second_part = second_part / both

        def attended(head):
            lanes = slice(head * HEAD_SIZE, (head + 1) * HEAD_SIZE)
            first = back_ref[:, 0, :, lanes].reshape(rows, HEAD_SIZE).astype(jnp.float32)
            second = back_ref[:, 1, :, lanes].reshape(rows, HEAD_SIZE).astype(jnp.float32)
            return (
                first * first_part[:, head : head + 1] + second * second_part[:, head : head + 1]
            ).astype(jnp.bfloat16)

        for head in range(OWN_HEADS):
            low = attended(head)
            high = attended(head + OWN_HEADS)
            lanes = slice(head * HEAD_SIZE, (head + 1) * HEAD_SIZE)
            mixed[0, :, lanes] = jnp.where(half == 0, low, high)
            mixed[1, :, lanes] = jnp.where(half == 0, high, low)

    out_ref[...] = (
        jnp.dot(mixed[0], own_ref[...], preferred_element_type=jnp.float32)
        + jnp.dot(mixed[1], other_ref[...], preferred_element_type=jnp.float32)
    ).astype(jnp.bfloat16)


def output_part(place, back, own_weight, other_weight):
    tile = 2560
    rows = GROUPS * HALF_ROWS
    return pl.pallas_call(
        output_kernel,
        grid_spec=pltpu.PrefetchScalarGridSpec(
            num_scalar_prefetch=1,
            grid=(MODEL_WIDTH // tile,),
            in_specs=[
                pl.BlockSpec((GROUPS, 2, HALF_ROWS, BACK_WIDTH), lambda n, p: (0, 0, 0, 0)),
                pl.BlockSpec((OWN_WIDTH, tile), lambda n, p: (0, n)),
                pl.BlockSpec((OWN_WIDTH, tile), lambda n, p: (0, n)),
            ],
            out_specs=pl.BlockSpec((rows, tile), lambda n, p: (0, n)),
            scratch_shapes=[pltpu.VMEM((2, rows, OWN_WIDTH), jnp.bfloat16)],
        ),
        out_shape=jax.ShapeDtypeStruct((rows, MODEL_WIDTH), jnp.bfloat16),
        compiler_params=pltpu.CompilerParams(vmem_limit_bytes=60 * 2**20),
        cost_estimate=pl.CostEstimate(
            flops=2 * rows * MODEL_WIDTH * 1024, bytes_accessed=14_000_000, transcendentals=0
        ),
        name="output_part",
    )(place, back, own_weight, other_weight)


def along_x(distance):
    return [(shard, shard // 4 * 4 + (shard + distance) % 4) for shard in range(SHARDS)]


def along_y(distance):
    return [(shard, (shard + 4 * distance) % SHARDS) for shard in range(SHARDS)]


def across_groups(bits):
    return [(group, group ^ bits) for group in range(GROUPS)]


def exchange_groups(blocks, group):
    by_core = blocks.reshape((GROUPS // 2, 2) + blocks.shape[1:])
    kept = lax.dynamic_index_in_dim(by_core, group % 2, 1, keepdims=True)
    given = lax.dynamic_index_in_dim(by_core, 1 - group % 2, 1, keepdims=True)
    given = lax.ppermute(given, "grp", across_groups(1))
    both = jnp.concatenate([kept, given], axis=1)
    arrived = []
    for k in range(GROUPS // 2):
        block = lax.dynamic_index_in_dim(both, (group // 2) ^ k, 0, keepdims=False)
        arrived.append(lax.ppermute(block, "grp", across_groups(2 * k)) if k else block)
    return arrived


def swap(block, axes, groups=None):
    return lax.all_to_all(
        block, axes, split_axis=0, concat_axis=0, tiled=True, axis_index_groups=groups
    )


def shards(
    tokens,
    prompt_cache,
    generated_cache,
    suffix_lengths,
    fanout,
    prompt_adapter,
    query_weight,
    key_value_weight,
    output_weight,
    adapter_down_maps,
    adapter_up_maps,
    query_norm_gain,
    key_norm_gain,
):
    group = lax.axis_index("grp")
    shard = lax.axis_index("ad")
    head = shard // 2
    half = shard % 2
    local_table = slot_prompts(fanout, GROUPS, OWNED)

    part_rows = lax.all_gather(tokens, "ad", axis=0, tiled=True)

    slot_suffix = generated_cache.reshape(GROUPS, SLOT_SAMPLES * 16, 2 * HEAD_SIZE)
    slot_lengths = suffix_lengths.reshape(GROUPS, SLOT_SAMPLES, 1).astype(jnp.bfloat16)
    slot_suffix = jnp.concatenate(
        [slot_suffix, jnp.broadcast_to(slot_lengths, (GROUPS, SLOT_SAMPLES, 2 * HEAD_SIZE))], axis=1
    )
    suffix = jnp.concatenate(exchange_groups(slot_suffix, group), axis=0)

    owners = jnp.arange(GROUPS, dtype=jnp.int32)
    local_of_slot = lax.dynamic_index_in_dim(local_table, group, 1, keepdims=False)
    prompts = owners * OWNED + local_of_slot
    hit = prompts[:, None] == jnp.arange(prompt_adapter.shape[0], dtype=jnp.int32)[None, :]
    tasks = jnp.sum(hit.astype(jnp.int32) * prompt_adapter[None, :], axis=1)
    own_rows = tokens.shape[0]
    columns = swap(jnp.swapaxes(tokens.reshape(own_rows, SHARDS, -1), 0, 1), "ad")
    rank_all = jnp.dot(
        columns.reshape(ROWS, -1),
        adapter_down_maps.reshape(-1, ADAPTER_COUNT * ADAPTER_RANK),
        preferred_element_type=jnp.float32,
    ).reshape(GROUPS, SLOT_ROWS, ADAPTER_COUNT, ADAPTER_RANK)
    chosen = (tasks[:, None] == jnp.arange(ADAPTER_COUNT, dtype=jnp.int32)[None, :]).astype(
        jnp.float32
    )
    rank_part = jnp.sum(rank_all * chosen[:, None, :, None], axis=2)
    rank_rows = jnp.sum(swap(rank_part.reshape(SHARDS, own_rows, ADAPTER_RANK), "ad"), axis=0)
    rank_rows = rank_rows.astype(jnp.bfloat16)

    ring = [rank_rows] + [lax.ppermute(rank_rows, "ad", along_x(k)) for k in (1, 2, 3)]
    ring = jnp.stack(ring)

    low_rank = jnp.stack([ring] + [lax.ppermute(ring, "ad", along_y(k)) for k in (1, 2, 3)])
    every = jnp.arange(SHARDS, dtype=jnp.int32)
    spots = ((shard // 4 - every // 4) % 4) * 4 + (shard % 4 - every % 4) % 4

    slice_rows = OWN_WIDTH // GROUPS
    weight_slice = lax.dynamic_slice_in_dim(output_weight, group * slice_rows, slice_rows, 0)
    low_rank, head_pages, weight_slice = lax.optimization_barrier(
        (low_rank, jnp.swapaxes(prompt_cache, 0, 1), weight_slice)
    )
    arrived = swap(head_pages, "ad", ROLE_GROUPS)
    weight_slice = lax.ppermute(weight_slice, "ad", PARTNERS)
    part_rows, weight_slice = lax.optimization_barrier((part_rows, weight_slice))
    other_weight = lax.all_gather(weight_slice, "grp", axis=0, tiled=True)

    steps = jnp.arange(DECODE_STEPS, dtype=jnp.int32)
    position = (PROMPT_TOKENS + suffix_lengths[:, None] + steps[None, :]).astype(jnp.float32)
    cosine, sine = angle_tables(position.reshape(ROWS))
    sent = project(
        tasks,
        spots,
        part_rows,
        query_weight,
        key_value_weight.transpose(1, 2, 0).reshape(HEAD_SIZE, MODEL_WIDTH),
        low_rank.reshape(SHARDS, own_rows, ADAPTER_RANK),
        adapter_up_maps,
        cosine,
        sine,
        query_norm_gain.reshape(1, HEAD_SIZE) * exponent_scale,
    )
    own_sent = exchange_groups(sent, group)
    other_sent = jnp.concatenate([lax.ppermute(part, "ad", PARTNERS) for part in own_sent], axis=0)
    own_sent = jnp.concatenate(own_sent, axis=0)

    local = lax.dynamic_index_in_dim(local_table, group, 0, keepdims=False)
    rank_key = local * GROUPS + owners
    spot = jnp.sum((rank_key[None, :] < rank_key[:, None]).astype(jnp.int32), axis=1)
    placed = (spot[None, :] == owners[:, None]).astype(jnp.int32)
    order = jnp.sum(placed * owners[None, :], axis=1)
    local_sorted = jnp.sum(placed * local[None, :], axis=1)
    flip = (head + group) % 2
    place = jnp.stack([half, flip]).astype(jnp.int32)
    far_lengths = suffix[:, SLOT_SAMPLES * 16 :, 0].astype(jnp.float32)
    far_position = PROMPT_TOKENS + far_lengths[:, :, None] + steps.astype(jnp.float32)
    far_cosine, far_sine = angle_tables(far_position.reshape(GROUPS, SLOT_ROWS))
    partial = attend(
        order,
        local_sorted,
        order ^ group,
        place,
        own_sent,
        other_sent,
        arrived,
        suffix,
        far_cosine,
        far_sine,
        key_norm_gain.reshape(1, HEAD_SIZE),
    )
    back = swap(
        partial.reshape(2 * GROUPS, HALF_ROWS, BACK_WIDTH), ("grp", "ad"), HEAD_GROUPS
    ).reshape(GROUPS, 2, HALF_ROWS, BACK_WIDTH)
    product = output_part(place, back, output_weight, other_weight)
    blocks = swap(product.reshape(GROUPS, HALF_ROWS, MODEL_WIDTH), "ad", ROLE_GROUPS)
    return jnp.sum(blocks.astype(jnp.float32), axis=0).astype(jnp.bfloat16)


def solution(mesh):
    return jax.shard_map(
        shards,
        mesh=mesh,
        in_specs=(
            P(("grp", "ad"), None),
            P("grp", None, "ad", None),
            P("grp", "ad", None),
            P("grp"),
            P(),
            P(),
            P(None, "ad"),
            P(None, None, "ad"),
            P("ad", None),
            P("ad", None, None),
            P(None, None, "ad"),
            P(),
            P(),
        ),
        out_specs=P(("grp", "ad"), None),
        check_vma=False,
    )
```

```python
import functools

import jax
import jax.numpy as jnp
from jax import lax
from jax.experimental import pallas as pl
from jax.experimental.pallas import tpu as pltpu
from jax.sharding import PartitionSpec as P

MODEL_WIDTH = 5120
KEY_VALUE_HEADS = 8
HEAD_SIZE = 128
ADAPTER_RANK = 128
FAN = 2
DECODE_STEPS = 4
ADAPTER_COUNT = 4
PROMPT_TOKENS = 4096
GROUPS = 8
SHARDS = 16
OWNED = 4
SLOT_SAMPLES = 16
SLOT_ROWS = SLOT_SAMPLES * DECODE_STEPS
HALF_ROWS = SLOT_ROWS // 2
ROWS = GROUPS * SLOT_ROWS
OWN_HEADS = 4
OWN_WIDTH = OWN_HEADS * HEAD_SIZE
HEAD_FAN = 2 * OWN_HEADS
SENT_WIDTH = OWN_WIDTH + HEAD_SIZE
TILE_HEADS = 4
BACK_WIDTH = HEAD_FAN * HEAD_SIZE + HEAD_SIZE

theta_base = 1000000.0
norm_eps = 1e-06
masked_low = -1e30
exponent_scale = HEAD_SIZE**-0.5 * 1.4426950408889634

ROLE_GROUPS = [[0, 3, 4, 7, 8, 11, 12, 15], [1, 2, 5, 6, 9, 10, 13, 14]]
HEAD_GROUPS = [
    [group * SHARDS + 2 * head + half for group in range(GROUPS) for half in range(2)]
    for head in range(KEY_VALUE_HEADS)
]
ACROSS = [(shard, shard // 4 * 4 + 3 - shard % 4) for shard in range(SHARDS)]
PARTNERS = [(shard, shard ^ 1) for shard in range(SHARDS)]


def slot_prompts(fanout, groups, owned_count):
    listed = jnp.any(
        fanout[:, :, None] == jnp.arange(groups, dtype=jnp.int32)[None, None, :], axis=1
    )
    listed = listed.astype(jnp.int32).reshape(groups, owned_count, groups)
    return jnp.sum(listed * jnp.arange(owned_count, dtype=jnp.int32)[None, :, None], axis=1)


def angle_tables(position):
    half_len = HEAD_SIZE // 2
    inverse = theta_base ** (-2.0 * jnp.arange(half_len, dtype=jnp.float32) / HEAD_SIZE)
    angles = position[..., None] * inverse
    cosine = jnp.cos(angles)
    sine = jnp.sin(angles)
    return (
        jnp.concatenate([cosine, cosine], axis=-1),
        jnp.concatenate([-sine, sine], axis=-1),
    )


def norm_rotate(vector, gain, cosine, sine):
    mean_sq = jnp.mean(vector * vector, axis=-1, keepdims=True)
    scaled = vector * lax.rsqrt(mean_sq + norm_eps) * gain
    return scaled * cosine + pltpu.roll(scaled, HEAD_SIZE // 2, 1) * sine


def dot_nt(left, right):
    return lax.dot_general(
        left, right, (((1,), (1,)), ((), ())), preferred_element_type=jnp.float32
    )


def project_kernel(
    task_ref,
    spot_ref,
    tokens_ref,
    query_ref,
    keyval_ref,
    rank_ref,
    up_ref,
    cos_ref,
    sin_ref,
    gain_ref,
    out_ref,
    query_sum,
    keyval_sum,
):
    step = pl.program_id(0)

    @pl.when(step == 0)
    def _():
        query_sum[...] = jnp.zeros_like(query_sum)
        keyval_sum[...] = jnp.zeros_like(keyval_sum)

    part = tokens_ref[...]
    query_sum[...] += jnp.dot(part, query_ref[...], preferred_element_type=jnp.float32)
    keyval_sum[...] += dot_nt(part, keyval_ref[...])

    @pl.when(step == pl.num_programs(0) - 1)
    def _():
        for slot in range(GROUPS):
            rows = slice(slot * SLOT_ROWS, (slot + 1) * SLOT_ROWS)
            low_rank = jnp.concatenate(
                [rank_ref[spot_ref[2 * slot]], rank_ref[spot_ref[2 * slot + 1]]], axis=0
            )
            query = query_sum[rows, :] + jnp.dot(
                low_rank, up_ref[task_ref[slot]], preferred_element_type=jnp.float32
            )
            for head in range(OWN_HEADS):
                lanes = slice(head * HEAD_SIZE, (head + 1) * HEAD_SIZE)
                turned = norm_rotate(
                    query[:, lanes], gain_ref[...], cos_ref[rows, :], sin_ref[rows, :]
                ).astype(jnp.bfloat16)
                out_ref[slot, :, lanes] = turned
            out_ref[slot, :, OWN_WIDTH:] = keyval_sum[rows, :].astype(jnp.bfloat16)


def project(tasks, spots, tokens, query_weight, keyval_weight, low_rank, up_maps, cosine, sine, gain):
    tile = 2560
    whole = lambda *shape: pl.BlockSpec(shape, lambda k, t, s: (0,) * len(shape))
    return pl.pallas_call(
        project_kernel,
        grid_spec=pltpu.PrefetchScalarGridSpec(
            num_scalar_prefetch=2,
            grid=(MODEL_WIDTH // tile,),
            in_specs=[
                pl.BlockSpec((ROWS, tile), lambda k, t, s: (0, k)),
                pl.BlockSpec((tile, OWN_WIDTH), lambda k, t, s: (k, 0)),
                pl.BlockSpec((HEAD_SIZE, tile), lambda k, t, s: (0, k)),
                whole(SHARDS, HALF_ROWS, ADAPTER_RANK),
                whole(ADAPTER_COUNT, ADAPTER_RANK, OWN_WIDTH),
                whole(ROWS, HEAD_SIZE),
                whole(ROWS, HEAD_SIZE),
                whole(1, HEAD_SIZE),
            ],
            out_specs=whole(GROUPS, SLOT_ROWS, SENT_WIDTH),
            scratch_shapes=[
                pltpu.VMEM((ROWS, OWN_WIDTH), jnp.float32),
                pltpu.VMEM((ROWS, HEAD_SIZE), jnp.float32),
            ],
        ),
        out_shape=jax.ShapeDtypeStruct((GROUPS, SLOT_ROWS, SENT_WIDTH), jnp.bfloat16),
        compiler_params=pltpu.CompilerParams(vmem_limit_bytes=60 * 2**20),
        cost_estimate=pl.CostEstimate(
            flops=20 * ROWS * MODEL_WIDTH * SENT_WIDTH, bytes_accessed=13_000_000, transcendentals=0
        ),
        name="project",
    )(tasks, spots, tokens, query_weight, keyval_weight, low_rank, up_maps, cosine, sine, gain)


def attend_kernel(
    order_ref,
    local_ref,
    reach_ref,
    place_ref,
    own_ref,
    other_ref,
    page_ref,
    suffix_ref,
    cos_ref,
    sin_ref,
    gain_ref,
    out_ref,
):
    half = place_ref[0]
    flip = place_ref[1]
    span = GROUPS * PROMPT_TOKENS // SHARDS
    pages = page_ref[...].reshape(span, 2 * HEAD_SIZE)
    keys = pages[:, :HEAD_SIZE]
    values = jnp.concatenate(
        [jnp.ones((span, HEAD_SIZE), jnp.bfloat16), pages[:, HEAD_SIZE:]], axis=1
    )
    first_sent = jnp.where(half == 0, own_ref[0], other_ref[0])
    second_sent = jnp.where(half == 0, other_ref[0], own_ref[0])
    low_part = first_sent[:, OWN_WIDTH:].astype(jnp.float32)
    high_part = second_sent[:, OWN_WIDTH:].astype(jnp.float32)
    lane = lax.broadcasted_iota(jnp.int32, (SLOT_ROWS, HEAD_SIZE), 1)
    low_lanes = lane < HEAD_SIZE // 2
    new_keys = jnp.where(low_lanes, low_part, pltpu.roll(high_part, HEAD_SIZE // 2, 1))
    new_values = jnp.where(low_lanes, pltpu.roll(low_part, HEAD_SIZE // 2, 1), high_part)
    new_keys = norm_rotate(new_keys, gain_ref[...], cos_ref[0], sin_ref[0])
    suffix_rows = SLOT_SAMPLES * 16
    extra = suffix_rows + 2 * SLOT_ROWS
    suffix = suffix_ref[0, :suffix_rows, :]
    zeros = jnp.zeros((SLOT_ROWS, HEAD_SIZE), jnp.bfloat16)
    extra_keys = jnp.concatenate(
        [suffix[:, :HEAD_SIZE], new_keys.astype(jnp.bfloat16), zeros], axis=0
    )
    extra_values = jnp.concatenate(
        [suffix[:, HEAD_SIZE:], new_values.astype(jnp.bfloat16), zeros], axis=0
    )
    extra_values = jnp.concatenate(
        [jnp.ones((extra, HEAD_SIZE), jnp.bfloat16), extra_values], axis=1
    )
    lengths = suffix_ref[0, suffix_rows:, :].astype(jnp.float32)
    sample_of = lax.broadcasted_iota(jnp.int32, (SLOT_SAMPLES, suffix_rows), 0)
    column_sample = lax.broadcasted_iota(jnp.int32, (SLOT_SAMPLES, suffix_rows), 1) // 16
    column_length = jnp.sum(
        jnp.where(sample_of == column_sample, lengths, 0.0), axis=0, keepdims=True
    )
    row = lax.broadcasted_iota(jnp.int32, (SLOT_ROWS, suffix_rows), 0)
    column = lax.broadcasted_iota(jnp.int32, (SLOT_ROWS, suffix_rows), 1)
    suffix_seen = (row // DECODE_STEPS == column // 16) & (
        (half * 16 + column % 16).astype(jnp.float32) < column_length
    )
    row = lax.broadcasted_iota(jnp.int32, (SLOT_ROWS, 2 * SLOT_ROWS), 0)
    column = lax.broadcasted_iota(jnp.int32, (SLOT_ROWS, 2 * SLOT_ROWS), 1)
    new_seen = (
        (row // DECODE_STEPS == column // DECODE_STEPS)
        & (column % DECODE_STEPS <= row % DECODE_STEPS)
        & (column // HALF_ROWS == half)
    )
    bias = jnp.concatenate(
        [jnp.where(suffix_seen, 0.0, masked_low), jnp.where(new_seen, 0.0, masked_low)], axis=1
    )
    bias = jnp.concatenate([bias] * TILE_HEADS, axis=0)
    logs = jnp.zeros((SLOT_ROWS, HEAD_SIZE), jnp.float32)

    def finish(first, total, peak):
        nonlocal logs
        denominator = total[:, :HEAD_SIZE]
        attended = (total[:, HEAD_SIZE:] / denominator).astype(jnp.bfloat16)
        log_sum = peak + jnp.log2(denominator)
        for index in range(TILE_HEADS):
            head = first + index
            rows = slice(index * SLOT_ROWS, (index + 1) * SLOT_ROWS)
            top = attended[rows][:HALF_ROWS]
            low = attended[rows][HALF_ROWS:]
            lanes = slice(head * HEAD_SIZE, (head + 1) * HEAD_SIZE)
            out_ref[0, 0, :, lanes] = jnp.where(flip == 0, top, low)
            out_ref[0, 1, :, lanes] = jnp.where(flip == 0, low, top)
            logs = jnp.where(lane == head, log_sum[rows], logs)

    def query_of(first):
        query = []
        for head in range(first, first + TILE_HEADS):
            source, start = divmod(head, OWN_HEADS)
            sent = second_sent if source else first_sent
            query.append(sent[:, start * HEAD_SIZE : (start + 1) * HEAD_SIZE])
        return jnp.concatenate(query, axis=0)


    def scores(first):
        query = query_of(first)
        return dot_nt(query, keys), dot_nt(query, extra_keys) + bias

    tiles = list(range(0, HEAD_FAN, TILE_HEADS))
    ready = scores(tiles[0])
    for number, first in enumerate(tiles):
        prefix_score, extra_score = ready
        if number + 1 < len(tiles):
            ready = scores(tiles[number + 1])
        peak = jnp.maximum(
            jnp.max(prefix_score, axis=-1, keepdims=True),
            jnp.max(extra_score, axis=-1, keepdims=True),
        )
        prefix_weight = jnp.exp2(prefix_score - peak).astype(jnp.bfloat16)
        extra_weight = jnp.exp2(extra_score - peak).astype(jnp.bfloat16)
        total = jnp.dot(prefix_weight, values, preferred_element_type=jnp.float32) + jnp.dot(
            extra_weight, extra_values, preferred_element_type=jnp.float32
        )
        finish(first, total, peak)
    high_term = logs.astype(jnp.bfloat16).astype(jnp.float32)
    rest = logs - high_term
    mid_term = rest.astype(jnp.bfloat16).astype(jnp.float32)
    low_term = rest - mid_term
    packed = (
        high_term + pltpu.roll(mid_term, HEAD_FAN, 1) + pltpu.roll(low_term, 2 * HEAD_FAN, 1)
    ).astype(jnp.bfloat16)
    top = packed[:HALF_ROWS]
    low = packed[HALF_ROWS:]
    out_ref[0, 0, :, HEAD_FAN * HEAD_SIZE :] = jnp.where(flip == 0, top, low)
    out_ref[0, 1, :, HEAD_FAN * HEAD_SIZE :] = jnp.where(flip == 0, low, top)


def attend(order, local, reach, place, own, other, pages, suffix, cosine, sine, gain):
    block = PROMPT_TOKENS // SHARDS
    return pl.pallas_call(
        attend_kernel,
        grid_spec=pltpu.PrefetchScalarGridSpec(
            num_scalar_prefetch=4,
            grid=(GROUPS,),
            in_specs=[
                pl.BlockSpec((1, SLOT_ROWS, SENT_WIDTH), lambda i, o, l, r, p: (r[i], 0, 0)),
                pl.BlockSpec((1, SLOT_ROWS, SENT_WIDTH), lambda i, o, l, r, p: (r[i], 0, 0)),
                pl.BlockSpec(
                    (GROUPS, 1, block, 2 * HEAD_SIZE), lambda i, o, l, r, p: (0, l[i], 0, 0)
                ),
                pl.BlockSpec(
                    (1, suffix.shape[1], 2 * HEAD_SIZE), lambda i, o, l, r, p: (r[i], 0, 0)
                ),
                pl.BlockSpec((1, SLOT_ROWS, HEAD_SIZE), lambda i, o, l, r, p: (r[i], 0, 0)),
                pl.BlockSpec((1, SLOT_ROWS, HEAD_SIZE), lambda i, o, l, r, p: (r[i], 0, 0)),
                pl.BlockSpec((1, HEAD_SIZE), lambda i, o, l, r, p: (0, 0)),
            ],
            out_specs=pl.BlockSpec(
                (1, 2, HALF_ROWS, BACK_WIDTH), lambda i, o, l, r, p: (o[i], 0, 0, 0)
            ),
        ),
        out_shape=jax.ShapeDtypeStruct((GROUPS, 2, HALF_ROWS, BACK_WIDTH), jnp.bfloat16),
        compiler_params=pltpu.CompilerParams(vmem_limit_bytes=60 * 2**20),
        cost_estimate=pl.CostEstimate(
            flops=20 * GROUPS * 512 * 2432 * 384,
            bytes_accessed=8_000_000,
            transcendentals=GROUPS * 512 * 2432,
        ),
        name="attend",
    )(order, local, reach, place, own, other, pages, suffix, cosine, sine, gain)


def combine(place_ref, back_ref, mixed_ref):
    half = place_ref[0]
    rows = GROUPS * HALF_ROWS
    slots = [
        (place_ref[1] + index // 2) % 4 * 2 + (place_ref[2] ^ (index % 2))
        for index in range(GROUPS)
    ]

    def part_of(source, lanes):
        parts = [back_ref[slot, source, :, lanes] for slot in slots]
        return jnp.concatenate(parts, axis=0).astype(jnp.float32)

    def log_of(source):
        packed = part_of(source, slice(HEAD_FAN * HEAD_SIZE, BACK_WIDTH))
        return (
            packed
            + pltpu.roll(packed, HEAD_SIZE - HEAD_FAN, 1)
            + pltpu.roll(packed, HEAD_SIZE - 2 * HEAD_FAN, 1)
        )

    first_log = log_of(0)
    second_log = log_of(1)
    peak = jnp.maximum(first_log, second_log)
    first_part = jnp.exp2(first_log - peak)
    second_part = jnp.exp2(second_log - peak)
    both = first_part + second_part
    first_part = first_part / both
    second_part = second_part / both

    def attended(head):
        lanes = slice(head * HEAD_SIZE, (head + 1) * HEAD_SIZE)
        return (
            part_of(0, lanes) * first_part[:, head : head + 1]
            + part_of(1, lanes) * second_part[:, head : head + 1]
        ).astype(jnp.bfloat16)

    for head in range(OWN_HEADS):
        low = attended(head)
        high = attended(head + OWN_HEADS)
        lanes = slice(head * HEAD_SIZE, (head + 1) * HEAD_SIZE)
        mixed_ref[:, lanes] = jnp.where(half == 0, low, high)
        lanes = slice((head + OWN_HEADS) * HEAD_SIZE, (head + OWN_HEADS + 1) * HEAD_SIZE)
        mixed_ref[:, lanes] = jnp.where(half == 0, high, low)


def times_weights(mixed_ref, own_ref, other_ref):
    return (
        jnp.dot(mixed_ref[:, :OWN_WIDTH], own_ref[...], preferred_element_type=jnp.float32)
        + jnp.dot(mixed_ref[:, OWN_WIDTH:], other_ref[...], preferred_element_type=jnp.float32)
    ).astype(jnp.bfloat16)


def left_kernel(place_ref, back_ref, own_ref, other_ref, mixed_ref, *out_refs):
    @pl.when(pl.program_id(0) == 0)
    def _():
        combine(place_ref, back_ref, mixed_ref)

    product = times_weights(mixed_ref, own_ref, other_ref)
    for index, out_ref in enumerate(out_refs):
        out_ref[...] = product[2 * index * HALF_ROWS : 2 * (index + 1) * HALF_ROWS]


def right_kernel(mixed_ref, own_ref, other_ref, kept_ref, given_ref):
    product = times_weights(mixed_ref, own_ref, other_ref)
    for index in range(4):
        rows = slice(index * HALF_ROWS, (index + 1) * HALF_ROWS)
        start = 2 * index * HALF_ROWS
        kept_ref[rows, :] = product[start : start + HALF_ROWS]
        given_ref[rows, :] = product[start + HALF_ROWS : start + 2 * HALF_ROWS]


OUT_TILE = 1280
SIDE = MODEL_WIDTH // 2
OUT_COST = pl.CostEstimate(
    flops=8 * GROUPS * HALF_ROWS * SIDE * 1024, bytes_accessed=8_000_000, transcendentals=0
)


def left_product(place, back, own_weight, other_weight):
    rows = GROUPS * HALF_ROWS
    return pl.pallas_call(
        left_kernel,
        grid_spec=pltpu.PrefetchScalarGridSpec(
            num_scalar_prefetch=1,
            grid=(SIDE // OUT_TILE,),
            in_specs=[
                pl.BlockSpec((GROUPS, 2, HALF_ROWS, BACK_WIDTH), lambda n, p: (0, 0, 0, 0)),
                pl.BlockSpec((OWN_WIDTH, OUT_TILE), lambda n, p: (0, n)),
                pl.BlockSpec((OWN_WIDTH, OUT_TILE), lambda n, p: (0, n)),
            ],
            out_specs=[pl.BlockSpec((rows, 2 * OWN_WIDTH), lambda n, p: (0, 0))]
            + [pl.BlockSpec((rows // 4, OUT_TILE), lambda n, p: (0, n))] * 4,
        ),
        out_shape=[jax.ShapeDtypeStruct((rows, 2 * OWN_WIDTH), jnp.bfloat16)]
        + [jax.ShapeDtypeStruct((rows // 4, SIDE), jnp.bfloat16)] * 4,
        compiler_params=pltpu.CompilerParams(vmem_limit_bytes=60 * 2**20),
        cost_estimate=OUT_COST,
        name="left_product",
    )(place, back, own_weight, other_weight)


def right_product(mixed, own_weight, other_weight):
    rows = GROUPS * HALF_ROWS
    skip = SIDE // OUT_TILE
    return pl.pallas_call(
        right_kernel,
        grid=(SIDE // OUT_TILE,),
        in_specs=[
            pl.BlockSpec((rows, 2 * OWN_WIDTH), lambda n: (0, 0)),
            pl.BlockSpec((OWN_WIDTH, OUT_TILE), lambda n: (0, n + skip)),
            pl.BlockSpec((OWN_WIDTH, OUT_TILE), lambda n: (0, n + skip)),
        ],
        out_specs=[pl.BlockSpec((rows // 2, OUT_TILE), lambda n: (0, n))] * 2,
        out_shape=[jax.ShapeDtypeStruct((rows // 2, SIDE), jnp.bfloat16)] * 2,
        compiler_params=pltpu.CompilerParams(vmem_limit_bytes=60 * 2**20),
        cost_estimate=OUT_COST,
        name="right_product",
    )(mixed, own_weight, other_weight)


def total_of(parts):
    total = parts[0].astype(jnp.float32)
    for part in parts[1:]:
        total = total + part.astype(jnp.float32)
    return total


def along_x(distance):
    return [(shard, shard // 4 * 4 + (shard + distance) % 4) for shard in range(SHARDS)]


def along_y(distance):
    return [(shard, (shard + 4 * distance) % SHARDS) for shard in range(SHARDS)]


def across_groups(bits):
    return [(group, group ^ bits) for group in range(GROUPS)]


def exchange_groups(blocks, group):
    by_core = blocks.reshape((GROUPS // 2, 2) + blocks.shape[1:])
    kept = lax.dynamic_index_in_dim(by_core, group % 2, 1, keepdims=True)
    given = lax.dynamic_index_in_dim(by_core, 1 - group % 2, 1, keepdims=True)
    given = lax.ppermute(given, "grp", across_groups(1))
    both = jnp.concatenate([kept, given], axis=1)
    arrived = []
    for k in range(GROUPS // 2):
        block = lax.dynamic_index_in_dim(both, (group // 2) ^ k, 0, keepdims=False)
        arrived.append(lax.ppermute(block, "grp", across_groups(2 * k)) if k else block)
    return arrived


def swap(block, axes, groups=None):
    return lax.all_to_all(
        block, axes, split_axis=0, concat_axis=0, tiled=True, axis_index_groups=groups
    )


def shards(
    tokens,
    prompt_cache,
    generated_cache,
    suffix_lengths,
    fanout,
    prompt_adapter,
    query_weight,
    key_value_weight,
    output_weight,
    adapter_down_maps,
    adapter_up_maps,
    query_norm_gain,
    key_norm_gain,
):
    group = lax.axis_index("grp")
    shard = lax.axis_index("ad")
    head = shard // 2
    half = shard % 2
    local_table = slot_prompts(fanout, GROUPS, OWNED)

    part_rows = lax.all_gather(tokens, "ad", axis=0, tiled=True)

    slot_suffix = generated_cache.reshape(GROUPS, SLOT_SAMPLES * 16, 2 * HEAD_SIZE)
    slot_lengths = suffix_lengths.reshape(GROUPS, SLOT_SAMPLES, 1).astype(jnp.bfloat16)
    slot_suffix = jnp.concatenate(
        [slot_suffix, jnp.broadcast_to(slot_lengths, (GROUPS, SLOT_SAMPLES, 2 * HEAD_SIZE))], axis=1
    )
    suffix = jnp.concatenate(exchange_groups(slot_suffix, group), axis=0)

    owners = jnp.arange(GROUPS, dtype=jnp.int32)
    local_of_slot = lax.dynamic_index_in_dim(local_table, group, 1, keepdims=False)
    prompts = owners * OWNED + local_of_slot
    hit = prompts[:, None] == jnp.arange(prompt_adapter.shape[0], dtype=jnp.int32)[None, :]
    tasks = jnp.sum(hit.astype(jnp.int32) * prompt_adapter[None, :], axis=1)
    own_rows = tokens.shape[0]
    columns = swap(jnp.swapaxes(tokens.reshape(own_rows, SHARDS, -1), 0, 1), "ad")
    rank_all = jnp.dot(
        columns.reshape(ROWS, -1),
        adapter_down_maps.reshape(-1, ADAPTER_COUNT * ADAPTER_RANK),
        preferred_element_type=jnp.float32,
    ).reshape(GROUPS, SLOT_ROWS, ADAPTER_COUNT, ADAPTER_RANK)
    chosen = (tasks[:, None] == jnp.arange(ADAPTER_COUNT, dtype=jnp.int32)[None, :]).astype(
        jnp.float32
    )
    rank_part = jnp.sum(rank_all * chosen[:, None, :, None], axis=2)
    rank_rows = jnp.sum(swap(rank_part.reshape(SHARDS, own_rows, ADAPTER_RANK), "ad"), axis=0)
    rank_rows = rank_rows.astype(jnp.bfloat16)

    ring = [rank_rows] + [lax.ppermute(rank_rows, "ad", along_x(k)) for k in (1, 2, 3)]
    ring = jnp.stack(ring)

    low_rank = jnp.stack([ring] + [lax.ppermute(ring, "ad", along_y(k)) for k in (1, 2, 3)])
    every = jnp.arange(SHARDS, dtype=jnp.int32)
    spots = ((shard // 4 - every // 4) % 4) * 4 + (shard % 4 - every % 4) % 4

    slice_rows = OWN_WIDTH // GROUPS
    weight_slice = lax.dynamic_slice_in_dim(output_weight, group * slice_rows, slice_rows, 0)
    low_rank, head_pages, weight_slice = lax.optimization_barrier(
        (low_rank, jnp.swapaxes(prompt_cache, 0, 1), weight_slice)
    )
    arrived = swap(head_pages, "ad", ROLE_GROUPS)
    weight_slice = lax.ppermute(weight_slice, "ad", PARTNERS)
    part_rows, weight_slice = lax.optimization_barrier((part_rows, weight_slice))
    other_weight = lax.all_gather(weight_slice, "grp", axis=0, tiled=True)

    steps = jnp.arange(DECODE_STEPS, dtype=jnp.int32)
    position = (PROMPT_TOKENS + suffix_lengths[:, None] + steps[None, :]).astype(jnp.float32)
    cosine, sine = angle_tables(position.reshape(ROWS))
    sent = project(
        tasks,
        spots,
        part_rows,
        query_weight,
        key_value_weight.transpose(1, 2, 0).reshape(HEAD_SIZE, MODEL_WIDTH),
        low_rank.reshape(SHARDS, own_rows, ADAPTER_RANK),
        adapter_up_maps,
        cosine,
        sine,
        query_norm_gain.reshape(1, HEAD_SIZE) * exponent_scale,
    )
    own_sent = exchange_groups(sent, group)
    other_sent = jnp.concatenate([lax.ppermute(part, "ad", PARTNERS) for part in own_sent], axis=0)
    own_sent = jnp.concatenate(own_sent, axis=0)

    local = lax.dynamic_index_in_dim(local_table, group, 0, keepdims=False)
    rank_key = local * GROUPS + owners
    spot = jnp.sum((rank_key[None, :] < rank_key[:, None]).astype(jnp.int32), axis=1)
    placed = (spot[None, :] == owners[:, None]).astype(jnp.int32)
    order = jnp.sum(placed * owners[None, :], axis=1)
    local_sorted = jnp.sum(placed * local[None, :], axis=1)
    flip = (head + group) % 2
    place = jnp.stack([half, flip]).astype(jnp.int32)
    far_lengths = suffix[:, SLOT_SAMPLES * 16 :, 0].astype(jnp.float32)
    far_position = PROMPT_TOKENS + far_lengths[:, :, None] + steps.astype(jnp.float32)
    far_cosine, far_sine = angle_tables(far_position.reshape(GROUPS, SLOT_ROWS))
    partial = attend(
        order,
        local_sorted,
        order ^ group,
        place,
        own_sent,
        other_sent,
        arrived,
        suffix,
        far_cosine,
        far_sine,
        key_norm_gain.reshape(1, HEAD_SIZE),
    )
    back = swap(
        partial.reshape(2 * GROUPS, HALF_ROWS, BACK_WIDTH), ("grp", "ad"), HEAD_GROUPS
    ).reshape(GROUPS, 2, HALF_ROWS, BACK_WIDTH)
    place = jnp.stack([half, shard // 4, head % 2]).astype(jnp.int32)
    mixed, *by_y = left_product(place, back, output_weight, other_weight)
    by_y = by_y[:1] + [lax.ppermute(by_y[k], "ad", along_y(k)) for k in (1, 2, 3)]
    kept, given = right_product(mixed, output_weight, other_weight)
    given = lax.ppermute(given, "ad", ACROSS)
    left = total_of(by_y)
    left_given = lax.ppermute(left[HALF_ROWS:].astype(jnp.bfloat16), "ad", ACROSS)
    right = total_of([kept, given]).reshape(4, HALF_ROWS, SIDE)
    right_parts = [right[0]] + [
        lax.ppermute(right[k].astype(jnp.bfloat16), "ad", along_y(k)) for k in (1, 2, 3)
    ]
    left = left[:HALF_ROWS] + left_given.astype(jnp.float32)
    right = total_of(right_parts)
    return jnp.concatenate([left.astype(jnp.bfloat16), right.astype(jnp.bfloat16)], axis=1)


def solution(mesh):
    return jax.shard_map(
        shards,
        mesh=mesh,
        in_specs=(
            P(("grp", "ad"), None),
            P("grp", None, "ad", None),
            P("grp", "ad", None),
            P("grp"),
            P(),
            P(),
            P(None, "ad"),
            P(None, None, "ad"),
            P("ad", None),
            P("ad", None, None),
            P(None, None, "ad"),
            P(),
            P(),
        ),
        out_specs=P(("grp", "ad"), None),
        check_vma=False,
    )
```

```python
import functools

import jax
import jax.numpy as jnp
from jax import lax
from jax.experimental import pallas as pl
from jax.experimental.pallas import tpu as pltpu
from jax.sharding import PartitionSpec as P

MODEL_WIDTH = 5120
KEY_VALUE_HEADS = 8
HEAD_SIZE = 128
ADAPTER_RANK = 128
FAN = 2
DECODE_STEPS = 4
ADAPTER_COUNT = 4
PROMPT_TOKENS = 4096
GROUPS = 8
SHARDS = 16
OWNED = 4
SLOT_SAMPLES = 16
SLOT_ROWS = SLOT_SAMPLES * DECODE_STEPS
HALF_ROWS = SLOT_ROWS // 2
ROWS = GROUPS * SLOT_ROWS
OWN_HEADS = 4
PIECES = 4
PIECE = MODEL_WIDTH // PIECES
OWN_WIDTH = OWN_HEADS * HEAD_SIZE
HEAD_FAN = 2 * OWN_HEADS
SENT_WIDTH = OWN_WIDTH + HEAD_SIZE
TILE_HEADS = 4
BACK_WIDTH = HEAD_FAN * HEAD_SIZE + HEAD_SIZE

theta_base = 1000000.0
norm_eps = 1e-06
masked_low = -1e30
exponent_scale = HEAD_SIZE**-0.5 * 1.4426950408889634

ROLE_GROUPS = [[0, 3, 4, 7, 8, 11, 12, 15], [1, 2, 5, 6, 9, 10, 13, 14]]
HEAD_GROUPS = [
    [group * SHARDS + 2 * head + half for group in range(GROUPS) for half in range(2)]
    for head in range(KEY_VALUE_HEADS)
]
ACROSS = [(shard, shard // 4 * 4 + 3 - shard % 4) for shard in range(SHARDS)]
PARTNERS = [(shard, shard ^ 1) for shard in range(SHARDS)]


def slot_prompts(fanout, groups, owned_count):
    listed = jnp.any(
        fanout[:, :, None] == jnp.arange(groups, dtype=jnp.int32)[None, None, :], axis=1
    )
    listed = listed.astype(jnp.int32).reshape(groups, owned_count, groups)
    return jnp.sum(listed * jnp.arange(owned_count, dtype=jnp.int32)[None, :, None], axis=1)


def angle_tables(position):
    half_len = HEAD_SIZE // 2
    inverse = theta_base ** (-2.0 * jnp.arange(half_len, dtype=jnp.float32) / HEAD_SIZE)
    angles = position[..., None] * inverse
    cosine = jnp.cos(angles)
    sine = jnp.sin(angles)
    return (
        jnp.concatenate([cosine, cosine], axis=-1),
        jnp.concatenate([-sine, sine], axis=-1),
    )


def norm_rotate(vector, gain, cosine, sine):
    mean_sq = jnp.mean(vector * vector, axis=-1, keepdims=True)
    scaled = vector * lax.rsqrt(mean_sq + norm_eps) * gain
    return scaled * cosine + pltpu.roll(scaled, HEAD_SIZE // 2, 1) * sine


def dot_nt(left, right):
    return lax.dot_general(
        left, right, (((1,), (1,)), ((), ())), preferred_element_type=jnp.float32
    )


def project_kernel(
    task_ref,
    spot_ref,
    tokens_ref,
    query_ref,
    keyval_ref,
    rank_ref,
    up_ref,
    cos_ref,
    sin_ref,
    gain_ref,
    out_ref,
    tokens,
    query_weight,
    keyval_weight,
    query_sum,
    keyval_sum,
    sems,
):
    copies = []
    for piece in range(PIECES):
        span = pl.ds(piece * PIECE, PIECE)
        copies.append(
            [
                pltpu.make_async_copy(
                    tokens_ref.at[:, span], tokens.at[:, span], sems.at[0, piece]
                ),
                pltpu.make_async_copy(
                    query_ref.at[span, :], query_weight.at[span, :], sems.at[1, piece]
                ),
                pltpu.make_async_copy(
                    keyval_ref.at[:, span], keyval_weight.at[:, span], sems.at[2, piece]
                ),
            ]
        )
        for copy in copies[-1]:
            copy.start()
    for piece in range(PIECES):
        for copy in copies[piece]:
            copy.wait()
        span = slice(piece * PIECE, (piece + 1) * PIECE)
        part = tokens[:, span]
        query = jnp.dot(part, query_weight[span, :], preferred_element_type=jnp.float32)
        keyval = dot_nt(part, keyval_weight[:, span])
        query_sum[...] = query if piece == 0 else query_sum[...] + query
        keyval_sum[...] = keyval if piece == 0 else keyval_sum[...] + keyval

    for slot in range(GROUPS):
        rows = slice(slot * SLOT_ROWS, (slot + 1) * SLOT_ROWS)
        low_rank = jnp.concatenate(
            [rank_ref[spot_ref[2 * slot]], rank_ref[spot_ref[2 * slot + 1]]], axis=0
        )
        query = query_sum[rows, :] + jnp.dot(
            low_rank, up_ref[task_ref[slot]], preferred_element_type=jnp.float32
        )
        for head in range(OWN_HEADS):
            lanes = slice(head * HEAD_SIZE, (head + 1) * HEAD_SIZE)
            turned = norm_rotate(
                query[:, lanes], gain_ref[...], cos_ref[rows, :], sin_ref[rows, :]
            ).astype(jnp.bfloat16)
            out_ref[slot, :, lanes] = turned
        out_ref[slot, :, OWN_WIDTH:] = keyval_sum[rows, :].astype(jnp.bfloat16)


def project(tasks, spots, tokens, query_weight, keyval_weight, low_rank, up_maps, cosine, sine, gain):
    whole = lambda *shape: pl.BlockSpec(shape, lambda k, t, s: (0,) * len(shape))
    return pl.pallas_call(
        project_kernel,
        grid_spec=pltpu.PrefetchScalarGridSpec(
            num_scalar_prefetch=2,
            grid=(1,),
            in_specs=[pl.BlockSpec(memory_space=pl.ANY)] * 3
            + [
                whole(SHARDS, HALF_ROWS, ADAPTER_RANK),
                whole(ADAPTER_COUNT, ADAPTER_RANK, OWN_WIDTH),
                whole(ROWS, HEAD_SIZE),
                whole(ROWS, HEAD_SIZE),
                whole(1, HEAD_SIZE),
            ],
            out_specs=whole(GROUPS, SLOT_ROWS, SENT_WIDTH),
            scratch_shapes=[
                pltpu.VMEM((ROWS, MODEL_WIDTH), jnp.bfloat16),
                pltpu.VMEM((MODEL_WIDTH, OWN_WIDTH), jnp.bfloat16),
                pltpu.VMEM((HEAD_SIZE, MODEL_WIDTH), jnp.bfloat16),
                pltpu.VMEM((ROWS, OWN_WIDTH), jnp.float32),
                pltpu.VMEM((ROWS, HEAD_SIZE), jnp.float32),
                pltpu.SemaphoreType.DMA((3, PIECES)),
            ],
        ),
        out_shape=jax.ShapeDtypeStruct((GROUPS, SLOT_ROWS, SENT_WIDTH), jnp.bfloat16),
        compiler_params=pltpu.CompilerParams(vmem_limit_bytes=60 * 2**20),
        cost_estimate=pl.CostEstimate(
            flops=20 * ROWS * MODEL_WIDTH * SENT_WIDTH, bytes_accessed=13_000_000, transcendentals=0
        ),
        name="project",
    )(tasks, spots, tokens, query_weight, keyval_weight, low_rank, up_maps, cosine, sine, gain)


def attend_kernel(
    order_ref,
    local_ref,
    reach_ref,
    place_ref,
    own_ref,
    other_ref,
    page_ref,
    suffix_ref,
    cos_ref,
    sin_ref,
    gain_ref,
    out_ref,
):
    half = place_ref[0]
    flip = place_ref[1]
    span = GROUPS * PROMPT_TOKENS // SHARDS
    pages = page_ref[...].reshape(span, 2 * HEAD_SIZE)
    keys = pages[:, :HEAD_SIZE]
    values = jnp.concatenate(
        [jnp.ones((span, HEAD_SIZE), jnp.bfloat16), pages[:, HEAD_SIZE:]], axis=1
    )
    first_sent = jnp.where(half == 0, own_ref[0], other_ref[0])
    second_sent = jnp.where(half == 0, other_ref[0], own_ref[0])
    low_part = first_sent[:, OWN_WIDTH:].astype(jnp.float32)
    high_part = second_sent[:, OWN_WIDTH:].astype(jnp.float32)
    lane = lax.broadcasted_iota(jnp.int32, (SLOT_ROWS, HEAD_SIZE), 1)
    low_lanes = lane < HEAD_SIZE // 2
    new_keys = jnp.where(low_lanes, low_part, pltpu.roll(high_part, HEAD_SIZE // 2, 1))
    new_values = jnp.where(low_lanes, pltpu.roll(low_part, HEAD_SIZE // 2, 1), high_part)
    new_keys = norm_rotate(new_keys, gain_ref[...], cos_ref[0], sin_ref[0])
    suffix_rows = SLOT_SAMPLES * 16
    extra = suffix_rows + 2 * SLOT_ROWS
    suffix = suffix_ref[0, :suffix_rows, :]
    zeros = jnp.zeros((SLOT_ROWS, HEAD_SIZE), jnp.bfloat16)
    extra_keys = jnp.concatenate(
        [suffix[:, :HEAD_SIZE], new_keys.astype(jnp.bfloat16), zeros], axis=0
    )
    extra_values = jnp.concatenate(
        [suffix[:, HEAD_SIZE:], new_values.astype(jnp.bfloat16), zeros], axis=0
    )
    extra_values = jnp.concatenate(
        [jnp.ones((extra, HEAD_SIZE), jnp.bfloat16), extra_values], axis=1
    )
    lengths = suffix_ref[0, suffix_rows:, :].astype(jnp.float32)
    sample_of = lax.broadcasted_iota(jnp.int32, (SLOT_SAMPLES, suffix_rows), 0)
    column_sample = lax.broadcasted_iota(jnp.int32, (SLOT_SAMPLES, suffix_rows), 1) // 16
    column_length = jnp.sum(
        jnp.where(sample_of == column_sample, lengths, 0.0), axis=0, keepdims=True
    )
    row = lax.broadcasted_iota(jnp.int32, (SLOT_ROWS, suffix_rows), 0)
    column = lax.broadcasted_iota(jnp.int32, (SLOT_ROWS, suffix_rows), 1)
    suffix_seen = (row // DECODE_STEPS == column // 16) & (
        (half * 16 + column % 16).astype(jnp.float32) < column_length
    )
    row = lax.broadcasted_iota(jnp.int32, (SLOT_ROWS, 2 * SLOT_ROWS), 0)
    column = lax.broadcasted_iota(jnp.int32, (SLOT_ROWS, 2 * SLOT_ROWS), 1)
    new_seen = (
        (row // DECODE_STEPS == column // DECODE_STEPS)
        & (column % DECODE_STEPS <= row % DECODE_STEPS)
        & (column // HALF_ROWS == half)
    )
    bias = jnp.concatenate(
        [jnp.where(suffix_seen, 0.0, masked_low), jnp.where(new_seen, 0.0, masked_low)], axis=1
    )
    bias = jnp.concatenate([bias] * TILE_HEADS, axis=0)
    logs = jnp.zeros((SLOT_ROWS, HEAD_SIZE), jnp.float32)

    def finish(first, total, peak):
        nonlocal logs
        denominator = total[:, :HEAD_SIZE]
        attended = (total[:, HEAD_SIZE:] / denominator).astype(jnp.bfloat16)
        log_sum = peak + jnp.log2(denominator)
        for index in range(TILE_HEADS):
            head = first + index
            rows = slice(index * SLOT_ROWS, (index + 1) * SLOT_ROWS)
            top = attended[rows][:HALF_ROWS]
            low = attended[rows][HALF_ROWS:]
            lanes = slice(head * HEAD_SIZE, (head + 1) * HEAD_SIZE)
            out_ref[0, 0, :, lanes] = jnp.where(flip == 0, top, low)
            out_ref[0, 1, :, lanes] = jnp.where(flip == 0, low, top)
            logs = jnp.where(lane == head, log_sum[rows], logs)

    def query_of(first):
        query = []
        for head in range(first, first + TILE_HEADS):
            source, start = divmod(head, OWN_HEADS)
            sent = second_sent if source else first_sent
            query.append(sent[:, start * HEAD_SIZE : (start + 1) * HEAD_SIZE])
        return jnp.concatenate(query, axis=0)


    def scores(first):
        query = query_of(first)
        return dot_nt(query, keys), dot_nt(query, extra_keys) + bias

    tiles = list(range(0, HEAD_FAN, TILE_HEADS))
    ready = scores(tiles[0])
    for number, first in enumerate(tiles):
        prefix_score, extra_score = ready
        if number + 1 < len(tiles):
            ready = scores(tiles[number + 1])
        peak = jnp.maximum(
            jnp.max(prefix_score, axis=-1, keepdims=True),
            jnp.max(extra_score, axis=-1, keepdims=True),
        )
        prefix_weight = jnp.exp2(prefix_score - peak).astype(jnp.bfloat16)
        extra_weight = jnp.exp2(extra_score - peak).astype(jnp.bfloat16)
        total = jnp.dot(prefix_weight, values, preferred_element_type=jnp.float32) + jnp.dot(
            extra_weight, extra_values, preferred_element_type=jnp.float32
        )
        finish(first, total, peak)
    high_term = logs.astype(jnp.bfloat16).astype(jnp.float32)
    rest = logs - high_term
    mid_term = rest.astype(jnp.bfloat16).astype(jnp.float32)
    low_term = rest - mid_term
    packed = (
        high_term + pltpu.roll(mid_term, HEAD_FAN, 1) + pltpu.roll(low_term, 2 * HEAD_FAN, 1)
    ).astype(jnp.bfloat16)
    top = packed[:HALF_ROWS]
    low = packed[HALF_ROWS:]
    out_ref[0, 0, :, HEAD_FAN * HEAD_SIZE :] = jnp.where(flip == 0, top, low)
    out_ref[0, 1, :, HEAD_FAN * HEAD_SIZE :] = jnp.where(flip == 0, low, top)


def attend(order, local, reach, place, own, other, pages, suffix, cosine, sine, gain):
    block = PROMPT_TOKENS // SHARDS
    return pl.pallas_call(
        attend_kernel,
        grid_spec=pltpu.PrefetchScalarGridSpec(
            num_scalar_prefetch=4,
            grid=(GROUPS,),
            in_specs=[
                pl.BlockSpec((1, SLOT_ROWS, SENT_WIDTH), lambda i, o, l, r, p: (r[i], 0, 0)),
                pl.BlockSpec((1, SLOT_ROWS, SENT_WIDTH), lambda i, o, l, r, p: (r[i], 0, 0)),
                pl.BlockSpec(
                    (GROUPS, 1, block, 2 * HEAD_SIZE), lambda i, o, l, r, p: (0, l[i], 0, 0)
                ),
                pl.BlockSpec(
                    (1, suffix.shape[1], 2 * HEAD_SIZE), lambda i, o, l, r, p: (r[i], 0, 0)
                ),
                pl.BlockSpec((1, SLOT_ROWS, HEAD_SIZE), lambda i, o, l, r, p: (r[i], 0, 0)),
                pl.BlockSpec((1, SLOT_ROWS, HEAD_SIZE), lambda i, o, l, r, p: (r[i], 0, 0)),
                pl.BlockSpec((1, HEAD_SIZE), lambda i, o, l, r, p: (0, 0)),
            ],
            out_specs=pl.BlockSpec(
                (1, 2, HALF_ROWS, BACK_WIDTH), lambda i, o, l, r, p: (o[i], 0, 0, 0)
            ),
        ),
        out_shape=jax.ShapeDtypeStruct((GROUPS, 2, HALF_ROWS, BACK_WIDTH), jnp.bfloat16),
        compiler_params=pltpu.CompilerParams(vmem_limit_bytes=60 * 2**20),
        cost_estimate=pl.CostEstimate(
            flops=20 * GROUPS * 512 * 2432 * 384,
            bytes_accessed=8_000_000,
            transcendentals=GROUPS * 512 * 2432,
        ),
        name="attend",
    )(order, local, reach, place, own, other, pages, suffix, cosine, sine, gain)


def combine(place_ref, back_ref, mixed_ref):
    half = place_ref[0]
    rows = GROUPS * HALF_ROWS
    slots = [
        (place_ref[1] + index // 2) % 4 * 2 + (place_ref[2] ^ (index % 2))
        for index in range(GROUPS)
    ]

    def part_of(source, lanes):
        parts = [back_ref[slot, source, :, lanes] for slot in slots]
        return jnp.concatenate(parts, axis=0).astype(jnp.float32)

    def log_of(source):
        packed = part_of(source, slice(HEAD_FAN * HEAD_SIZE, BACK_WIDTH))
        return (
            packed
            + pltpu.roll(packed, HEAD_SIZE - HEAD_FAN, 1)
            + pltpu.roll(packed, HEAD_SIZE - 2 * HEAD_FAN, 1)
        )

    first_log = log_of(0)
    second_log = log_of(1)
    peak = jnp.maximum(first_log, second_log)
    first_part = jnp.exp2(first_log - peak)
    second_part = jnp.exp2(second_log - peak)
    both = first_part + second_part
    first_part = first_part / both
    second_part = second_part / both

    def attended(head):
        lanes = slice(head * HEAD_SIZE, (head + 1) * HEAD_SIZE)
        return (
            part_of(0, lanes) * first_part[:, head : head + 1]
            + part_of(1, lanes) * second_part[:, head : head + 1]
        ).astype(jnp.bfloat16)

    for head in range(OWN_HEADS):
        low = attended(head)
        high = attended(head + OWN_HEADS)
        lanes = slice(head * HEAD_SIZE, (head + 1) * HEAD_SIZE)
        mixed_ref[:, lanes] = jnp.where(half == 0, low, high)
        lanes = slice((head + OWN_HEADS) * HEAD_SIZE, (head + OWN_HEADS + 1) * HEAD_SIZE)
        mixed_ref[:, lanes] = jnp.where(half == 0, high, low)


def times_weights(mixed_ref, own_ref, other_ref):
    return (
        jnp.dot(mixed_ref[:, :OWN_WIDTH], own_ref[...], preferred_element_type=jnp.float32)
        + jnp.dot(mixed_ref[:, OWN_WIDTH:], other_ref[...], preferred_element_type=jnp.float32)
    ).astype(jnp.bfloat16)


def left_kernel(place_ref, back_ref, own_ref, other_ref, mixed_ref, *out_refs):
    @pl.when(pl.program_id(0) == 0)
    def _():
        combine(place_ref, back_ref, mixed_ref)

    product = times_weights(mixed_ref, own_ref, other_ref)
    for index, out_ref in enumerate(out_refs):
        out_ref[...] = product[2 * index * HALF_ROWS : 2 * (index + 1) * HALF_ROWS]


def right_kernel(mixed_ref, own_ref, other_ref, kept_ref, given_ref):
    product = times_weights(mixed_ref, own_ref, other_ref)
    for index in range(4):
        rows = slice(index * HALF_ROWS, (index + 1) * HALF_ROWS)
        start = 2 * index * HALF_ROWS
        kept_ref[rows, :] = product[start : start + HALF_ROWS]
        given_ref[rows, :] = product[start + HALF_ROWS : start + 2 * HALF_ROWS]


OUT_TILE = 1024
LEFT = 3 * OUT_TILE
RIGHT = MODEL_WIDTH - LEFT
OUT_COST = pl.CostEstimate(
    flops=4 * GROUPS * HALF_ROWS * MODEL_WIDTH * 1024, bytes_accessed=8_000_000, transcendentals=0
)


def left_product(place, back, own_weight, other_weight):
    rows = GROUPS * HALF_ROWS
    return pl.pallas_call(
        left_kernel,
        grid_spec=pltpu.PrefetchScalarGridSpec(
            num_scalar_prefetch=1,
            grid=(LEFT // OUT_TILE,),
            in_specs=[
                pl.BlockSpec((GROUPS, 2, HALF_ROWS, BACK_WIDTH), lambda n, p: (0, 0, 0, 0)),
                pl.BlockSpec((OWN_WIDTH, OUT_TILE), lambda n, p: (0, n)),
                pl.BlockSpec((OWN_WIDTH, OUT_TILE), lambda n, p: (0, n)),
            ],
            out_specs=[pl.BlockSpec((rows, 2 * OWN_WIDTH), lambda n, p: (0, 0))]
            + [pl.BlockSpec((rows // 4, OUT_TILE), lambda n, p: (0, n))] * 4,
        ),
        out_shape=[jax.ShapeDtypeStruct((rows, 2 * OWN_WIDTH), jnp.bfloat16)]
        + [jax.ShapeDtypeStruct((rows // 4, LEFT), jnp.bfloat16)] * 4,
        compiler_params=pltpu.CompilerParams(vmem_limit_bytes=60 * 2**20),
        cost_estimate=OUT_COST,
        name="left_product",
    )(place, back, own_weight, other_weight)


def right_product(mixed, own_weight, other_weight):
    rows = GROUPS * HALF_ROWS
    skip = LEFT // OUT_TILE
    return pl.pallas_call(
        right_kernel,
        grid=(RIGHT // OUT_TILE,),
        in_specs=[
            pl.BlockSpec((rows, 2 * OWN_WIDTH), lambda n: (0, 0)),
            pl.BlockSpec((OWN_WIDTH, OUT_TILE), lambda n: (0, n + skip)),
            pl.BlockSpec((OWN_WIDTH, OUT_TILE), lambda n: (0, n + skip)),
        ],
        out_specs=[pl.BlockSpec((rows // 2, OUT_TILE), lambda n: (0, n))] * 2,
        out_shape=[jax.ShapeDtypeStruct((rows // 2, RIGHT), jnp.bfloat16)] * 2,
        compiler_params=pltpu.CompilerParams(vmem_limit_bytes=60 * 2**20),
        cost_estimate=OUT_COST,
        name="right_product",
    )(mixed, own_weight, other_weight)


def total_of(parts):
    total = parts[0].astype(jnp.float32)
    for part in parts[1:]:
        total = total + part.astype(jnp.float32)
    return total


def along_x(distance):
    return [(shard, shard // 4 * 4 + (shard + distance) % 4) for shard in range(SHARDS)]


def along_y(distance):
    return [(shard, (shard + 4 * distance) % SHARDS) for shard in range(SHARDS)]


def across_groups(bits):
    return [(group, group ^ bits) for group in range(GROUPS)]


def exchange_groups(blocks, group):
    by_core = blocks.reshape((GROUPS // 2, 2) + blocks.shape[1:])
    kept = lax.dynamic_index_in_dim(by_core, group % 2, 1, keepdims=True)
    given = lax.dynamic_index_in_dim(by_core, 1 - group % 2, 1, keepdims=True)
    given = lax.ppermute(given, "grp", across_groups(1))
    both = jnp.concatenate([kept, given], axis=1)
    arrived = []
    for k in range(GROUPS // 2):
        block = lax.dynamic_index_in_dim(both, (group // 2) ^ k, 0, keepdims=False)
        arrived.append(lax.ppermute(block, "grp", across_groups(2 * k)) if k else block)
    return arrived


def swap(block, axes, groups=None):
    return lax.all_to_all(
        block, axes, split_axis=0, concat_axis=0, tiled=True, axis_index_groups=groups
    )


def shards(
    tokens,
    prompt_cache,
    generated_cache,
    suffix_lengths,
    fanout,
    prompt_adapter,
    query_weight,
    key_value_weight,
    output_weight,
    adapter_down_maps,
    adapter_up_maps,
    query_norm_gain,
    key_norm_gain,
):
    group = lax.axis_index("grp")
    shard = lax.axis_index("ad")
    head = shard // 2
    half = shard % 2
    local_table = slot_prompts(fanout, GROUPS, OWNED)

    part_rows = lax.all_gather(tokens, "ad", axis=0, tiled=True)

    slot_suffix = generated_cache.reshape(GROUPS, SLOT_SAMPLES * 16, 2 * HEAD_SIZE)
    slot_lengths = suffix_lengths.reshape(GROUPS, SLOT_SAMPLES, 1).astype(jnp.bfloat16)
    slot_suffix = jnp.concatenate(
        [slot_suffix, jnp.broadcast_to(slot_lengths, (GROUPS, SLOT_SAMPLES, 2 * HEAD_SIZE))], axis=1
    )
    suffix = jnp.concatenate(exchange_groups(slot_suffix, group), axis=0)

    owners = jnp.arange(GROUPS, dtype=jnp.int32)
    local_of_slot = lax.dynamic_index_in_dim(local_table, group, 1, keepdims=False)
    prompts = owners * OWNED + local_of_slot
    hit = prompts[:, None] == jnp.arange(prompt_adapter.shape[0], dtype=jnp.int32)[None, :]
    tasks = jnp.sum(hit.astype(jnp.int32) * prompt_adapter[None, :], axis=1)
    own_rows = tokens.shape[0]
    columns = swap(jnp.swapaxes(tokens.reshape(own_rows, SHARDS, -1), 0, 1), "ad")
    rank_all = jnp.dot(
        columns.reshape(ROWS, -1),
        adapter_down_maps.reshape(-1, ADAPTER_COUNT * ADAPTER_RANK),
        preferred_element_type=jnp.float32,
    ).reshape(GROUPS, SLOT_ROWS, ADAPTER_COUNT, ADAPTER_RANK)
    chosen = (tasks[:, None] == jnp.arange(ADAPTER_COUNT, dtype=jnp.int32)[None, :]).astype(
        jnp.float32
    )
    rank_part = jnp.sum(rank_all * chosen[:, None, :, None], axis=2)
    rank_rows = jnp.sum(swap(rank_part.reshape(SHARDS, own_rows, ADAPTER_RANK), "ad"), axis=0)
    rank_rows = rank_rows.astype(jnp.bfloat16)

    ring = [rank_rows] + [lax.ppermute(rank_rows, "ad", along_x(k)) for k in (1, 2, 3)]
    ring = jnp.stack(ring)

    low_rank = jnp.stack([ring] + [lax.ppermute(ring, "ad", along_y(k)) for k in (1, 2, 3)])
    every = jnp.arange(SHARDS, dtype=jnp.int32)
    spots = ((shard // 4 - every // 4) % 4) * 4 + (shard % 4 - every % 4) % 4

    slice_rows = OWN_WIDTH // GROUPS
    weight_slice = lax.dynamic_slice_in_dim(output_weight, group * slice_rows, slice_rows, 0)
    low_rank, head_pages, weight_slice = lax.optimization_barrier(
        (low_rank, jnp.swapaxes(prompt_cache, 0, 1), weight_slice)
    )
    arrived = swap(head_pages, "ad", ROLE_GROUPS)
    weight_slice = lax.ppermute(weight_slice, "ad", PARTNERS)
    part_rows, weight_slice = lax.optimization_barrier((part_rows, weight_slice))
    other_weight = lax.all_gather(weight_slice, "grp", axis=0, tiled=True)

    steps = jnp.arange(DECODE_STEPS, dtype=jnp.int32)
    position = (PROMPT_TOKENS + suffix_lengths[:, None] + steps[None, :]).astype(jnp.float32)
    cosine, sine = angle_tables(position.reshape(ROWS))
    sent = project(
        tasks,
        spots,
        part_rows,
        query_weight,
        key_value_weight.transpose(1, 2, 0).reshape(HEAD_SIZE, MODEL_WIDTH),
        low_rank.reshape(SHARDS, own_rows, ADAPTER_RANK),
        adapter_up_maps,
        cosine,
        sine,
        query_norm_gain.reshape(1, HEAD_SIZE) * exponent_scale,
    )
    own_sent = exchange_groups(sent, group)
    other_sent = jnp.concatenate([lax.ppermute(part, "ad", PARTNERS) for part in own_sent], axis=0)
    own_sent = jnp.concatenate(own_sent, axis=0)

    local = lax.dynamic_index_in_dim(local_table, group, 0, keepdims=False)
    rank_key = local * GROUPS + owners
    spot = jnp.sum((rank_key[None, :] < rank_key[:, None]).astype(jnp.int32), axis=1)
    placed = (spot[None, :] == owners[:, None]).astype(jnp.int32)
    order = jnp.sum(placed * owners[None, :], axis=1)
    local_sorted = jnp.sum(placed * local[None, :], axis=1)
    flip = (head + group) % 2
    place = jnp.stack([half, flip]).astype(jnp.int32)
    far_lengths = suffix[:, SLOT_SAMPLES * 16 :, 0].astype(jnp.float32)
    far_position = PROMPT_TOKENS + far_lengths[:, :, None] + steps.astype(jnp.float32)
    far_cosine, far_sine = angle_tables(far_position.reshape(GROUPS, SLOT_ROWS))
    partial = attend(
        order,
        local_sorted,
        order ^ group,
        place,
        own_sent,
        other_sent,
        arrived,
        suffix,
        far_cosine,
        far_sine,
        key_norm_gain.reshape(1, HEAD_SIZE),
    )
    back = swap(
        partial.reshape(2 * GROUPS, HALF_ROWS, BACK_WIDTH), ("grp", "ad"), HEAD_GROUPS
    ).reshape(GROUPS, 2, HALF_ROWS, BACK_WIDTH)
    place = jnp.stack([half, shard // 4, head % 2]).astype(jnp.int32)
    mixed, *by_y = left_product(place, back, output_weight, other_weight)
    by_y = by_y[:1] + [lax.ppermute(by_y[k], "ad", along_y(k)) for k in (1, 2, 3)]
    kept, given = right_product(mixed, output_weight, other_weight)
    given = lax.ppermute(given, "ad", ACROSS)
    left = total_of(by_y)
    left_given = lax.ppermute(left[HALF_ROWS:].astype(jnp.bfloat16), "ad", ACROSS)
    right = total_of([kept, given]).reshape(4, HALF_ROWS, RIGHT)
    right_parts = [right[0]] + [
        lax.ppermute(right[k].astype(jnp.bfloat16), "ad", along_y(k)) for k in (1, 2, 3)
    ]
    left = left[:HALF_ROWS] + left_given.astype(jnp.float32)
    right = total_of(right_parts)
    return jnp.concatenate([left.astype(jnp.bfloat16), right.astype(jnp.bfloat16)], axis=1)


def solution(mesh):
    return jax.shard_map(
        shards,
        mesh=mesh,
        in_specs=(
            P(("grp", "ad"), None),
            P("grp", None, "ad", None),
            P("grp", "ad", None),
            P("grp"),
            P(),
            P(),
            P(None, "ad"),
            P(None, None, "ad"),
            P("ad", None),
            P("ad", None, None),
            P(None, None, "ad"),
            P(),
            P(),
        ),
        out_specs=P(("grp", "ad"), None),
        check_vma=False,
    )
```

```python
import functools

import jax
import jax.numpy as jnp
from jax import lax
from jax.experimental import pallas as pl
from jax.experimental.pallas import tpu as pltpu
from jax.sharding import PartitionSpec as P

MODEL_WIDTH = 5120
KEY_VALUE_HEADS = 8
HEAD_SIZE = 128
ADAPTER_RANK = 128
FAN = 2
DECODE_STEPS = 4
ADAPTER_COUNT = 4
PROMPT_TOKENS = 4096
GROUPS = 8
SHARDS = 16
OWNED = 4
SLOT_SAMPLES = 16
SLOT_ROWS = SLOT_SAMPLES * DECODE_STEPS
HALF_ROWS = SLOT_ROWS // 2
ROWS = GROUPS * SLOT_ROWS
OWN_HEADS = 4
PIECES = 4
PIECE = MODEL_WIDTH // PIECES
OWN_WIDTH = OWN_HEADS * HEAD_SIZE
HEAD_FAN = 2 * OWN_HEADS
SENT_WIDTH = OWN_WIDTH + HEAD_SIZE
TILE_HEADS = 4
BACK_WIDTH = HEAD_FAN * HEAD_SIZE + HEAD_SIZE

theta_base = 1000000.0
norm_eps = 1e-06
masked_low = -1e30
exponent_scale = HEAD_SIZE**-0.5 * 1.4426950408889634

ROLE_GROUPS = [[0, 3, 4, 7, 8, 11, 12, 15], [1, 2, 5, 6, 9, 10, 13, 14]]
HEAD_GROUPS = [
    [group * SHARDS + 2 * head + half for group in range(GROUPS) for half in range(2)]
    for head in range(KEY_VALUE_HEADS)
]
ACROSS = [(shard, shard // 4 * 4 + 3 - shard % 4) for shard in range(SHARDS)]
PARTNERS = [(shard, shard ^ 1) for shard in range(SHARDS)]


def slot_prompts(fanout, groups, owned_count):
    listed = jnp.any(
        fanout[:, :, None] == jnp.arange(groups, dtype=jnp.int32)[None, None, :], axis=1
    )
    listed = listed.astype(jnp.int32).reshape(groups, owned_count, groups)
    return jnp.sum(listed * jnp.arange(owned_count, dtype=jnp.int32)[None, :, None], axis=1)


def angle_tables(position):
    half_len = HEAD_SIZE // 2
    inverse = theta_base ** (-2.0 * jnp.arange(half_len, dtype=jnp.float32) / HEAD_SIZE)
    angles = position[..., None] * inverse
    cosine = jnp.cos(angles)
    sine = jnp.sin(angles)
    return (
        jnp.concatenate([cosine, cosine], axis=-1),
        jnp.concatenate([-sine, sine], axis=-1),
    )


def norm_rotate(vector, gain, cosine, sine):
    mean_sq = jnp.mean(vector * vector, axis=-1, keepdims=True)
    scaled = vector * lax.rsqrt(mean_sq + norm_eps) * gain
    return scaled * cosine + pltpu.roll(scaled, HEAD_SIZE // 2, 1) * sine


def dot_nt(left, right):
    return lax.dot_general(
        left, right, (((1,), (1,)), ((), ())), preferred_element_type=jnp.float32
    )


def project_kernel(
    task_ref,
    spot_ref,
    tokens_ref,
    query_ref,
    keyval_ref,
    rank_ref,
    up_ref,
    cos_ref,
    sin_ref,
    gain_ref,
    out_ref,
    tokens,
    query_weight,
    keyval_weight,
    query_sum,
    keyval_sum,
    sems,
):
    copies = []
    for piece in range(PIECES):
        span = pl.ds(piece * PIECE, PIECE)
        copies.append(
            [
                pltpu.make_async_copy(
                    tokens_ref.at[:, span], tokens.at[:, span], sems.at[0, piece]
                ),
                pltpu.make_async_copy(
                    query_ref.at[span, :], query_weight.at[span, :], sems.at[1, piece]
                ),
                pltpu.make_async_copy(
                    keyval_ref.at[:, span], keyval_weight.at[:, span], sems.at[2, piece]
                ),
            ]
        )
        for copy in copies[-1]:
            copy.start()
    for piece in range(PIECES):
        for copy in copies[piece]:
            copy.wait()
        span = slice(piece * PIECE, (piece + 1) * PIECE)
        part = tokens[:, span]
        query = jnp.dot(part, query_weight[span, :], preferred_element_type=jnp.float32)
        keyval = dot_nt(part, keyval_weight[:, span])
        query_sum[...] = query if piece == 0 else query_sum[...] + query
        keyval_sum[...] = keyval if piece == 0 else keyval_sum[...] + keyval

    for slot in range(GROUPS):
        rows = slice(slot * SLOT_ROWS, (slot + 1) * SLOT_ROWS)
        low_rank = jnp.concatenate(
            [rank_ref[spot_ref[2 * slot]], rank_ref[spot_ref[2 * slot + 1]]], axis=0
        )
        query = query_sum[rows, :] + jnp.dot(
            low_rank, up_ref[task_ref[slot]], preferred_element_type=jnp.float32
        )
        for head in range(OWN_HEADS):
            lanes = slice(head * HEAD_SIZE, (head + 1) * HEAD_SIZE)
            turned = norm_rotate(
                query[:, lanes], gain_ref[...], cos_ref[rows, :], sin_ref[rows, :]
            ).astype(jnp.bfloat16)
            out_ref[slot, :, lanes] = turned
        out_ref[slot, :, OWN_WIDTH:] = keyval_sum[rows, :].astype(jnp.bfloat16)


def project(tasks, spots, tokens, query_weight, keyval_weight, low_rank, up_maps, cosine, sine, gain):
    whole = lambda *shape: pl.BlockSpec(shape, lambda k, t, s: (0,) * len(shape))
    return pl.pallas_call(
        project_kernel,
        grid_spec=pltpu.PrefetchScalarGridSpec(
            num_scalar_prefetch=2,
            grid=(1,),
            in_specs=[pl.BlockSpec(memory_space=pl.ANY)] * 3
            + [
                whole(SHARDS, HALF_ROWS, ADAPTER_RANK),
                whole(ADAPTER_COUNT, ADAPTER_RANK, OWN_WIDTH),
                whole(ROWS, HEAD_SIZE),
                whole(ROWS, HEAD_SIZE),
                whole(1, HEAD_SIZE),
            ],
            out_specs=whole(GROUPS, SLOT_ROWS, SENT_WIDTH),
            scratch_shapes=[
                pltpu.VMEM((ROWS, MODEL_WIDTH), jnp.bfloat16),
                pltpu.VMEM((MODEL_WIDTH, OWN_WIDTH), jnp.bfloat16),
                pltpu.VMEM((HEAD_SIZE, MODEL_WIDTH), jnp.bfloat16),
                pltpu.VMEM((ROWS, OWN_WIDTH), jnp.float32),
                pltpu.VMEM((ROWS, HEAD_SIZE), jnp.float32),
                pltpu.SemaphoreType.DMA((3, PIECES)),
            ],
        ),
        out_shape=jax.ShapeDtypeStruct((GROUPS, SLOT_ROWS, SENT_WIDTH), jnp.bfloat16),
        compiler_params=pltpu.CompilerParams(vmem_limit_bytes=60 * 2**20),
        cost_estimate=pl.CostEstimate(
            flops=20 * ROWS * MODEL_WIDTH * SENT_WIDTH, bytes_accessed=13_000_000, transcendentals=0
        ),
        name="project",
    )(tasks, spots, tokens, query_weight, keyval_weight, low_rank, up_maps, cosine, sine, gain)


def attend_kernel(
    order_ref,
    local_ref,
    reach_ref,
    place_ref,
    own_ref,
    other_ref,
    page_ref,
    suffix_ref,
    cos_ref,
    sin_ref,
    gain_ref,
    out_ref,
):
    half = place_ref[0]
    flip = place_ref[1]
    span = GROUPS * PROMPT_TOKENS // SHARDS
    pages = page_ref[...].reshape(span, 2 * HEAD_SIZE)
    keys = pages[:, :HEAD_SIZE]
    values = jnp.concatenate(
        [jnp.ones((span, HEAD_SIZE), jnp.bfloat16), pages[:, HEAD_SIZE:]], axis=1
    )
    first_sent = jnp.where(half == 0, own_ref[0], other_ref[0])
    second_sent = jnp.where(half == 0, other_ref[0], own_ref[0])
    low_part = first_sent[:, OWN_WIDTH:].astype(jnp.float32)
    high_part = second_sent[:, OWN_WIDTH:].astype(jnp.float32)
    lane = lax.broadcasted_iota(jnp.int32, (SLOT_ROWS, HEAD_SIZE), 1)
    low_lanes = lane < HEAD_SIZE // 2
    new_keys = jnp.where(low_lanes, low_part, pltpu.roll(high_part, HEAD_SIZE // 2, 1))
    new_values = jnp.where(low_lanes, pltpu.roll(low_part, HEAD_SIZE // 2, 1), high_part)
    new_keys = norm_rotate(new_keys, gain_ref[...], cos_ref[0], sin_ref[0])
    suffix_rows = SLOT_SAMPLES * 16
    extra = suffix_rows + 2 * SLOT_ROWS
    suffix = suffix_ref[0, :suffix_rows, :]
    zeros = jnp.zeros((SLOT_ROWS, HEAD_SIZE), jnp.bfloat16)
    extra_keys = jnp.concatenate(
        [suffix[:, :HEAD_SIZE], new_keys.astype(jnp.bfloat16), zeros], axis=0
    )
    extra_values = jnp.concatenate(
        [suffix[:, HEAD_SIZE:], new_values.astype(jnp.bfloat16), zeros], axis=0
    )
    extra_values = jnp.concatenate(
        [jnp.ones((extra, HEAD_SIZE), jnp.bfloat16), extra_values], axis=1
    )
    lengths = suffix_ref[0, suffix_rows:, :].astype(jnp.float32)
    sample_of = lax.broadcasted_iota(jnp.int32, (SLOT_SAMPLES, suffix_rows), 0)
    column_sample = lax.broadcasted_iota(jnp.int32, (SLOT_SAMPLES, suffix_rows), 1) // 16
    column_length = jnp.sum(
        jnp.where(sample_of == column_sample, lengths, 0.0), axis=0, keepdims=True
    )
    row = lax.broadcasted_iota(jnp.int32, (SLOT_ROWS, suffix_rows), 0)
    column = lax.broadcasted_iota(jnp.int32, (SLOT_ROWS, suffix_rows), 1)
    suffix_seen = (row // DECODE_STEPS == column // 16) & (
        (half * 16 + column % 16).astype(jnp.float32) < column_length
    )
    row = lax.broadcasted_iota(jnp.int32, (SLOT_ROWS, 2 * SLOT_ROWS), 0)
    column = lax.broadcasted_iota(jnp.int32, (SLOT_ROWS, 2 * SLOT_ROWS), 1)
    new_seen = (
        (row // DECODE_STEPS == column // DECODE_STEPS)
        & (column % DECODE_STEPS <= row % DECODE_STEPS)
        & (column // HALF_ROWS == half)
    )
    bias = jnp.concatenate(
        [jnp.where(suffix_seen, 0.0, masked_low), jnp.where(new_seen, 0.0, masked_low)], axis=1
    )
    bias = jnp.concatenate([bias] * TILE_HEADS, axis=0)
    logs = jnp.zeros((SLOT_ROWS, HEAD_SIZE), jnp.float32)

    def finish(first, total, peak):
        nonlocal logs
        denominator = total[:, :HEAD_SIZE]
        attended = (total[:, HEAD_SIZE:] / denominator).astype(jnp.bfloat16)
        log_sum = peak + jnp.log2(denominator)
        for index in range(TILE_HEADS):
            head = first + index
            rows = slice(index * SLOT_ROWS, (index + 1) * SLOT_ROWS)
            top = attended[rows][:HALF_ROWS]
            low = attended[rows][HALF_ROWS:]
            lanes = slice(head * HEAD_SIZE, (head + 1) * HEAD_SIZE)
            out_ref[0, 0, :, lanes] = jnp.where(flip == 0, top, low)
            out_ref[0, 1, :, lanes] = jnp.where(flip == 0, low, top)
            logs = jnp.where(lane == head, log_sum[rows], logs)

    def query_of(first):
        query = []
        for head in range(first, first + TILE_HEADS):
            source, start = divmod(head, OWN_HEADS)
            sent = second_sent if source else first_sent
            query.append(sent[:, start * HEAD_SIZE : (start + 1) * HEAD_SIZE])
        return jnp.concatenate(query, axis=0)


    def scores(first):
        query = query_of(first)
        return dot_nt(query, keys), dot_nt(query, extra_keys) + bias

    tiles = list(range(0, HEAD_FAN, TILE_HEADS))
    ready = scores(tiles[0])
    for number, first in enumerate(tiles):
        prefix_score, extra_score = ready
        if number + 1 < len(tiles):
            ready = scores(tiles[number + 1])
        peak = jnp.maximum(
            jnp.max(prefix_score, axis=-1, keepdims=True),
            jnp.max(extra_score, axis=-1, keepdims=True),
        )
        prefix_weight = jnp.exp2(prefix_score - peak).astype(jnp.bfloat16)
        extra_weight = jnp.exp2(extra_score - peak).astype(jnp.bfloat16)
        total = jnp.dot(prefix_weight, values, preferred_element_type=jnp.float32) + jnp.dot(
            extra_weight, extra_values, preferred_element_type=jnp.float32
        )
        finish(first, total, peak)
    high_term = logs.astype(jnp.bfloat16).astype(jnp.float32)
    rest = logs - high_term
    mid_term = rest.astype(jnp.bfloat16).astype(jnp.float32)
    low_term = rest - mid_term
    packed = (
        high_term + pltpu.roll(mid_term, HEAD_FAN, 1) + pltpu.roll(low_term, 2 * HEAD_FAN, 1)
    ).astype(jnp.bfloat16)
    top = packed[:HALF_ROWS]
    low = packed[HALF_ROWS:]
    out_ref[0, 0, :, HEAD_FAN * HEAD_SIZE :] = jnp.where(flip == 0, top, low)
    out_ref[0, 1, :, HEAD_FAN * HEAD_SIZE :] = jnp.where(flip == 0, low, top)


def attend(order, local, reach, place, own, other, pages, suffix, cosine, sine, gain):
    block = PROMPT_TOKENS // SHARDS
    return pl.pallas_call(
        attend_kernel,
        grid_spec=pltpu.PrefetchScalarGridSpec(
            num_scalar_prefetch=4,
            grid=(GROUPS,),
            in_specs=[
                pl.BlockSpec((1, SLOT_ROWS, SENT_WIDTH), lambda i, o, l, r, p: (r[i], 0, 0)),
                pl.BlockSpec((1, SLOT_ROWS, SENT_WIDTH), lambda i, o, l, r, p: (r[i], 0, 0)),
                pl.BlockSpec(
                    (GROUPS, 1, block, 2 * HEAD_SIZE), lambda i, o, l, r, p: (0, l[i], 0, 0)
                ),
                pl.BlockSpec(
                    (1, suffix.shape[1], 2 * HEAD_SIZE), lambda i, o, l, r, p: (r[i], 0, 0)
                ),
                pl.BlockSpec((1, SLOT_ROWS, HEAD_SIZE), lambda i, o, l, r, p: (r[i], 0, 0)),
                pl.BlockSpec((1, SLOT_ROWS, HEAD_SIZE), lambda i, o, l, r, p: (r[i], 0, 0)),
                pl.BlockSpec((1, HEAD_SIZE), lambda i, o, l, r, p: (0, 0)),
            ],
            out_specs=pl.BlockSpec(
                (1, 2, HALF_ROWS, BACK_WIDTH), lambda i, o, l, r, p: (o[i], 0, 0, 0)
            ),
        ),
        out_shape=jax.ShapeDtypeStruct((GROUPS, 2, HALF_ROWS, BACK_WIDTH), jnp.bfloat16),
        compiler_params=pltpu.CompilerParams(vmem_limit_bytes=30 * 2**20),
        cost_estimate=pl.CostEstimate(
            flops=20 * GROUPS * 512 * 2432 * 384,
            bytes_accessed=8_000_000,
            transcendentals=GROUPS * 512 * 2432,
        ),
        name="attend",
    )(order, local, reach, place, own, other, pages, suffix, cosine, sine, gain)


def combine(place_ref, back_ref, mixed_ref):
    half = place_ref[0]
    rows = GROUPS * HALF_ROWS
    slots = [
        (place_ref[1] + index // 2) % 4 * 2 + (place_ref[2] ^ (index % 2))
        for index in range(GROUPS)
    ]

    def part_of(source, lanes):
        parts = [back_ref[slot, source, :, lanes] for slot in slots]
        return jnp.concatenate(parts, axis=0).astype(jnp.float32)

    def log_of(source):
        packed = part_of(source, slice(HEAD_FAN * HEAD_SIZE, BACK_WIDTH))
        return (
            packed
            + pltpu.roll(packed, HEAD_SIZE - HEAD_FAN, 1)
            + pltpu.roll(packed, HEAD_SIZE - 2 * HEAD_FAN, 1)
        )

    first_log = log_of(0)
    second_log = log_of(1)
    peak = jnp.maximum(first_log, second_log)
    first_part = jnp.exp2(first_log - peak)
    second_part = jnp.exp2(second_log - peak)
    both = first_part + second_part
    first_part = first_part / both
    second_part = second_part / both

    def attended(head):
        lanes = slice(head * HEAD_SIZE, (head + 1) * HEAD_SIZE)
        return (
            part_of(0, lanes) * first_part[:, head : head + 1]
            + part_of(1, lanes) * second_part[:, head : head + 1]
        ).astype(jnp.bfloat16)

    for head in range(OWN_HEADS):
        low = attended(head)
        high = attended(head + OWN_HEADS)
        lanes = slice(head * HEAD_SIZE, (head + 1) * HEAD_SIZE)
        mixed_ref[:, lanes] = jnp.where(half == 0, low, high)
        lanes = slice((head + OWN_HEADS) * HEAD_SIZE, (head + OWN_HEADS + 1) * HEAD_SIZE)
        mixed_ref[:, lanes] = jnp.where(half == 0, high, low)


def times_weights(mixed_ref, own_ref, other_ref):
    return (
        jnp.dot(mixed_ref[:, :OWN_WIDTH], own_ref[...], preferred_element_type=jnp.float32)
        + jnp.dot(mixed_ref[:, OWN_WIDTH:], other_ref[...], preferred_element_type=jnp.float32)
    ).astype(jnp.bfloat16)


def left_kernel(place_ref, back_ref, own_ref, other_ref, mixed_ref, *out_refs):
    @pl.when(pl.program_id(0) == 0)
    def _():
        combine(place_ref, back_ref, mixed_ref)

    product = times_weights(mixed_ref, own_ref, other_ref)
    for index, out_ref in enumerate(out_refs):
        out_ref[...] = product[2 * index * HALF_ROWS : 2 * (index + 1) * HALF_ROWS]


def right_kernel(mixed_ref, own_ref, other_ref, kept_ref, given_ref):
    product = times_weights(mixed_ref, own_ref, other_ref)
    for index in range(4):
        rows = slice(index * HALF_ROWS, (index + 1) * HALF_ROWS)
        start = 2 * index * HALF_ROWS
        kept_ref[rows, :] = product[start : start + HALF_ROWS]
        given_ref[rows, :] = product[start + HALF_ROWS : start + 2 * HALF_ROWS]


OUT_TILE = 1024
LEFT = 3 * OUT_TILE
RIGHT = MODEL_WIDTH - LEFT
OUT_COST = pl.CostEstimate(
    flops=4 * GROUPS * HALF_ROWS * MODEL_WIDTH * 1024, bytes_accessed=8_000_000, transcendentals=0
)


def left_product(place, back, own_weight, other_weight):
    rows = GROUPS * HALF_ROWS
    return pl.pallas_call(
        left_kernel,
        grid_spec=pltpu.PrefetchScalarGridSpec(
            num_scalar_prefetch=1,
            grid=(LEFT // OUT_TILE,),
            in_specs=[
                pl.BlockSpec((GROUPS, 2, HALF_ROWS, BACK_WIDTH), lambda n, p: (0, 0, 0, 0)),
                pl.BlockSpec((OWN_WIDTH, OUT_TILE), lambda n, p: (0, n)),
                pl.BlockSpec((OWN_WIDTH, OUT_TILE), lambda n, p: (0, n)),
            ],
            out_specs=[pl.BlockSpec((rows, 2 * OWN_WIDTH), lambda n, p: (0, 0))]
            + [pl.BlockSpec((rows // 4, OUT_TILE), lambda n, p: (0, n))] * 4,
        ),
        out_shape=[jax.ShapeDtypeStruct((rows, 2 * OWN_WIDTH), jnp.bfloat16)]
        + [jax.ShapeDtypeStruct((rows // 4, LEFT), jnp.bfloat16)] * 4,
        compiler_params=pltpu.CompilerParams(vmem_limit_bytes=60 * 2**20),
        cost_estimate=OUT_COST,
        name="left_product",
    )(place, back, own_weight, other_weight)


def right_product(mixed, own_weight, other_weight):
    rows = GROUPS * HALF_ROWS
    skip = LEFT // OUT_TILE
    return pl.pallas_call(
        right_kernel,
        grid=(RIGHT // OUT_TILE,),
        in_specs=[
            pl.BlockSpec((rows, 2 * OWN_WIDTH), lambda n: (0, 0)),
            pl.BlockSpec((OWN_WIDTH, OUT_TILE), lambda n: (0, n + skip)),
            pl.BlockSpec((OWN_WIDTH, OUT_TILE), lambda n: (0, n + skip)),
        ],
        out_specs=[pl.BlockSpec((rows // 2, OUT_TILE), lambda n: (0, n))] * 2,
        out_shape=[jax.ShapeDtypeStruct((rows // 2, RIGHT), jnp.bfloat16)] * 2,
        compiler_params=pltpu.CompilerParams(vmem_limit_bytes=60 * 2**20),
        cost_estimate=OUT_COST,
        name="right_product",
    )(mixed, own_weight, other_weight)


def total_of(parts):
    total = parts[0].astype(jnp.float32)
    for part in parts[1:]:
        total = total + part.astype(jnp.float32)
    return total


def along_x(distance):
    return [(shard, shard // 4 * 4 + (shard + distance) % 4) for shard in range(SHARDS)]


def along_y(distance):
    return [(shard, (shard + 4 * distance) % SHARDS) for shard in range(SHARDS)]


def across_groups(bits):
    return [(group, group ^ bits) for group in range(GROUPS)]


def exchange_groups(blocks, group):
    by_core = blocks.reshape((GROUPS // 2, 2) + blocks.shape[1:])
    kept = lax.dynamic_index_in_dim(by_core, group % 2, 1, keepdims=True)
    given = lax.dynamic_index_in_dim(by_core, 1 - group % 2, 1, keepdims=True)
    given = lax.ppermute(given, "grp", across_groups(1))
    both = jnp.concatenate([kept, given], axis=1)
    arrived = []
    for k in range(GROUPS // 2):
        block = lax.dynamic_index_in_dim(both, (group // 2) ^ k, 0, keepdims=False)
        arrived.append(lax.ppermute(block, "grp", across_groups(2 * k)) if k else block)
    return arrived


def swap(block, axes, groups=None):
    return lax.all_to_all(
        block, axes, split_axis=0, concat_axis=0, tiled=True, axis_index_groups=groups
    )


def shards(
    tokens,
    prompt_cache,
    generated_cache,
    suffix_lengths,
    fanout,
    prompt_adapter,
    query_weight,
    key_value_weight,
    output_weight,
    adapter_down_maps,
    adapter_up_maps,
    query_norm_gain,
    key_norm_gain,
):
    group = lax.axis_index("grp")
    shard = lax.axis_index("ad")
    head = shard // 2
    half = shard % 2
    local_table = slot_prompts(fanout, GROUPS, OWNED)

    part_rows = lax.all_gather(tokens, "ad", axis=0, tiled=True)

    slot_suffix = generated_cache.reshape(GROUPS, SLOT_SAMPLES * 16, 2 * HEAD_SIZE)
    slot_lengths = suffix_lengths.reshape(GROUPS, SLOT_SAMPLES, 1).astype(jnp.bfloat16)
    slot_suffix = jnp.concatenate(
        [slot_suffix, jnp.broadcast_to(slot_lengths, (GROUPS, SLOT_SAMPLES, 2 * HEAD_SIZE))], axis=1
    )
    suffix = jnp.concatenate(exchange_groups(slot_suffix, group), axis=0)

    owners = jnp.arange(GROUPS, dtype=jnp.int32)
    local_of_slot = lax.dynamic_index_in_dim(local_table, group, 1, keepdims=False)
    prompts = owners * OWNED + local_of_slot
    hit = prompts[:, None] == jnp.arange(prompt_adapter.shape[0], dtype=jnp.int32)[None, :]
    tasks = jnp.sum(hit.astype(jnp.int32) * prompt_adapter[None, :], axis=1)
    own_rows = tokens.shape[0]
    columns = swap(jnp.swapaxes(tokens.reshape(own_rows, SHARDS, -1), 0, 1), "ad")
    rank_all = jnp.dot(
        columns.reshape(ROWS, -1),
        adapter_down_maps.reshape(-1, ADAPTER_COUNT * ADAPTER_RANK),
        preferred_element_type=jnp.float32,
    ).reshape(GROUPS, SLOT_ROWS, ADAPTER_COUNT, ADAPTER_RANK)
    chosen = (tasks[:, None] == jnp.arange(ADAPTER_COUNT, dtype=jnp.int32)[None, :]).astype(
        jnp.float32
    )
    rank_part = jnp.sum(rank_all * chosen[:, None, :, None], axis=2)
    rank_rows = jnp.sum(swap(rank_part.reshape(SHARDS, own_rows, ADAPTER_RANK), "ad"), axis=0)
    rank_rows = rank_rows.astype(jnp.bfloat16)

    ring = [rank_rows] + [lax.ppermute(rank_rows, "ad", along_x(k)) for k in (1, 2, 3)]
    ring = jnp.stack(ring)

    low_rank = jnp.stack([ring] + [lax.ppermute(ring, "ad", along_y(k)) for k in (1, 2, 3)])
    every = jnp.arange(SHARDS, dtype=jnp.int32)
    spots = ((shard // 4 - every // 4) % 4) * 4 + (shard % 4 - every % 4) % 4

    slice_rows = OWN_WIDTH // GROUPS
    weight_slice = lax.dynamic_slice_in_dim(output_weight, group * slice_rows, slice_rows, 0)
    low_rank, head_pages, weight_slice = lax.optimization_barrier(
        (low_rank, jnp.swapaxes(prompt_cache, 0, 1), weight_slice)
    )
    arrived = swap(head_pages, "ad", ROLE_GROUPS)
    weight_slice = lax.ppermute(weight_slice, "ad", PARTNERS)
    part_rows, weight_slice = lax.optimization_barrier((part_rows, weight_slice))
    other_weight = lax.all_gather(weight_slice, "grp", axis=0, tiled=True)

    steps = jnp.arange(DECODE_STEPS, dtype=jnp.int32)
    position = (PROMPT_TOKENS + suffix_lengths[:, None] + steps[None, :]).astype(jnp.float32)
    cosine, sine = angle_tables(position.reshape(ROWS))
    sent = project(
        tasks,
        spots,
        part_rows,
        query_weight,
        key_value_weight.transpose(1, 2, 0).reshape(HEAD_SIZE, MODEL_WIDTH),
        low_rank.reshape(SHARDS, own_rows, ADAPTER_RANK),
        adapter_up_maps,
        cosine,
        sine,
        query_norm_gain.reshape(1, HEAD_SIZE) * exponent_scale,
    )
    own_sent = exchange_groups(sent, group)
    other_sent = jnp.concatenate([lax.ppermute(part, "ad", PARTNERS) for part in own_sent], axis=0)
    own_sent = jnp.concatenate(own_sent, axis=0)

    local = lax.dynamic_index_in_dim(local_table, group, 0, keepdims=False)
    rank_key = local * GROUPS + owners
    spot = jnp.sum((rank_key[None, :] < rank_key[:, None]).astype(jnp.int32), axis=1)
    placed = (spot[None, :] == owners[:, None]).astype(jnp.int32)
    order = jnp.sum(placed * owners[None, :], axis=1)
    local_sorted = jnp.sum(placed * local[None, :], axis=1)
    flip = (head + group) % 2
    place = jnp.stack([half, flip]).astype(jnp.int32)
    far_lengths = suffix[:, SLOT_SAMPLES * 16 :, 0].astype(jnp.float32)
    far_position = PROMPT_TOKENS + far_lengths[:, :, None] + steps.astype(jnp.float32)
    far_cosine, far_sine = angle_tables(far_position.reshape(GROUPS, SLOT_ROWS))
    partial = attend(
        order,
        local_sorted,
        order ^ group,
        place,
        own_sent,
        other_sent,
        arrived,
        suffix,
        far_cosine,
        far_sine,
        key_norm_gain.reshape(1, HEAD_SIZE),
    )
    back = swap(
        partial.reshape(2 * GROUPS, HALF_ROWS, BACK_WIDTH), ("grp", "ad"), HEAD_GROUPS
    ).reshape(GROUPS, 2, HALF_ROWS, BACK_WIDTH)
    place = jnp.stack([half, shard // 4, head % 2]).astype(jnp.int32)
    mixed, *by_y = left_product(place, back, output_weight, other_weight)
    by_y = by_y[:1] + [lax.ppermute(by_y[k], "ad", along_y(k)) for k in (1, 2, 3)]
    kept, given = right_product(mixed, output_weight, other_weight)
    given = lax.ppermute(given, "ad", ACROSS)
    left = total_of(by_y)
    left_given = lax.ppermute(left[HALF_ROWS:].astype(jnp.bfloat16), "ad", ACROSS)
    right = total_of([kept, given]).reshape(4, HALF_ROWS, RIGHT)
    right_parts = [right[0]] + [
        lax.ppermute(right[k].astype(jnp.bfloat16), "ad", along_y(k)) for k in (1, 2, 3)
    ]
    left = left[:HALF_ROWS] + left_given.astype(jnp.float32)
    right = total_of(right_parts)
    return jnp.concatenate([left.astype(jnp.bfloat16), right.astype(jnp.bfloat16)], axis=1)


def solution(mesh):
    return jax.shard_map(
        shards,
        mesh=mesh,
        in_specs=(
            P(("grp", "ad"), None),
            P("grp", None, "ad", None),
            P("grp", "ad", None),
            P("grp"),
            P(),
            P(),
            P(None, "ad"),
            P(None, None, "ad"),
            P("ad", None),
            P("ad", None, None),
            P(None, None, "ad"),
            P(),
            P(),
        ),
        out_specs=P(("grp", "ad"), None),
        check_vma=False,
    )
```

```python
import functools

import jax
import jax.numpy as jnp
from jax import lax
from jax.experimental import pallas as pl
from jax.experimental.pallas import tpu as pltpu
from jax.sharding import PartitionSpec as P

MODEL_WIDTH = 5120
KEY_VALUE_HEADS = 8
HEAD_SIZE = 128
ADAPTER_RANK = 128
FAN = 2
DECODE_STEPS = 4
ADAPTER_COUNT = 4
PROMPT_TOKENS = 4096
GROUPS = 8
SHARDS = 16
OWNED = 4
SLOT_SAMPLES = 16
SLOT_ROWS = SLOT_SAMPLES * DECODE_STEPS
HALF_ROWS = SLOT_ROWS // 2
ROWS = GROUPS * SLOT_ROWS
OWN_HEADS = 4
PIECES = 4
PIECE = MODEL_WIDTH // PIECES
OWN_WIDTH = OWN_HEADS * HEAD_SIZE
HEAD_FAN = 2 * OWN_HEADS
SENT_WIDTH = OWN_WIDTH + HEAD_SIZE
TILE_HEADS = 4
BACK_WIDTH = HEAD_FAN * HEAD_SIZE + HEAD_SIZE

theta_base = 1000000.0
norm_eps = 1e-06
masked_low = -1e30
exponent_scale = HEAD_SIZE**-0.5 * 1.4426950408889634

ROLE_GROUPS = [[0, 3, 4, 7, 8, 11, 12, 15], [1, 2, 5, 6, 9, 10, 13, 14]]
HEAD_GROUPS = [
    [group * SHARDS + 2 * head + half for group in range(GROUPS) for half in range(2)]
    for head in range(KEY_VALUE_HEADS)
]
ACROSS = [(shard, shard // 4 * 4 + 3 - shard % 4) for shard in range(SHARDS)]
PARTNERS = [(shard, shard ^ 1) for shard in range(SHARDS)]


def slot_prompts(fanout, groups, owned_count):
    listed = jnp.any(
        fanout[:, :, None] == jnp.arange(groups, dtype=jnp.int32)[None, None, :], axis=1
    )
    listed = listed.astype(jnp.int32).reshape(groups, owned_count, groups)
    return jnp.sum(listed * jnp.arange(owned_count, dtype=jnp.int32)[None, :, None], axis=1)


def angle_tables(position):
    half_len = HEAD_SIZE // 2
    inverse = theta_base ** (-2.0 * jnp.arange(half_len, dtype=jnp.float32) / HEAD_SIZE)
    angles = position[..., None] * inverse
    cosine = jnp.cos(angles)
    sine = jnp.sin(angles)
    return (
        jnp.concatenate([cosine, cosine], axis=-1),
        jnp.concatenate([-sine, sine], axis=-1),
    )


def norm_rotate(vector, gain, cosine, sine):
    mean_sq = jnp.mean(vector * vector, axis=-1, keepdims=True)
    scaled = vector * lax.rsqrt(mean_sq + norm_eps) * gain
    return scaled * cosine + pltpu.roll(scaled, HEAD_SIZE // 2, 1) * sine


def dot_nt(left, right):
    return lax.dot_general(
        left, right, (((1,), (1,)), ((), ())), preferred_element_type=jnp.float32
    )


def project_kernel(
    task_ref,
    spot_ref,
    tokens_ref,
    query_ref,
    keyval_ref,
    rank_ref,
    up_ref,
    cos_ref,
    sin_ref,
    gain_ref,
    out_ref,
    tokens,
    query_weight,
    keyval_weight,
    query_sum,
    keyval_sum,
    sems,
):
    copies = []
    for piece in range(PIECES):
        span = pl.ds(piece * PIECE, PIECE)
        copies.append(
            [
                pltpu.make_async_copy(
                    tokens_ref.at[:, span], tokens.at[:, span], sems.at[0, piece]
                ),
                pltpu.make_async_copy(
                    query_ref.at[span, :], query_weight.at[span, :], sems.at[1, piece]
                ),
                pltpu.make_async_copy(
                    keyval_ref.at[:, span], keyval_weight.at[:, span], sems.at[2, piece]
                ),
            ]
        )
        for copy in copies[-1]:
            copy.start()
    for piece in range(PIECES):
        for copy in copies[piece]:
            copy.wait()
        span = slice(piece * PIECE, (piece + 1) * PIECE)
        part = tokens[:, span]
        query = jnp.dot(part, query_weight[span, :], preferred_element_type=jnp.float32)
        keyval = dot_nt(part, keyval_weight[:, span])
        query_sum[...] = query if piece == 0 else query_sum[...] + query
        keyval_sum[...] = keyval if piece == 0 else keyval_sum[...] + keyval

    for slot in range(GROUPS):
        rows = slice(slot * SLOT_ROWS, (slot + 1) * SLOT_ROWS)
        low_rank = jnp.concatenate(
            [rank_ref[spot_ref[2 * slot]], rank_ref[spot_ref[2 * slot + 1]]], axis=0
        )
        query = query_sum[rows, :] + jnp.dot(
            low_rank, up_ref[task_ref[slot]], preferred_element_type=jnp.float32
        )
        for head in range(OWN_HEADS):
            lanes = slice(head * HEAD_SIZE, (head + 1) * HEAD_SIZE)
            turned = norm_rotate(
                query[:, lanes], gain_ref[...], cos_ref[rows, :], sin_ref[rows, :]
            ).astype(jnp.bfloat16)
            out_ref[slot, :, lanes] = turned
        out_ref[slot, :, OWN_WIDTH:] = keyval_sum[rows, :].astype(jnp.bfloat16)


def project(tasks, spots, tokens, query_weight, keyval_weight, low_rank, up_maps, cosine, sine, gain):
    whole = lambda *shape: pl.BlockSpec(shape, lambda k, t, s: (0,) * len(shape))
    return pl.pallas_call(
        project_kernel,
        grid_spec=pltpu.PrefetchScalarGridSpec(
            num_scalar_prefetch=2,
            grid=(1,),
            in_specs=[pl.BlockSpec(memory_space=pl.ANY)] * 3
            + [
                whole(SHARDS, HALF_ROWS, ADAPTER_RANK),
                whole(ADAPTER_COUNT, ADAPTER_RANK, OWN_WIDTH),
                whole(ROWS, HEAD_SIZE),
                whole(ROWS, HEAD_SIZE),
                whole(1, HEAD_SIZE),
            ],
            out_specs=whole(GROUPS, SLOT_ROWS, SENT_WIDTH),
            scratch_shapes=[
                pltpu.VMEM((ROWS, MODEL_WIDTH), jnp.bfloat16),
                pltpu.VMEM((MODEL_WIDTH, OWN_WIDTH), jnp.bfloat16),
                pltpu.VMEM((HEAD_SIZE, MODEL_WIDTH), jnp.bfloat16),
                pltpu.VMEM((ROWS, OWN_WIDTH), jnp.float32),
                pltpu.VMEM((ROWS, HEAD_SIZE), jnp.float32),
                pltpu.SemaphoreType.DMA((3, PIECES)),
            ],
        ),
        out_shape=jax.ShapeDtypeStruct((GROUPS, SLOT_ROWS, SENT_WIDTH), jnp.bfloat16),
        compiler_params=pltpu.CompilerParams(vmem_limit_bytes=60 * 2**20),
        cost_estimate=pl.CostEstimate(
            flops=20 * ROWS * MODEL_WIDTH * SENT_WIDTH, bytes_accessed=13_000_000, transcendentals=0
        ),
        name="project",
    )(tasks, spots, tokens, query_weight, keyval_weight, low_rank, up_maps, cosine, sine, gain)


def attend_kernel(
    order_ref,
    local_ref,
    reach_ref,
    place_ref,
    own_ref,
    other_ref,
    page_ref,
    suffix_ref,
    cos_ref,
    sin_ref,
    gain_ref,
    out_ref,
):
    half = place_ref[0]
    flip = place_ref[1]
    span = GROUPS * PROMPT_TOKENS // SHARDS
    pages = page_ref[...].reshape(span, 2 * HEAD_SIZE)
    keys = pages[:, :HEAD_SIZE]
    values = jnp.concatenate(
        [jnp.ones((span, HEAD_SIZE), jnp.bfloat16), pages[:, HEAD_SIZE:]], axis=1
    )
    first_sent = jnp.where(half == 0, own_ref[0], other_ref[0])
    second_sent = jnp.where(half == 0, other_ref[0], own_ref[0])
    low_part = first_sent[:, OWN_WIDTH:].astype(jnp.float32)
    high_part = second_sent[:, OWN_WIDTH:].astype(jnp.float32)
    lane = lax.broadcasted_iota(jnp.int32, (SLOT_ROWS, HEAD_SIZE), 1)
    low_lanes = lane < HEAD_SIZE // 2
    new_keys = jnp.where(low_lanes, low_part, pltpu.roll(high_part, HEAD_SIZE // 2, 1))
    new_values = jnp.where(low_lanes, pltpu.roll(low_part, HEAD_SIZE // 2, 1), high_part)
    new_keys = norm_rotate(new_keys, gain_ref[...], cos_ref[0], sin_ref[0])
    suffix_rows = SLOT_SAMPLES * 16
    extra = suffix_rows + 2 * SLOT_ROWS
    suffix = suffix_ref[0, :suffix_rows, :]
    zeros = jnp.zeros((SLOT_ROWS, HEAD_SIZE), jnp.bfloat16)
    extra_keys = jnp.concatenate(
        [suffix[:, :HEAD_SIZE], new_keys.astype(jnp.bfloat16), zeros], axis=0
    )
    extra_values = jnp.concatenate(
        [suffix[:, HEAD_SIZE:], new_values.astype(jnp.bfloat16), zeros], axis=0
    )
    extra_values = jnp.concatenate(
        [jnp.ones((extra, HEAD_SIZE), jnp.bfloat16), extra_values], axis=1
    )
    lengths = suffix_ref[0, suffix_rows:, :].astype(jnp.float32)
    sample_of = lax.broadcasted_iota(jnp.int32, (SLOT_SAMPLES, suffix_rows), 0)
    column_sample = lax.broadcasted_iota(jnp.int32, (SLOT_SAMPLES, suffix_rows), 1) // 16
    column_length = jnp.sum(
        jnp.where(sample_of == column_sample, lengths, 0.0), axis=0, keepdims=True
    )
    row = lax.broadcasted_iota(jnp.int32, (SLOT_ROWS, suffix_rows), 0)
    column = lax.broadcasted_iota(jnp.int32, (SLOT_ROWS, suffix_rows), 1)
    suffix_seen = (row // DECODE_STEPS == column // 16) & (
        (half * 16 + column % 16).astype(jnp.float32) < column_length
    )
    row = lax.broadcasted_iota(jnp.int32, (SLOT_ROWS, 2 * SLOT_ROWS), 0)
    column = lax.broadcasted_iota(jnp.int32, (SLOT_ROWS, 2 * SLOT_ROWS), 1)
    new_seen = (
        (row // DECODE_STEPS == column // DECODE_STEPS)
        & (column % DECODE_STEPS <= row % DECODE_STEPS)
        & (column // HALF_ROWS == half)
    )
    bias = jnp.concatenate(
        [jnp.where(suffix_seen, 0.0, masked_low), jnp.where(new_seen, 0.0, masked_low)], axis=1
    )
    bias = jnp.concatenate([bias] * TILE_HEADS, axis=0)
    logs = jnp.zeros((SLOT_ROWS, HEAD_SIZE), jnp.float32)

    def finish(first, total, peak):
        nonlocal logs
        denominator = total[:, :HEAD_SIZE]
        attended = (total[:, HEAD_SIZE:] / denominator).astype(jnp.bfloat16)
        log_sum = peak + jnp.log2(denominator)
        for index in range(TILE_HEADS):
            head = first + index
            rows = slice(index * SLOT_ROWS, (index + 1) * SLOT_ROWS)
            top = attended[rows][:HALF_ROWS]
            low = attended[rows][HALF_ROWS:]
            lanes = slice(head * HEAD_SIZE, (head + 1) * HEAD_SIZE)
            out_ref[0, 0, :, lanes] = jnp.where(flip == 0, top, low)
            out_ref[0, 1, :, lanes] = jnp.where(flip == 0, low, top)
            logs = jnp.where(lane == head, log_sum[rows], logs)

    def query_of(first):
        query = []
        for head in range(first, first + TILE_HEADS):
            source, start = divmod(head, OWN_HEADS)
            sent = second_sent if source else first_sent
            query.append(sent[:, start * HEAD_SIZE : (start + 1) * HEAD_SIZE])
        return jnp.concatenate(query, axis=0)


    def scores(first):
        query = query_of(first)
        return dot_nt(query, keys), dot_nt(query, extra_keys) + bias

    tiles = list(range(0, HEAD_FAN, TILE_HEADS))
    ready = scores(tiles[0])
    for number, first in enumerate(tiles):
        prefix_score, extra_score = ready
        if number + 1 < len(tiles):
            ready = scores(tiles[number + 1])
        peak = jnp.maximum(
            jnp.max(prefix_score, axis=-1, keepdims=True),
            jnp.max(extra_score, axis=-1, keepdims=True),
        )
        prefix_weight = jnp.exp2(prefix_score - peak).astype(jnp.bfloat16)
        extra_weight = jnp.exp2(extra_score - peak).astype(jnp.bfloat16)
        total = jnp.dot(prefix_weight, values, preferred_element_type=jnp.float32) + jnp.dot(
            extra_weight, extra_values, preferred_element_type=jnp.float32
        )
        finish(first, total, peak)
    high_term = logs.astype(jnp.bfloat16).astype(jnp.float32)
    rest = logs - high_term
    mid_term = rest.astype(jnp.bfloat16).astype(jnp.float32)
    low_term = rest - mid_term
    packed = (
        high_term + pltpu.roll(mid_term, HEAD_FAN, 1) + pltpu.roll(low_term, 2 * HEAD_FAN, 1)
    ).astype(jnp.bfloat16)
    top = packed[:HALF_ROWS]
    low = packed[HALF_ROWS:]
    out_ref[0, 0, :, HEAD_FAN * HEAD_SIZE :] = jnp.where(flip == 0, top, low)
    out_ref[0, 1, :, HEAD_FAN * HEAD_SIZE :] = jnp.where(flip == 0, low, top)


def attend(order, local, reach, place, own, other, pages, suffix, cosine, sine, gain):
    block = PROMPT_TOKENS // SHARDS
    return pl.pallas_call(
        attend_kernel,
        grid_spec=pltpu.PrefetchScalarGridSpec(
            num_scalar_prefetch=4,
            grid=(GROUPS,),
            in_specs=[
                pl.BlockSpec((1, SLOT_ROWS, SENT_WIDTH), lambda i, o, l, r, p: (r[i], 0, 0)),
                pl.BlockSpec((1, SLOT_ROWS, SENT_WIDTH), lambda i, o, l, r, p: (r[i], 0, 0)),
                pl.BlockSpec(
                    (GROUPS, 1, block, 2 * HEAD_SIZE), lambda i, o, l, r, p: (0, l[i], 0, 0)
                ),
                pl.BlockSpec(
                    (1, suffix.shape[1], 2 * HEAD_SIZE), lambda i, o, l, r, p: (r[i], 0, 0)
                ),
                pl.BlockSpec((1, SLOT_ROWS, HEAD_SIZE), lambda i, o, l, r, p: (r[i], 0, 0)),
                pl.BlockSpec((1, SLOT_ROWS, HEAD_SIZE), lambda i, o, l, r, p: (r[i], 0, 0)),
                pl.BlockSpec((1, HEAD_SIZE), lambda i, o, l, r, p: (0, 0)),
            ],
            out_specs=pl.BlockSpec(
                (1, 2, HALF_ROWS, BACK_WIDTH), lambda i, o, l, r, p: (o[i], 0, 0, 0)
            ),
        ),
        out_shape=jax.ShapeDtypeStruct((GROUPS, 2, HALF_ROWS, BACK_WIDTH), jnp.bfloat16),
        compiler_params=pltpu.CompilerParams(vmem_limit_bytes=30 * 2**20),
        cost_estimate=pl.CostEstimate(
            flops=20 * GROUPS * 512 * 2432 * 384,
            bytes_accessed=8_000_000,
            transcendentals=GROUPS * 512 * 2432,
        ),
        name="attend",
    )(order, local, reach, place, own, other, pages, suffix, cosine, sine, gain)


def combine(place_ref, back_ref, mixed_ref):
    half = place_ref[0]
    rows = GROUPS * HALF_ROWS
    slots = [
        (place_ref[1] + index // 2) % 4 * 2 + (place_ref[2] ^ (index % 2))
        for index in range(GROUPS)
    ]

    def part_of(source, lanes):
        parts = [back_ref[slot, source, :, lanes] for slot in slots]
        return jnp.concatenate(parts, axis=0).astype(jnp.float32)

    def log_of(source):
        packed = part_of(source, slice(HEAD_FAN * HEAD_SIZE, BACK_WIDTH))
        return (
            packed
            + pltpu.roll(packed, HEAD_SIZE - HEAD_FAN, 1)
            + pltpu.roll(packed, HEAD_SIZE - 2 * HEAD_FAN, 1)
        )

    first_log = log_of(0)
    second_log = log_of(1)
    peak = jnp.maximum(first_log, second_log)
    first_part = jnp.exp2(first_log - peak)
    second_part = jnp.exp2(second_log - peak)
    both = first_part + second_part
    first_part = first_part / both
    second_part = second_part / both

    def attended(head):
        lanes = slice(head * HEAD_SIZE, (head + 1) * HEAD_SIZE)
        return (
            part_of(0, lanes) * first_part[:, head : head + 1]
            + part_of(1, lanes) * second_part[:, head : head + 1]
        ).astype(jnp.bfloat16)

    for head in range(OWN_HEADS):
        low = attended(head)
        high = attended(head + OWN_HEADS)
        lanes = slice(head * HEAD_SIZE, (head + 1) * HEAD_SIZE)
        mixed_ref[:, lanes] = jnp.where(half == 0, low, high)
        lanes = slice((head + OWN_HEADS) * HEAD_SIZE, (head + OWN_HEADS + 1) * HEAD_SIZE)
        mixed_ref[:, lanes] = jnp.where(half == 0, high, low)


def times_weights(mixed_ref, own_ref, other_ref):
    return (
        jnp.dot(mixed_ref[:, :OWN_WIDTH], own_ref[...], preferred_element_type=jnp.float32)
        + jnp.dot(mixed_ref[:, OWN_WIDTH:], other_ref[...], preferred_element_type=jnp.float32)
    ).astype(jnp.bfloat16)


def left_kernel(place_ref, back_ref, own_ref, other_ref, mixed_ref, *out_refs):
    @pl.when(pl.program_id(0) == 0)
    def _():
        combine(place_ref, back_ref, mixed_ref)

    product = times_weights(mixed_ref, own_ref, other_ref)
    for index, out_ref in enumerate(out_refs):
        out_ref[...] = product[2 * index * HALF_ROWS : 2 * (index + 1) * HALF_ROWS]


def right_kernel(mixed_ref, own_ref, other_ref, kept_ref, given_ref):
    product = times_weights(mixed_ref, own_ref, other_ref)
    for index in range(4):
        rows = slice(index * HALF_ROWS, (index + 1) * HALF_ROWS)
        start = 2 * index * HALF_ROWS
        kept_ref[rows, :] = product[start : start + HALF_ROWS]
        given_ref[rows, :] = product[start + HALF_ROWS : start + 2 * HALF_ROWS]


OUT_TILE = 1024
LEFT = 3 * OUT_TILE
RIGHT = MODEL_WIDTH - LEFT
OUT_COST = pl.CostEstimate(
    flops=4 * GROUPS * HALF_ROWS * MODEL_WIDTH * 1024, bytes_accessed=8_000_000, transcendentals=0
)


def left_product(place, back, own_weight, other_weight):
    rows = GROUPS * HALF_ROWS
    return pl.pallas_call(
        left_kernel,
        grid_spec=pltpu.PrefetchScalarGridSpec(
            num_scalar_prefetch=1,
            grid=(LEFT // OUT_TILE,),
            in_specs=[
                pl.BlockSpec((GROUPS, 2, HALF_ROWS, BACK_WIDTH), lambda n, p: (0, 0, 0, 0)),
                pl.BlockSpec((OWN_WIDTH, OUT_TILE), lambda n, p: (0, n)),
                pl.BlockSpec((OWN_WIDTH, OUT_TILE), lambda n, p: (0, n)),
            ],
            out_specs=[pl.BlockSpec((rows, 2 * OWN_WIDTH), lambda n, p: (0, 0))]
            + [pl.BlockSpec((rows // 4, OUT_TILE), lambda n, p: (0, n))] * 4,
        ),
        out_shape=[jax.ShapeDtypeStruct((rows, 2 * OWN_WIDTH), jnp.bfloat16)]
        + [jax.ShapeDtypeStruct((rows // 4, LEFT), jnp.bfloat16)] * 4,
        compiler_params=pltpu.CompilerParams(vmem_limit_bytes=60 * 2**20),
        cost_estimate=OUT_COST,
        name="left_product",
    )(place, back, own_weight, other_weight)


def right_product(mixed, own_weight, other_weight):
    rows = GROUPS * HALF_ROWS
    skip = LEFT // OUT_TILE
    return pl.pallas_call(
        right_kernel,
        grid=(RIGHT // OUT_TILE,),
        in_specs=[
            pl.BlockSpec((rows, 2 * OWN_WIDTH), lambda n: (0, 0)),
            pl.BlockSpec((OWN_WIDTH, OUT_TILE), lambda n: (0, n + skip)),
            pl.BlockSpec((OWN_WIDTH, OUT_TILE), lambda n: (0, n + skip)),
        ],
        out_specs=[pl.BlockSpec((rows // 2, OUT_TILE), lambda n: (0, n))] * 2,
        out_shape=[jax.ShapeDtypeStruct((rows // 2, RIGHT), jnp.bfloat16)] * 2,
        compiler_params=pltpu.CompilerParams(vmem_limit_bytes=60 * 2**20),
        cost_estimate=OUT_COST,
        name="right_product",
    )(mixed, own_weight, other_weight)


def total_of(parts):
    total = parts[0].astype(jnp.float32)
    for part in parts[1:]:
        total = total + part.astype(jnp.float32)
    return total


def along_x(distance):
    return [(shard, shard // 4 * 4 + (shard + distance) % 4) for shard in range(SHARDS)]


def along_y(distance):
    return [(shard, (shard + 4 * distance) % SHARDS) for shard in range(SHARDS)]


def across_groups(bits):
    return [(group, group ^ bits) for group in range(GROUPS)]


def exchange_groups(blocks, group):
    return exchange_along_z(exchange_cores(blocks, group), group)


def exchange_cores(blocks, group):
    by_core = blocks.reshape((GROUPS // 2, 2) + blocks.shape[1:])
    kept = lax.dynamic_index_in_dim(by_core, group % 2, 1, keepdims=True)
    given = lax.dynamic_index_in_dim(by_core, 1 - group % 2, 1, keepdims=True)
    given = lax.ppermute(given, "grp", across_groups(1))
    return jnp.concatenate([kept, given], axis=1)


def exchange_along_z(both, group):
    arrived = []
    for k in range(GROUPS // 2):
        block = lax.dynamic_index_in_dim(both, (group // 2) ^ k, 0, keepdims=False)
        arrived.append(lax.ppermute(block, "grp", across_groups(2 * k)) if k else block)
    return arrived


def swap(block, axes, groups=None):
    return lax.all_to_all(
        block, axes, split_axis=0, concat_axis=0, tiled=True, axis_index_groups=groups
    )


def shards(
    tokens,
    prompt_cache,
    generated_cache,
    suffix_lengths,
    fanout,
    prompt_adapter,
    query_weight,
    key_value_weight,
    output_weight,
    adapter_down_maps,
    adapter_up_maps,
    query_norm_gain,
    key_norm_gain,
):
    group = lax.axis_index("grp")
    shard = lax.axis_index("ad")
    head = shard // 2
    half = shard % 2
    local_table = slot_prompts(fanout, GROUPS, OWNED)

    part_rows = lax.all_gather(tokens, "ad", axis=0, tiled=True)

    slot_suffix = generated_cache.reshape(GROUPS, SLOT_SAMPLES * 16, 2 * HEAD_SIZE)
    slot_lengths = suffix_lengths.reshape(GROUPS, SLOT_SAMPLES, 1).astype(jnp.bfloat16)
    slot_suffix = jnp.concatenate(
        [slot_suffix, jnp.broadcast_to(slot_lengths, (GROUPS, SLOT_SAMPLES, 2 * HEAD_SIZE))], axis=1
    )
    both = exchange_cores(slot_suffix, group)

    owners = jnp.arange(GROUPS, dtype=jnp.int32)
    local_of_slot = lax.dynamic_index_in_dim(local_table, group, 1, keepdims=False)
    prompts = owners * OWNED + local_of_slot
    hit = prompts[:, None] == jnp.arange(prompt_adapter.shape[0], dtype=jnp.int32)[None, :]
    tasks = jnp.sum(hit.astype(jnp.int32) * prompt_adapter[None, :], axis=1)
    own_rows = tokens.shape[0]
    columns = swap(jnp.swapaxes(tokens.reshape(own_rows, SHARDS, -1), 0, 1), "ad")
    rank_all = jnp.dot(
        columns.reshape(ROWS, -1),
        adapter_down_maps.reshape(-1, ADAPTER_COUNT * ADAPTER_RANK),
        preferred_element_type=jnp.float32,
    ).reshape(GROUPS, SLOT_ROWS, ADAPTER_COUNT, ADAPTER_RANK)
    chosen = (tasks[:, None] == jnp.arange(ADAPTER_COUNT, dtype=jnp.int32)[None, :]).astype(
        jnp.float32
    )
    rank_part = jnp.sum(rank_all * chosen[:, None, :, None], axis=2)
    rank_rows = jnp.sum(swap(rank_part.reshape(SHARDS, own_rows, ADAPTER_RANK), "ad"), axis=0)
    rank_rows = rank_rows.astype(jnp.bfloat16)

    ring = [rank_rows] + [lax.ppermute(rank_rows, "ad", along_x(k)) for k in (1, 2, 3)]
    ring = jnp.stack(ring)

    low_rank = jnp.stack([ring] + [lax.ppermute(ring, "ad", along_y(k)) for k in (1, 2, 3)])
    every = jnp.arange(SHARDS, dtype=jnp.int32)
    spots = ((shard // 4 - every // 4) % 4) * 4 + (shard % 4 - every % 4) % 4

    slice_rows = OWN_WIDTH // GROUPS
    weight_slice = lax.dynamic_slice_in_dim(output_weight, group * slice_rows, slice_rows, 0)
    low_rank, head_pages, weight_slice, both = lax.optimization_barrier(
        (low_rank, jnp.swapaxes(prompt_cache, 0, 1), weight_slice, both)
    )
    arrived = swap(head_pages, "ad", ROLE_GROUPS)
    weight_slice = lax.ppermute(weight_slice, "ad", PARTNERS)
    part_rows, weight_slice = lax.optimization_barrier((part_rows, weight_slice))
    other_weight = lax.all_gather(weight_slice, "grp", axis=0, tiled=True)

    suffix = jnp.concatenate(exchange_along_z(both, group), axis=0)
    steps = jnp.arange(DECODE_STEPS, dtype=jnp.int32)
    position = (PROMPT_TOKENS + suffix_lengths[:, None] + steps[None, :]).astype(jnp.float32)
    cosine, sine = angle_tables(position.reshape(ROWS))
    sent = project(
        tasks,
        spots,
        part_rows,
        query_weight,
        key_value_weight.transpose(1, 2, 0).reshape(HEAD_SIZE, MODEL_WIDTH),
        low_rank.reshape(SHARDS, own_rows, ADAPTER_RANK),
        adapter_up_maps,
        cosine,
        sine,
        query_norm_gain.reshape(1, HEAD_SIZE) * exponent_scale,
    )
    own_sent = exchange_groups(sent, group)
    other_sent = jnp.concatenate([lax.ppermute(part, "ad", PARTNERS) for part in own_sent], axis=0)
    own_sent = jnp.concatenate(own_sent, axis=0)

    local = lax.dynamic_index_in_dim(local_table, group, 0, keepdims=False)
    rank_key = local * GROUPS + owners
    spot = jnp.sum((rank_key[None, :] < rank_key[:, None]).astype(jnp.int32), axis=1)
    placed = (spot[None, :] == owners[:, None]).astype(jnp.int32)
    order = jnp.sum(placed * owners[None, :], axis=1)
    local_sorted = jnp.sum(placed * local[None, :], axis=1)
    flip = (head + group) % 2
    place = jnp.stack([half, flip]).astype(jnp.int32)
    far_lengths = suffix[:, SLOT_SAMPLES * 16 :, 0].astype(jnp.float32)
    far_position = PROMPT_TOKENS + far_lengths[:, :, None] + steps.astype(jnp.float32)
    far_cosine, far_sine = angle_tables(far_position.reshape(GROUPS, SLOT_ROWS))
    partial = attend(
        order,
        local_sorted,
        order ^ group,
        place,
        own_sent,
        other_sent,
        arrived,
        suffix,
        far_cosine,
        far_sine,
        key_norm_gain.reshape(1, HEAD_SIZE),
    )
    back = swap(
        partial.reshape(2 * GROUPS, HALF_ROWS, BACK_WIDTH), ("grp", "ad"), HEAD_GROUPS
    ).reshape(GROUPS, 2, HALF_ROWS, BACK_WIDTH)
    place = jnp.stack([half, shard // 4, head % 2]).astype(jnp.int32)
    mixed, *by_y = left_product(place, back, output_weight, other_weight)
    by_y = by_y[:1] + [lax.ppermute(by_y[k], "ad", along_y(k)) for k in (1, 2, 3)]
    kept, given = right_product(mixed, output_weight, other_weight)
    given = lax.ppermute(given, "ad", ACROSS)
    left = total_of(by_y)
    left_given = lax.ppermute(left[HALF_ROWS:].astype(jnp.bfloat16), "ad", ACROSS)
    right = total_of([kept, given]).reshape(4, HALF_ROWS, RIGHT)
    right_parts = [right[0]] + [
        lax.ppermute(right[k].astype(jnp.bfloat16), "ad", along_y(k)) for k in (1, 2, 3)
    ]
    left = left[:HALF_ROWS] + left_given.astype(jnp.float32)
    right = total_of(right_parts)
    return jnp.concatenate([left.astype(jnp.bfloat16), right.astype(jnp.bfloat16)], axis=1)


def solution(mesh):
    return jax.shard_map(
        shards,
        mesh=mesh,
        in_specs=(
            P(("grp", "ad"), None),
            P("grp", None, "ad", None),
            P("grp", "ad", None),
            P("grp"),
            P(),
            P(),
            P(None, "ad"),
            P(None, None, "ad"),
            P("ad", None),
            P("ad", None, None),
            P(None, None, "ad"),
            P(),
            P(),
        ),
        out_specs=P(("grp", "ad"), None),
        check_vma=False,
    )
```
